32 devices in a mesh: row: 8 (over z, core), col: 4 (over y, x).
Axes of the slice: x: 2, y: 2, z: 4, core: 2. Of those that a mesh axis runs over, the one named last changes fastest.
Arguments:
- pair_input: float32 [96, 96, 128], P('row', 'col'), may hold values from -6 to 6
- block_valid: int32 [12], replicated, may hold values from 4 to 8, as said below
- proj_weight: bfloat16 [128, 640], replicated, may hold values from -0.5 to 0.5
- out_weight: bfloat16 [128, 128], replicated, may hold values from -0.5 to 0.5
- cotangent: float32 [96, 96, 128], P('row', 'col'), may hold values from -6 to 6
Outputs:
- pair_out: float32 [96, 96, 128], P('row', 'col')
- pair_grad: float32 [96, 96, 128], P('row', 'col')
- proj_grad: float32 [128, 640], replicated
- out_grad: float32 [128, 128], replicated
The draws below stay inside these ranges and needn't reach their ends.
Inputs may be any that keep to these rules, and one draw needn't show every extreme that they name: `block_valid`: entry q counts the valid tokens at the start of mask block q of 8 tokens.
All inputs are finite; a program needn't handle non-finite values.
Results may differ from the reference program's by a relative error of at most 0.0082.
Values may be sent and summed in bfloat16 or wider, within the bound.
No kernel may reach another device: no remote copies, remote signals or barrier semaphores. Data moves between devices by JAX's collectives and lax.ppermute only.
A program may use at most 128 MiB of HBM per device.

```python
import jax
import jax.numpy as jnp
from jax import lax

C = 128
CH = 128
SEG = 8
N = 96


def draw_block_valid(key, part):
    key = jax.random.fold_in(key, 7)
    blocks = N // SEG
    counts = jax.random.randint(key, (blocks,), SEG // 2, SEG + 1)
    spot = jax.random.randint(jax.random.fold_in(key, 1), (), 0, blocks)
    counts = counts.at[spot].set(SEG)
    counts = counts.at[(spot + 1) % blocks].set(SEG // 2)
    return counts.astype(jnp.int32)


def steps_of(stream_key, extent, pieces, smallest, largest):
    loudness, own = 1.0, jax.random.fold_in(stream_key, 6)
    for axis_at, parts in pieces:
        draws = jnp.exp(jax.random.uniform(jax.random.fold_in(own, axis_at), (parts,), jnp.float32, smallest / len(pieces), largest / len(pieces)))
        loudness = loudness * jnp.repeat(draws, extent[axis_at] // parts).reshape([-1 if axis == axis_at else 1 for axis in range(len(extent))])
    return loudness


def scatter_about(own_key, shape, scale, reach, cuts=(), kind=jnp.bfloat16):
    loudness = steps_of(own_key, shape, cuts, -0.22, 0.18) if cuts else 1.0
    array = jax.random.normal(own_key, shape, jnp.float32) * scale * loudness
    return jnp.minimum(jnp.maximum(array, -reach), reach).astype(kind)


def setup_inputs(seed: int = 0) -> dict:
    streams_of = jax.random.split(jax.random.key(seed), 6)
    return {
        "pair_input": scatter_about(streams_of[0], (N, N, C), 1.0, 6.0, ((0, 8), (1, 4)), jnp.float32),
        "block_valid": draw_block_valid(jax.random.fold_in(streams_of[5], 71), 0),
        "proj_weight": scatter_about(streams_of[2], (C, 4 * CH + C), C ** -0.5, 0.5),
        "out_weight": scatter_about(streams_of[3], (CH, C), CH ** -0.5, 0.5),
        "cotangent": scatter_about(streams_of[4], (N, N, C), 1.0, 6.0, ((0, 8), (1, 4)), jnp.float32),
    }


def layer_norm(values):
    middle = lax.optimization_barrier(jnp.mean(values, axis=-1, keepdims=True))
    center = values - middle
    spread = lax.optimization_barrier(jnp.mean(center * center, axis=-1, keepdims=True))
    scaled = lax.rsqrt(spread + 1e-05)
    return (center * scaled, scaled)

def norm_back(grad_norm, normed, scaled):
    first_mean = lax.optimization_barrier(jnp.mean(grad_norm, axis=-1, keepdims=True))
    second = lax.optimization_barrier(jnp.mean(grad_norm * normed, axis=-1, keepdims=True))
    return scaled * (grad_norm - first_mean - normed * second)

def gate_back(grad_in, pair_mask, gate_part, value_part):
    sigma_val = jax.nn.sigmoid(gate_part)
    masked = grad_in * pair_mask
    return (masked * value_part * sigma_val * (1.0 - sigma_val), masked * sigma_val)

def reference(pair_input, block_valid, proj_weight, out_weight, cotangent):
    token_mask = (jnp.arange(N) % SEG < jnp.repeat(block_valid, SEG)).astype(jnp.float32)
    pair_mask = token_mask[:, None, None] * token_mask[None, :, None]
    normed, scaled = layer_norm(pair_input)
    normed_low = normed.astype(jnp.bfloat16)
    projected = jnp.einsum('ijc,cd->ijd', normed_low.astype(jnp.float32), proj_weight.astype(jnp.float32))
    left_gate = projected[..., :CH]
    left_value = projected[..., CH:2 * CH]
    right_gate = projected[..., 2 * CH:3 * CH]
    right_value = projected[..., 3 * CH:4 * CH]
    out_logit = projected[..., 4 * CH:]
    left_proj = (pair_mask * jax.nn.sigmoid(left_gate) * left_value).astype(jnp.bfloat16)
    right_proj = (pair_mask * jax.nn.sigmoid(right_gate) * right_value).astype(jnp.bfloat16)
    mixed_sum = jnp.einsum('ikc,jkc->ijc', left_proj.astype(jnp.float32), right_proj.astype(jnp.float32))
    mixed_norm, mixed_scale = layer_norm(mixed_sum)
    mixed_low = mixed_norm.astype(jnp.bfloat16)
    update = jnp.einsum('ijh,hc->ijc', mixed_low.astype(jnp.float32), out_weight.astype(jnp.float32))
    out_gate = jax.nn.sigmoid(out_logit)
    pair_out = out_gate * update
    grad_logit = cotangent * update * out_gate * (1.0 - out_gate)
    grad_update = (cotangent * out_gate).astype(jnp.bfloat16)
    out_grad = jnp.einsum('ijh,ijc->hc', mixed_low.astype(jnp.float32), grad_update.astype(jnp.float32))
    grad_mixed_norm = jnp.einsum('ijc,hc->ijh', grad_update.astype(jnp.float32), out_weight.astype(jnp.float32))
    grad_mixed = norm_back(grad_mixed_norm, mixed_norm, mixed_scale).astype(jnp.bfloat16)
    grad_left = jnp.einsum('ijc,jkc->ikc', grad_mixed.astype(jnp.float32), right_proj.astype(jnp.float32))
    grad_right = jnp.einsum('ijc,ikc->jkc', grad_mixed.astype(jnp.float32), left_proj.astype(jnp.float32))
    left_dg, left_dv = gate_back(grad_left, pair_mask, left_gate, left_value)
    right_dg, right_dv = gate_back(grad_right, pair_mask, right_gate, right_value)
    grad_proj = jnp.concatenate([left_dg, left_dv, right_dg, right_dv, grad_logit], axis=-1).astype(jnp.bfloat16)
    proj_grad = jnp.einsum('ijc,ijd->cd', normed_low.astype(jnp.float32), grad_proj.astype(jnp.float32))
    grad_normed = jnp.einsum('ijd,cd->ijc', grad_proj.astype(jnp.float32), proj_weight.astype(jnp.float32))
    pair_grad = norm_back(grad_normed, normed, scaled)
    return (pair_out, pair_grad, proj_grad, out_grad)
```

```python
import functools

import jax
import jax.numpy as jnp
from jax import lax
from jax.experimental import pallas as pl
from jax.experimental.pallas import tpu as pltpu
from jax.sharding import PartitionSpec as P

SEG = 8
F32 = jnp.float32
BF16 = jnp.bfloat16


def sigmoid(values):
    return 0.5 * jnp.tanh(0.5 * values) + 0.5


def layer_norm(values):
    center = values - jnp.mean(values, axis=-1, keepdims=True)
    scaled = lax.rsqrt(jnp.mean(center * center, axis=-1, keepdims=True) + 1e-05)
    return center * scaled, scaled


def norm_back(grad_norm, normed, scaled):
    first_mean = jnp.mean(grad_norm, axis=-1, keepdims=True)
    second = jnp.mean(grad_norm * normed, axis=-1, keepdims=True)
    return scaled * (grad_norm - first_mean - normed * second)


def dot(a, b):
    return jnp.dot(a, b, preferred_element_type=F32)


def dot_nt(a, b):
    return lax.dot_general(a, b, (((1,), (1,)), ((), ())), preferred_element_type=F32)


def dot_tn(a, b):
    return lax.dot_general(a, b, (((0,), (0,)), ((), ())), preferred_element_type=F32)


def flip(z, count):
    out, bit = z & 0, 1
    top = count >> 1
    while bit < count:
        if isinstance(z, int):
            out |= top if z & bit else 0
        else:
            out = out + jnp.where((z & bit) != 0, top, 0)
        bit, top = bit << 1, top >> 1
    return out


def place(cols):
    row, col = lax.axis_index("row"), lax.axis_index("col")
    z, core = row >> 1, row & 1
    step = flip(z, cols)
    return row, core, col, step, col ^ step


def norm_kernel(pair_ref, low_ref):
    low_ref[...] = layer_norm(pair_ref[...])[0].astype(BF16)


def project_block(projected, valid_ref, row, block, sizes, index, v_ref, a_ref, b_ref):
    row_len, col_len, width = sizes
    spot = lax.broadcasted_iota(jnp.int32, (SEG, width), 0)
    groups = col_len // SEG
    keep_col = jnp.concatenate(
        [jnp.where(spot < valid_ref[block * groups + g], 1.0, 0.0) for g in range(groups)], axis=0
    )
    for i in range(row_len):
        token = row * row_len + i
        valid = (token & (SEG - 1)) < valid_ref[token >> 3]
        keep = keep_col * jnp.where(valid, 1.0, 0.0)
        part = projected[i * col_len : (i + 1) * col_len]
        gate = sigmoid(part[:, :width])
        kept = keep * gate
        gated = kept * part[:, width:]
        v_ref[index + (i,)] = gated.astype(BF16).astype(F32)
        a_ref[index + (i,)] = gated * (1.0 - gate)
        b_ref[index + (i,)] = kept


def project_kernel(side, cols, sizes, valid_ref, x_ref, w_ref, v_ref, a_ref, b_ref):
    row_len, col_len, width = sizes
    area = row_len * col_len
    row, core, col, step, pair = place(cols)
    if side == 1:
        row = 2 * pair + core

    def one(d, carry):
        rows = pl.ds(pl.multiple_of(d * area, area), area)
        projected = dot(x_ref[rows, :], w_ref[:, side * 2 * width : (side + 1) * 2 * width])
        project_block(projected, valid_ref, row, col ^ d, sizes, (d,), v_ref, a_ref, b_ref)
        return carry

    lax.fori_loop(0, cols, one, 0)


def main_kernel(
    cols,
    sizes,
    valid_ref,
    lv_ref,
    la_ref,
    lb_ref,
    ov_ref,
    oa_ref,
    ob_ref,
    x_ref,
    own_x_ref,
    other_x_ref,
    cot_ref,
    w_ref,
    wout_ref,
    out_ref,
    send_ref,
    keep_y_ref,
    gx_ref,
    keep_w_ref,
    rv_ref,
    ra_ref,
    rb_ref,
    mixed_ref,
    grad_ref,
    wide_ref,
    dl_ref,
    dr_ref,
    wg_ref,
):
    row_len, col_len, width = sizes
    area = row_len * col_len
    row, core, col, step, pair = place(cols)
    groups = col_len // SEG
    other = 1 - core
    zero = jnp.zeros((SEG, width), F32)

    def block_rows(d):
        return pl.ds(pl.multiple_of(d * area, area), area)

    def tile(g):
        return slice(g * SEG, (g + 1) * SEG)

    def right_side(d, carry):
        projected = dot(other_x_ref[block_rows(d), :], w_ref[:, 2 * width : 4 * width])
        project_block(
            projected, valid_ref, 2 * pair + other, col ^ d, sizes, (other, d), rv_ref, ra_ref, rb_ref
        )
        rv_ref[core, d] = ov_ref[d]
        ra_ref[core, d] = oa_ref[d]
        rb_ref[core, d] = ob_ref[d]
        return carry

    lax.fori_loop(0, cols, right_side, 0)

    def mix_rows(pair_at, carry):
        for jt in range(col_len // SEG):

            def over(d, acc):
                for g in range(groups):
                    left = [lv_ref[d, 2 * pair_at + a, tile(g), :] for a in range(2)]
                    right = [
                        rv_ref[j // row_len, d, j % row_len, tile(g), :]
                        for j in range(jt * SEG, (jt + 1) * SEG)
                    ]
                    acc = tuple(acc[n] + left[n // SEG] * right[n % SEG] for n in range(2 * SEG))
                return acc

            acc = lax.fori_loop(0, cols, over, (zero,) * (2 * SEG))
            for a in range(2):
                mixed_ref[2 * pair_at + a, tile(jt), :] = jnp.concatenate(
                    [jnp.sum(acc[a * SEG + n], axis=0, keepdims=True) for n in range(SEG)], axis=0
                )
        return carry

    lax.fori_loop(0, row_len // 2, mix_rows, 0)

    mixed_norm, mixed_scale = layer_norm(mixed_ref[...].reshape(area, width))
    mixed_low = mixed_norm.astype(BF16)
    update = dot(mixed_low, wout_ref[...])
    home = x_ref[block_rows(step), :]
    out_gate = sigmoid(dot(home, w_ref[:, 4 * width :]))
    out_ref[...] = out_gate * update
    cot = cot_ref[...]
    gated_cot = cot * out_gate
    grad_logit = (gated_cot * update * (1.0 - out_gate)).astype(BF16)
    grad_update = gated_cot.astype(BF16)
    wg_ref[1, 2 * width :, :] = dot_tn(mixed_low, grad_update)
    wg_ref[1, width : 2 * width, :] = dot_tn(home, grad_logit)
    grad_mixed = norm_back(dot_nt(grad_update, wout_ref[...]), mixed_norm, mixed_scale)
    grad_ref[...] = grad_mixed.astype(BF16).astype(F32).reshape(row_len, col_len, width)

    def widen(i, carry):
        for j in range(col_len):
            wide_ref[i, j] = jnp.broadcast_to(grad_ref[i, j : j + 1, :], (SEG, width))
        return carry

    lax.fori_loop(0, row_len, widen, 0)

    def gradient(load, count, first, a_ref, b_ref, index, d_ref, d_index):
        acc = [[zero] * groups for _ in range(4)]
        for n in range(count):
            value, weights = load(n)
            for a in range(4):
                for g in range(groups):
                    acc[a][g] = acc[a][g] + value[g] * weights[a]
        full = [jnp.concatenate(acc[a], axis=0) for a in range(4)]
        gates = [full[a] * a_ref[index + (first + a,)] for a in range(4)]
        values = [full[a] * b_ref[index + (first + a,)] for a in range(4)]
        d_ref[d_index + (slice(0, width),)] = jnp.concatenate(gates, axis=0).astype(BF16)
        d_ref[d_index + (slice(width, 2 * width),)] = jnp.concatenate(values, axis=0).astype(BF16)

    quarter = 4 * col_len

    def spot(d, b):
        return pl.ds(pl.multiple_of(d * area + b * quarter, quarter), quarter)

    for half in range(2):

        def right_back(n, carry):
            b, d = n // cols, n % cols

            def load(i):
                return (
                    [lv_ref[d, i, tile(g), :] for g in range(groups)],
                    [wide_ref[i, half * row_len + 4 * b + a] for a in range(4)],
                )

            gradient(load, row_len, 4 * b, ra_ref, rb_ref, (half, d), dr_ref, (half, spot(d, b)))
            return carry

        lax.fori_loop(0, (row_len // 4) * cols, right_back, 0)

    def left_back(n, carry):
        b, d = n // cols, n % cols

        def load(j):
            return (
                [rv_ref[j // row_len, d, j % row_len, tile(g), :] for g in range(groups)],
                [wide_ref[4 * b + a, j] for a in range(4)],
            )

        gradient(load, col_len, 4 * b, la_ref, lb_ref, (d,), dl_ref, (spot(d, b),))
        return carry

    lax.fori_loop(0, (row_len // 4) * cols, left_back, 0)

    def back(d, carry):
        rows = block_rows(d)
        w_left = w_ref[:, : 2 * width]
        w_right = w_ref[:, 2 * width : 4 * width]
        send_ref[rows, :] = dot_nt(dr_ref[other, rows, :], w_right).astype(BF16)
        keep_y_ref[rows, :] = dot_nt(dr_ref[core, rows, :], w_right)
        gx_ref[rows, :] = dot_nt(dl_ref[rows, :], w_left)
        return carry

    lax.fori_loop(0, cols, back, 0)
    gx_ref[block_rows(step), :] += dot_nt(grad_logit, w_ref[:, 4 * width :])

    left_w = dot_tn(x_ref[...], dl_ref[...])
    right_w = dot_tn(own_x_ref[...], dr_ref[core]) + dot_tn(other_x_ref[...], dr_ref[other])
    wg_ref[0, :width, :] = left_w[:, :width]
    wg_ref[0, width : 2 * width, :] = left_w[:, width:]
    wg_ref[0, 2 * width :, :] = right_w[:, :width]
    wg_ref[1, :width, :] = right_w[:, width:]
    send_ref[cols * area :, :] = wg_ref[other].astype(BF16)
    keep_w_ref[...] = wg_ref[core]


def core_sum_kernel(cols, rows, keep_y_ref, keep_w_ref, got_ref, y_ref, own_ref, *rest):
    chunk_refs, sum_ref = rest[:-1], rest[-1]
    col = lax.axis_index("col")
    y_ref[...] = (keep_y_ref[...] + got_ref[:rows, :].astype(F32)).astype(BF16)
    total = keep_w_ref[...] + got_ref[rows:, :].astype(F32)
    sum_ref[...] = total.reshape(sum_ref.shape)
    own_ref[...] = sum_ref[col]
    for d in range(1, cols):
        chunk_refs[d - 1][...] = sum_ref[col ^ d].astype(BF16)


def row_sum_kernel(cols, area, gx_ref, got_ref, chunk_ref, own_ref, *send_refs):
    own_ref[...] = gx_ref[:area, :] + got_ref[:area, :].astype(F32)
    for d in range(1, cols):
        rows = slice(d * area, (d + 1) * area)
        send_refs[d - 1][:area, :] = (gx_ref[rows, :] + got_ref[rows, :].astype(F32)).astype(BF16)
        send_refs[d - 1][area:, :] = chunk_ref[...]


def pair_grad_kernel(cols, area, own_ref, pair_ref, chunk_ref, *rest):
    got_refs, (grad_ref, half_ref, order_ref) = rest[: cols - 1], rest[cols - 1 :]
    col = lax.axis_index("col")
    total = own_ref[...]
    order_ref[col] = chunk_ref[...].astype(F32)
    for d in range(1, cols):
        total = total + got_refs[d - 1][:area, :].astype(F32)
        order_ref[col ^ d] = got_refs[d - 1][area:, :].astype(F32)
    normed, scaled = layer_norm(pair_ref[...])
    grad_ref[...] = norm_back(total, normed, scaled)
    half_ref[...] = order_ref[...].reshape(half_ref.shape).astype(BF16)


def weights_kernel(width, mine_ref, other_ref, proj_ref, out_ref):
    first = (lax.axis_index("row") & 1) == 0
    mine, other = mine_ref[...].astype(F32), other_ref[...].astype(F32)
    low, high = jnp.where(first, mine, other), jnp.where(first, other, mine)
    for n in range(3):
        proj_ref[:, n * width : (n + 1) * width] = low[n * width : (n + 1) * width]
    for n in range(2):
        proj_ref[:, (3 + n) * width : (4 + n) * width] = high[n * width : (n + 1) * width]
    out_ref[...] = high[2 * width :]


def call(kernel, name, out_shape, args, scratch=(), smem=0):
    specs = [pl.BlockSpec(memory_space=pltpu.SMEM if n < smem else pltpu.VMEM) for n in range(len(args))]
    total = sum(a.size * a.dtype.itemsize for a in list(args) + list(out_shape))
    total += sum(_bytes(s) for s in scratch)
    return pl.pallas_call(
        kernel,
        out_shape=tuple(out_shape),
        in_specs=specs,
        out_specs=tuple(pl.BlockSpec(memory_space=pltpu.VMEM) for _ in out_shape),
        scratch_shapes=list(scratch),
        compiler_params=pltpu.CompilerParams(vmem_limit_bytes=min(60 << 20, total + (8 << 20))),
        name=name,
    )(*args)


def _bytes(ref):
    size = jnp.dtype(ref.dtype).itemsize
    for n in ref.shape:
        size *= n
    return size


def body(rows, cols, pair_input, block_valid, proj_weight, out_weight, cotangent):
    row_len, col_len, width = pair_input.shape
    area = row_len * col_len
    sizes = (row_len, col_len, width)
    planes = rows // 2
    assert planes == cols and col_len == 2 * row_len and cols & (cols - 1) == 0
    assert col_len % SEG == 0 and out_weight.shape == (width, width)

    def permute(value, target):
        pairs = []
        for z in range(planes):
            for core in range(2):
                for col in range(cols):
                    to = target(z, core, col)
                    pairs.append(((2 * z + core) * cols + col, (2 * to[0] + to[1]) * cols + to[2]))
        return lax.ppermute(value, ("row", "col"), pairs)

    def in_plane(value, d):
        return permute(value, lambda z, core, col: (z, core, col ^ d))

    def across(value, d):
        return permute(value, lambda z, core, col: (z ^ d, core, col))

    def to_pair(value):
        return permute(value, lambda z, core, col: (z, core, col ^ flip(z, cols)))

    def swap(value):
        return permute(value, lambda z, core, col: (z, 1 - core, col))

    def like(*shape, dtype=F32):
        return jax.ShapeDtypeStruct(shape, dtype)

    pair = pair_input.reshape(area, width)
    cot = cotangent.reshape(area, width)
    (low,) = call(norm_kernel, "norm", [like(area, width, dtype=BF16)], [pair])
    blocks = [low] + [in_plane(low, d) for d in range(1, cols)]
    x = jnp.concatenate(blocks, axis=0)
    own_x = permute(x, lambda z, core, col: (flip(col ^ z, cols), core, col))
    cot = to_pair(cot)
    gated = [like(cols, row_len, col_len, width)] * 3
    left = call(
        functools.partial(project_kernel, 0, cols, sizes),
        "left",
        gated,
        [block_valid, x, proj_weight],
        smem=1,
    )
    other_x = swap(own_x)
    right = call(
        functools.partial(project_kernel, 1, cols, sizes),
        "right",
        gated,
        [block_valid, own_x, proj_weight],
        smem=1,
    )
    tall = cols * area
    half = 3 * width
    both = pltpu.VMEM((2, cols, row_len, col_len, width), F32)
    flat = pltpu.VMEM((row_len, col_len, width), F32)
    pair_out, send, keep_y, gx, keep_w = call(
        functools.partial(main_kernel, cols, sizes),
        "triangle",
        [
            like(area, width),
            like(tall + half, width, dtype=BF16),
            like(tall, width),
            like(tall, width),
            like(half, width),
        ],
        [block_valid, *left, *right, x, own_x, other_x, cot, proj_weight, out_weight],
        [
            both,
            both,
            both,
            flat,
            flat,
            pltpu.VMEM((row_len, col_len, SEG, width), F32),
            pltpu.VMEM((tall, 2 * width), BF16),
            pltpu.VMEM((2, tall, 2 * width), BF16),
            pltpu.VMEM((2, half, width), F32),
        ],
        smem=1,
    )
    got = swap(send)
    chunk = half // cols
    y, mine, *chunks = call(
        functools.partial(core_sum_kernel, cols, tall),
        "core_sum",
        [like(tall, width, dtype=BF16), like(chunk, width)]
        + [like(chunk, width, dtype=BF16)] * (cols - 1),
        [keep_y, keep_w, got],
        [pltpu.VMEM((cols, chunk, width), F32)],
    )
    pair_out = to_pair(pair_out)
    back_y = permute(y, lambda z, core, col: (col ^ flip(z, cols), core, col))
    for d in range(1, cols):
        mine = mine + in_plane(chunks[d - 1], d).astype(F32)
    low_mine = mine.astype(BF16)
    for d in range(1, cols):
        mine = mine + across(low_mine, d).astype(F32)
    low_mine = mine.astype(BF16)
    own, *sends = call(
        functools.partial(row_sum_kernel, cols, area),
        "row_sum",
        [like(area, width)] + [like(area + chunk, width, dtype=BF16)] * (cols - 1),
        [gx, back_y, low_mine],
    )
    gets = [in_plane(sends[d - 1], d) for d in range(1, cols)]
    pair_grad, mine_w = call(
        functools.partial(pair_grad_kernel, cols, area),
        "pair_grad",
        [like(area, width), like(half, width, dtype=BF16)],
        [own, pair, low_mine, *gets],
        [pltpu.VMEM((cols, chunk, width), F32)],
    )
    proj_grad, out_grad = call(
        functools.partial(weights_kernel, width),
        "weights",
        [like(*proj_weight.shape), like(width, width)],
        [mine_w, swap(mine_w)],
    )
    shape = pair_input.shape
    return pair_out.reshape(shape), pair_grad.reshape(shape), proj_grad, out_grad


def solution(mesh):
    return jax.shard_map(
        functools.partial(body, mesh.shape["row"], mesh.shape["col"]),
        mesh=mesh,
        in_specs=(P("row", "col", None), P(), P(), P(), P("row", "col", None)),
        out_specs=(P("row", "col", None), P("row", "col", None), P(), P()),
        check_vma=False,
    )
```

```python
import functools

import jax
import jax.numpy as jnp
from jax import lax
from jax.experimental import pallas as pl
from jax.experimental.pallas import tpu as pltpu
from jax.sharding import PartitionSpec as P

SEG = 8
F32 = jnp.float32
BF16 = jnp.bfloat16


def sigmoid(values):
    return 0.5 * jnp.tanh(0.5 * values) + 0.5


def layer_norm(values):
    center = values - jnp.mean(values, axis=-1, keepdims=True)
    scaled = lax.rsqrt(jnp.mean(center * center, axis=-1, keepdims=True) + 1e-05)
    return center * scaled, scaled


def norm_back(grad_norm, normed, scaled):
    first_mean = jnp.mean(grad_norm, axis=-1, keepdims=True)
    second = jnp.mean(grad_norm * normed, axis=-1, keepdims=True)
    return scaled * (grad_norm - first_mean - normed * second)


def dot(a, b):
    return jnp.dot(a, b, preferred_element_type=F32)


def dot_nt(a, b):
    return lax.dot_general(a, b, (((1,), (1,)), ((), ())), preferred_element_type=F32)


def dot_tn(a, b):
    return lax.dot_general(a, b, (((0,), (0,)), ((), ())), preferred_element_type=F32)


def flip(z, count):
    out, bit = z & 0, 1
    top = count >> 1
    while bit < count:
        if isinstance(z, int):
            out |= top if z & bit else 0
        else:
            out = out + jnp.where((z & bit) != 0, top, 0)
        bit, top = bit << 1, top >> 1
    return out


def place(cols):
    row, col = lax.axis_index("row"), lax.axis_index("col")
    z, core = row >> 1, row & 1
    step = flip(z, cols)
    return row, core, col, step, col ^ step


def norm_kernel(pair_ref, low_ref):
    low_ref[...] = layer_norm(pair_ref[...])[0].astype(BF16)


def project_block(projected, valid_ref, row, block, sizes, index, v_ref, a_ref, b_ref):
    row_len, col_len, width = sizes
    spot = lax.broadcasted_iota(jnp.int32, (SEG, width), 0)
    groups = col_len // SEG
    keep_col = jnp.concatenate(
        [jnp.where(spot < valid_ref[block * groups + g], 1.0, 0.0) for g in range(groups)], axis=0
    )
    for i in range(row_len):
        token = row * row_len + i
        valid = (token & (SEG - 1)) < valid_ref[token >> 3]
        keep = keep_col * jnp.where(valid, 1.0, 0.0)
        part = projected[i * col_len : (i + 1) * col_len]
        gate = sigmoid(part[:, :width])
        kept = keep * gate
        gated = kept * part[:, width:]
        v_ref[index + (i,)] = gated.astype(BF16).astype(F32)
        a_ref[index + (i,)] = gated * (1.0 - gate)
        b_ref[index + (i,)] = kept


def project_kernel(side, cols, sizes, valid_ref, x_ref, w_ref, *refs):
    row_len, col_len, width = sizes
    area = row_len * col_len
    row, core, col, step, pair = place(cols)
    half = core if side < 2 else 1 - core
    if side:
        row = 2 * pair + half
    base = 2 * width if side else 0
    outs = refs[-3:]

    def one(d, carry):
        rows = pl.ds(pl.multiple_of(d * area, area), area)
        projected = dot(x_ref[rows, :], w_ref[:, base : base + 2 * width])
        index = (half, d) if side else (d,)
        project_block(projected, valid_ref, row, col ^ d, sizes, index, *outs)
        return carry

    lax.fori_loop(0, cols, one, 0)


def tile(g):
    return slice(g * SEG, (g + 1) * SEG)


def rows_of(d, area):
    return pl.ds(pl.multiple_of(d * area, area), area)


def mix_kernel(
    cols,
    sizes,
    lv_ref,
    rv_ref,
    x_ref,
    cot_ref,
    w_ref,
    wout_ref,
    out_ref,
    logit_ref,
    wide_ref,
    wg_ref,
    mixed_ref,
    grad_ref,
):
    row_len, col_len, width = sizes
    area = row_len * col_len
    row, core, col, step, pair = place(cols)
    groups = col_len // SEG
    zero = jnp.zeros((SEG, width), F32)

    def mix_rows(pair_at, carry):
        for jt in range(groups):

            def over(d, acc):
                for g in range(groups):
                    left = [lv_ref[d, 2 * pair_at + a, tile(g), :] for a in range(2)]
                    right = [
                        rv_ref[j // row_len, d, j % row_len, tile(g), :]
                        for j in range(jt * SEG, (jt + 1) * SEG)
                    ]
                    acc = tuple(acc[n] + left[n // SEG] * right[n % SEG] for n in range(2 * SEG))
                return acc

            acc = lax.fori_loop(0, cols, over, (zero,) * (2 * SEG))
            for a in range(2):
                mixed_ref[2 * pair_at + a, tile(jt), :] = jnp.concatenate(
                    [jnp.sum(acc[a * SEG + n], axis=0, keepdims=True) for n in range(SEG)], axis=0
                )
        return carry

    lax.fori_loop(0, row_len // 2, mix_rows, 0)

    mixed_norm, mixed_scale = layer_norm(mixed_ref[...].reshape(area, width))
    mixed_low = mixed_norm.astype(BF16)
    update = dot(mixed_low, wout_ref[...])
    home = x_ref[rows_of(step, area), :]
    out_gate = sigmoid(dot(home, w_ref[:, 4 * width :]))
    out_ref[...] = out_gate * update
    gated_cot = cot_ref[...] * out_gate
    grad_logit = (gated_cot * update * (1.0 - out_gate)).astype(BF16)
    grad_update = gated_cot.astype(BF16)
    logit_ref[...] = grad_logit
    wg_ref[:width, :] = dot_tn(home, grad_logit)
    wg_ref[width:, :] = dot_tn(mixed_low, grad_update)
    grad_mixed = norm_back(dot_nt(grad_update, wout_ref[...]), mixed_norm, mixed_scale)
    grad_ref[...] = grad_mixed.astype(BF16).astype(F32).reshape(row_len, col_len, width)

    def widen(i, carry):
        for j in range(col_len):
            wide_ref[i, j] = jnp.broadcast_to(grad_ref[i, j : j + 1, :], (SEG, width))
        return carry

    lax.fori_loop(0, row_len, widen, 0)


def gradient(load, count, first, sizes, a_ref, b_ref, index, d_ref, d_index):
    row_len, col_len, width = sizes
    groups = col_len // SEG
    acc = [[jnp.zeros((SEG, width), F32)] * groups for _ in range(4)]
    for n in range(count):
        value, weights = load(n)
        for a in range(4):
            for g in range(groups):
                acc[a][g] = acc[a][g] + value[g] * weights[a]
    full = [jnp.concatenate(acc[a], axis=0) for a in range(4)]
    gates = [full[a] * a_ref[index + (first + a,)] for a in range(4)]
    values = [full[a] * b_ref[index + (first + a,)] for a in range(4)]
    d_ref[d_index + (slice(0, width),)] = jnp.concatenate(gates, axis=0).astype(BF16)
    d_ref[d_index + (slice(width, 2 * width),)] = jnp.concatenate(values, axis=0).astype(BF16)


def grads_kernel(
    cols, sizes, lv_ref, la_ref, lb_ref, rv_ref, ra_ref, rb_ref, wide_ref, dl_ref, dr_ref
):
    row_len, col_len, width = sizes
    area = row_len * col_len
    groups = col_len // SEG
    quarter = 4 * col_len

    def spot(d, b):
        return pl.ds(pl.multiple_of(d * area + b * quarter, quarter), quarter)

    for half in range(2):

        def right_back(n, carry):
            b, d = n // cols, n % cols

            def load(i):
                return (
                    [lv_ref[d, i, tile(g), :] for g in range(groups)],
                    [wide_ref[i, half * row_len + 4 * b + a] for a in range(4)],
                )

            where = (half, spot(d, b))
            gradient(load, row_len, 4 * b, sizes, ra_ref, rb_ref, (half, d), dr_ref, where)
            return carry

        lax.fori_loop(0, (row_len // 4) * cols, right_back, 0)

    def left_back(n, carry):
        b, d = n // cols, n % cols

        def load(j):
            return (
                [rv_ref[j // row_len, d, j % row_len, tile(g), :] for g in range(groups)],
                [wide_ref[4 * b + a, j] for a in range(4)],
            )

        gradient(load, col_len, 4 * b, sizes, la_ref, lb_ref, (d,), dl_ref, (spot(d, b),))
        return carry

    lax.fori_loop(0, (row_len // 4) * cols, left_back, 0)


def weight_sums_kernel(
    width, x_ref, own_x_ref, other_x_ref, dl_ref, dr_ref, wg_ref, send_ref, keep_ref, sum_ref
):
    core = lax.axis_index("row") & 1
    left_w = dot_tn(x_ref[...], dl_ref[...])
    right_w = dot_tn(own_x_ref[...], dr_ref[core]) + dot_tn(other_x_ref[...], dr_ref[1 - core])
    sum_ref[0, :width, :] = left_w[:, :width]
    sum_ref[0, width : 2 * width, :] = left_w[:, width:]
    sum_ref[0, 2 * width :, :] = right_w[:, :width]
    sum_ref[1, :width, :] = right_w[:, width:]
    sum_ref[1, width:, :] = wg_ref[...]
    send_ref[...] = sum_ref[1 - core].astype(BF16)
    keep_ref[...] = sum_ref[core]


def back_other_kernel(cols, area, width, dr_ref, w_ref, send_ref):
    core = lax.axis_index("row") & 1

    def back(d, carry):
        rows = rows_of(d, area)
        part = dot_nt(dr_ref[1 - core, rows, :], w_ref[:, 2 * width : 4 * width])
        send_ref[rows, :] = part.astype(BF16)
        return carry

    lax.fori_loop(0, cols, back, 0)


def back_own_kernel(cols, area, width, dl_ref, dr_ref, logit_ref, w_ref, keep_ref, gx_ref):
    row, core, col, step, pair = place(cols)

    def back(d, carry):
        rows = rows_of(d, area)
        keep_ref[rows, :] = dot_nt(dr_ref[core, rows, :], w_ref[:, 2 * width : 4 * width])
        gx_ref[rows, :] = dot_nt(dl_ref[rows, :], w_ref[:, : 2 * width])
        return carry

    lax.fori_loop(0, cols, back, 0)
    gx_ref[rows_of(step, area), :] += dot_nt(logit_ref[...], w_ref[:, 4 * width :])


def core_sum_kernel(keep_ref, got_ref, y_ref):
    y_ref[...] = (keep_ref[...] + got_ref[...].astype(F32)).astype(BF16)


def chunks_kernel(cols, keep_ref, got_ref, own_ref, *rest):
    chunk_refs, sum_ref = rest[:-1], rest[-1]
    col = lax.axis_index("col")
    total = keep_ref[...] + got_ref[...].astype(F32)
    sum_ref[...] = total.reshape(sum_ref.shape)
    own_ref[...] = sum_ref[col]
    for d in range(1, cols):
        chunk_refs[d - 1][...] = sum_ref[col ^ d].astype(BF16)


def row_sum_kernel(cols, area, gx_ref, got_ref, chunk_ref, swapped_ref, own_ref, *send_refs):
    chunk = chunk_ref.shape[0]
    own_ref[...] = gx_ref[:area, :] + got_ref[:area, :].astype(F32)
    for d in range(1, cols):
        rows = slice(d * area, (d + 1) * area)
        send_refs[d - 1][:area, :] = (gx_ref[rows, :] + got_ref[rows, :].astype(F32)).astype(BF16)
        send_refs[d - 1][area : area + chunk, :] = chunk_ref[...]
        send_refs[d - 1][area + chunk :, :] = swapped_ref[...]


def final_kernel(cols, area, own_ref, pair_ref, chunk_ref, swapped_ref, home_ref, *rest):
    got_refs = rest[: cols - 1]
    grad_ref, proj_ref, out_ref, home_out_ref, order_ref = rest[cols - 1 :]
    chunk, width = chunk_ref.shape
    col, core = lax.axis_index("col"), lax.axis_index("row") & 1
    home_out_ref[...] = home_ref[...]
    total = own_ref[...]
    order_ref[core, col] = chunk_ref[...].astype(F32)
    order_ref[1 - core, col] = swapped_ref[...].astype(F32)
    for d in range(1, cols):
        got = got_refs[d - 1]
        total = total + got[:area, :].astype(F32)
        order_ref[core, col ^ d] = got[area : area + chunk, :].astype(F32)
        order_ref[1 - core, col ^ d] = got[area + chunk :, :].astype(F32)
    normed, scaled = layer_norm(pair_ref[...])
    grad_ref[...] = norm_back(total, normed, scaled)
    whole = order_ref[...].reshape(6 * width, width)
    for n in range(5):
        proj_ref[:, n * width : (n + 1) * width] = whole[n * width : (n + 1) * width]
    out_ref[...] = whole[5 * width :]


def call(kernel, name, micros, out_shape, args, scratch=(), smem=0, aliases=None):
    specs = [pl.BlockSpec(memory_space=pltpu.SMEM if n < smem else pltpu.VMEM) for n in range(len(args))]
    total = sum(_bytes(ref) for ref in [*args, *out_shape, *scratch])
    return pl.pallas_call(
        kernel,
        out_shape=tuple(out_shape),
        in_specs=specs,
        out_specs=tuple(pl.BlockSpec(memory_space=pltpu.VMEM) for _ in out_shape),
        scratch_shapes=list(scratch),
        input_output_aliases=aliases or {},
        cost_estimate=pl.CostEstimate(
            flops=0, transcendentals=0, bytes_accessed=int(micros * 3_690_000)
        ),
        compiler_params=pltpu.CompilerParams(vmem_limit_bytes=min(60 << 20, total + (8 << 20))),
        name=name,
    )(*args)


def _bytes(ref):
    size = jnp.dtype(ref.dtype).itemsize
    for n in ref.shape:
        size *= n
    return size


def body(rows, cols, pair_input, block_valid, proj_weight, out_weight, cotangent):
    row_len, col_len, width = pair_input.shape
    area = row_len * col_len
    sizes = (row_len, col_len, width)
    planes = rows // 2
    assert planes == cols and col_len == 2 * row_len and cols & (cols - 1) == 0
    assert col_len % SEG == 0 and out_weight.shape == (width, width)

    def permute(value, target):
        pairs = []
        for z in range(planes):
            for core in range(2):
                for col in range(cols):
                    to = target(z, core, col)
                    pairs.append(((2 * z + core) * cols + col, (2 * to[0] + to[1]) * cols + to[2]))
        return lax.ppermute(value, ("row", "col"), pairs)

    def in_plane(value, d):
        return permute(value, lambda z, core, col: (z, core, col ^ d))

    def across(value, d):
        return permute(value, lambda z, core, col: (z ^ d, core, col))

    def to_pair(value):
        return permute(value, lambda z, core, col: (z, core, col ^ flip(z, cols)))

    def swap(value):
        return permute(value, lambda z, core, col: (z, 1 - core, col))

    def like(*shape, dtype=F32):
        return jax.ShapeDtypeStruct(shape, dtype)

    pair = pair_input.reshape(area, width)
    cot = cotangent.reshape(area, width)
    tall, half = cols * area, 3 * width
    chunk = half // cols
    (low,) = call(norm_kernel, "norm", 0.3, [like(area, width, dtype=BF16)], [pair])
    blocks = [low] + [in_plane(low, d) for d in range(1, cols)]
    x = jnp.concatenate(blocks, axis=0)
    own_x = permute(x, lambda z, core, col: (flip(col ^ z, cols), core, col))
    cot, x = lax.optimization_barrier((cot, x))
    cot = to_pair(cot)
    left = call(
        functools.partial(project_kernel, 0, cols, sizes),
        "left",
        1.4,
        [like(cols, row_len, col_len, width)] * 3,
        [block_valid, x, proj_weight],
        smem=1,
    )
    left, cot, own_x = lax.optimization_barrier((left, cot, own_x))
    other_x = swap(own_x)
    right_shape = [like(2, cols, row_len, col_len, width)] * 3
    right = call(
        functools.partial(project_kernel, 1, cols, sizes),
        "right_own",
        1.4,
        right_shape,
        [block_valid, own_x, proj_weight],
        smem=1,
    )
    right = call(
        functools.partial(project_kernel, 2, cols, sizes),
        "right_other",
        1.4,
        right_shape,
        [block_valid, other_x, proj_weight, *right],
        smem=1,
        aliases={3: 0, 4: 1, 5: 2},
    )
    flat = pltpu.VMEM((row_len, col_len, width), F32)
    pair_out, grad_logit, wide, wg = call(
        functools.partial(mix_kernel, cols, sizes),
        "mix",
        3.0,
        [
            like(area, width),
            like(area, width, dtype=BF16),
            like(row_len, col_len, SEG, width),
            like(2 * width, width),
        ],
        [left[0], right[0], x, cot, proj_weight, out_weight],
        [flat, flat],
    )
    dl, dr = call(
        functools.partial(grads_kernel, cols, sizes),
        "grads",
        3.0,
        [like(tall, 2 * width, dtype=BF16), like(2, tall, 2 * width, dtype=BF16)],
        [*left, *right, wide],
    )
    send_w, keep_w = call(
        functools.partial(weight_sums_kernel, width),
        "weight_sums",
        1.0,
        [like(half, width, dtype=BF16), like(half, width)],
        [x, own_x, other_x, dl, dr, wg],
        [pltpu.VMEM((2, half, width), F32)],
    )
    got_w = swap(send_w)
    (send_y,) = call(
        functools.partial(back_other_kernel, cols, area, width),
        "back_other",
        0.4,
        [like(tall, width, dtype=BF16)],
        [dr, proj_weight],
    )
    got_y = swap(send_y)
    keep_y, gx = call(
        functools.partial(back_own_kernel, cols, area, width),
        "back_own",
        0.6,
        [like(tall, width)] * 2,
        [dl, dr, grad_logit, proj_weight],
    )
    mine, *chunks = call(
        functools.partial(chunks_kernel, cols),
        "chunks",
        0.1,
        [like(chunk, width)] + [like(chunk, width, dtype=BF16)] * (cols - 1),
        [keep_w, got_w],
        [pltpu.VMEM((cols, chunk, width), F32)],
    )
    (y,) = call(core_sum_kernel, "core_sum", 0.1, [like(tall, width, dtype=BF16)], [keep_y, got_y])
    back_y = permute(y, lambda z, core, col: (col ^ flip(z, cols), core, col))
    for d in range(1, cols):
        mine = mine + in_plane(chunks[d - 1], d).astype(F32)
    low_mine = mine.astype(BF16)
    low_mine, pair_out = lax.optimization_barrier((low_mine, pair_out))
    home = to_pair(pair_out)
    for d in range(1, cols):
        mine = mine + across(low_mine, d).astype(F32)
    low_mine = mine.astype(BF16)
    swapped = swap(low_mine)
    swapped, home = lax.optimization_barrier((swapped, home))
    own, *sends = call(
        functools.partial(row_sum_kernel, cols, area),
        "row_sum",
        0.1,
        [like(area, width)] + [like(area + 2 * chunk, width, dtype=BF16)] * (cols - 1),
        [gx, back_y, low_mine, swapped],
    )
    gets = [in_plane(sends[d - 1], d) for d in range(1, cols)]
    pair_grad, proj_grad, out_grad, pair_out = call(
        functools.partial(final_kernel, cols, area),
        "final",
        1.0,
        [like(area, width), like(*proj_weight.shape), like(width, width), like(area, width)],
        [own, pair, low_mine, swapped, home, *gets],
        [pltpu.VMEM((2, cols, chunk, width), F32)],
    )
    shape = pair_input.shape
    return pair_out.reshape(shape), pair_grad.reshape(shape), proj_grad, out_grad


def solution(mesh):
    return jax.shard_map(
        functools.partial(body, mesh.shape["row"], mesh.shape["col"]),
        mesh=mesh,
        in_specs=(P("row", "col", None), P(), P(), P(), P("row", "col", None)),
        out_specs=(P("row", "col", None), P("row", "col", None), P(), P()),
        check_vma=False,
    )
```

```python
import functools

import jax
import jax.numpy as jnp
from jax import lax
from jax.experimental import pallas as pl
from jax.experimental.pallas import tpu as pltpu
from jax.sharding import PartitionSpec as P

SEG = 8
F32 = jnp.float32
BF16 = jnp.bfloat16


def sigmoid(values):
    return 0.5 * jnp.tanh(0.5 * values) + 0.5


def layer_norm(values):
    center = values - jnp.mean(values, axis=-1, keepdims=True)
    scaled = lax.rsqrt(jnp.mean(center * center, axis=-1, keepdims=True) + 1e-05)
    return center * scaled, scaled


def norm_back(grad_norm, normed, scaled):
    first_mean = jnp.mean(grad_norm, axis=-1, keepdims=True)
    second = jnp.mean(grad_norm * normed, axis=-1, keepdims=True)
    return scaled * (grad_norm - first_mean - normed * second)


def dot(a, b):
    return jnp.dot(a, b, preferred_element_type=F32)


def dot_nt(a, b):
    return lax.dot_general(a, b, (((1,), (1,)), ((), ())), preferred_element_type=F32)


def dot_tn(a, b):
    return lax.dot_general(a, b, (((0,), (0,)), ((), ())), preferred_element_type=F32)


def flip(z, count):
    out, bit = z & 0, 1
    top = count >> 1
    while bit < count:
        if isinstance(z, int):
            out |= top if z & bit else 0
        else:
            out = out + jnp.where((z & bit) != 0, top, 0)
        bit, top = bit << 1, top >> 1
    return out


def place(cols):
    row, col = lax.axis_index("row"), lax.axis_index("col")
    z, core = row >> 1, row & 1
    step = flip(z, cols)
    return row, core, col, step, col ^ step


def norm_kernel(pair_ref, low_ref):
    low_ref[...] = layer_norm(pair_ref[...])[0].astype(BF16)


def project_block(projected, valid_ref, row, block, sizes, index, v_ref, a_ref, b_ref):
    row_len, col_len, width = sizes
    spot = lax.broadcasted_iota(jnp.int32, (SEG, width), 0)
    groups = col_len // SEG
    keep_col = jnp.concatenate(
        [jnp.where(spot < valid_ref[block * groups + g], 1.0, 0.0) for g in range(groups)], axis=0
    )
    for i in range(row_len):
        token = row * row_len + i
        valid = (token & (SEG - 1)) < valid_ref[token >> 3]
        keep = keep_col * jnp.where(valid, 1.0, 0.0)
        part = projected[i * col_len : (i + 1) * col_len]
        gate = sigmoid(part[:, :width])
        kept = keep * gate
        gated = kept * part[:, width:]
        v_ref[index + (i,)] = gated.astype(BF16).astype(F32)
        a_ref[index + (i,)] = gated * (1.0 - gate)
        b_ref[index + (i,)] = kept


def project_kernel(side, cols, sizes, valid_ref, x_ref, home_ref, w_ref, *refs):
    row_len, col_len, width = sizes
    area = row_len * col_len
    row, core, col, step, pair = place(cols)
    half = core if side < 2 else 1 - core
    row_here = row
    if side:
        row = 2 * pair + half
    base = 2 * width if side else 0
    outs = refs[-3:]

    def one(d):
        rows = rows_of(d, area)
        used = x_ref[rows, :]
        if side:
            used = jnp.where(pair == row_here >> 1, home_ref[rows, :], used)
            refs[-4][rows, :] = used
        projected = dot(used, w_ref[:, base : base + 2 * width])
        index = (half, d) if side else (d,)
        project_block(projected, valid_ref, row, col ^ d, sizes, index, *outs)

    by_fours(cols, one)


def tile(g):
    return slice(g * SEG, (g + 1) * SEG)


def rows_of(d, area):
    if isinstance(d, int):
        return pl.ds(d * area, area)
    return pl.ds(pl.multiple_of(d * area, area), area)


def by_fours(count, one):
    def four(q, carry):
        for n in range(4):
            one(4 * q + n)
        return carry

    if count == 4:
        four(0, 0)
    else:
        lax.fori_loop(0, count // 4, four, 0)


def gate_kernel(cols, area, width, x_ref, cot_ref, own_cot_ref, w_ref, wout_ref, gate_ref, cot_out_ref, grad_ref, low_ref):
    row, core, col, step, pair = place(cols)
    out_gate = sigmoid(dot(x_ref[rows_of(step, area), :], w_ref[:, 4 * width :]))
    gated = jnp.where(step == 0, own_cot_ref[...], cot_ref[...]) * out_gate
    low = gated.astype(BF16)
    gate_ref[...] = out_gate
    cot_out_ref[...] = gated * (1.0 - out_gate)
    low_ref[...] = low
    grad_ref[...] = dot_nt(low, wout_ref[...])


def mix_kernel(cols, sizes, lv_ref, rv_ref, back_ref, low_ref, wide_ref, mixed_ref, grad_ref):
    row_len, col_len, width = sizes
    area = row_len * col_len
    groups = col_len // SEG
    zero = jnp.zeros((SEG, width), F32)

    def mix_rows(pair_at, carry):
        for jt in range(groups):

            def over(d, acc):
                for g in range(groups):
                    left = [lv_ref[d, 2 * pair_at + a, tile(g), :] for a in range(2)]
                    right = [
                        rv_ref[j // row_len, d, j % row_len, tile(g), :]
                        for j in range(jt * SEG, (jt + 1) * SEG)
                    ]
                    acc = tuple(acc[n] + left[n // SEG] * right[n % SEG] for n in range(2 * SEG))
                return acc

            acc = lax.fori_loop(0, cols, over, (zero,) * (2 * SEG))
            for a in range(2):
                mixed_ref[2 * pair_at + a, tile(jt), :] = jnp.concatenate(
                    [jnp.sum(acc[a * SEG + n], axis=0, keepdims=True) for n in range(SEG)], axis=0
                )
        return carry

    lax.fori_loop(0, row_len // 2, mix_rows, 0)

    mixed_norm, mixed_scale = layer_norm(mixed_ref[...].reshape(area, width))
    low_ref[...] = mixed_norm.astype(BF16)
    grad_mixed = norm_back(back_ref[...], mixed_norm, mixed_scale)
    grad_ref[...] = grad_mixed.astype(BF16).astype(F32).reshape(row_len, col_len, width)

    def widen(i, carry):
        for j in range(col_len):
            wide_ref[i, j] = jnp.broadcast_to(grad_ref[i, j : j + 1, :], (SEG, width))
        return carry

    lax.fori_loop(0, row_len, widen, 0)


def gradient(load, count, first, sizes, a_ref, b_ref, index, d_ref, d_index):
    row_len, col_len, width = sizes
    groups = col_len // SEG
    acc = [[jnp.zeros((SEG, width), F32)] * groups for _ in range(4)]
    for n in range(count):
        value, weights = load(n)
        for a in range(4):
            for g in range(groups):
                acc[a][g] = acc[a][g] + value[g] * weights[a]
    full = [jnp.concatenate(acc[a], axis=0) for a in range(4)]
    gates = [full[a] * a_ref[index + (first + a,)] for a in range(4)]
    values = [full[a] * b_ref[index + (first + a,)] for a in range(4)]
    d_ref[d_index + (slice(0, width),)] = jnp.concatenate(gates, axis=0).astype(BF16)
    d_ref[d_index + (slice(width, 2 * width),)] = jnp.concatenate(values, axis=0).astype(BF16)


def grads_kernel(
    cols, sizes, lv_ref, la_ref, lb_ref, rv_ref, ra_ref, rb_ref, wide_ref, dl_ref, dr_ref
):
    row_len, col_len, width = sizes
    area = row_len * col_len
    groups = col_len // SEG
    quarter = 4 * col_len

    def spot(d, b):
        return pl.ds(pl.multiple_of(d * area + b * quarter, quarter), quarter)

    for half in range(2):

        def right_back(n, carry):
            b, d = n // cols, n % cols

            def load(i):
                return (
                    [lv_ref[d, i, tile(g), :] for g in range(groups)],
                    [wide_ref[i, half * row_len + 4 * b + a] for a in range(4)],
                )

            where = (half, spot(d, b))
            gradient(load, row_len, 4 * b, sizes, ra_ref, rb_ref, (half, d), dr_ref, where)
            return carry

        lax.fori_loop(0, (row_len // 4) * cols, right_back, 0)

    def left_back(n, carry):
        b, d = n // cols, n % cols

        def load(j):
            return (
                [rv_ref[j // row_len, d, j % row_len, tile(g), :] for g in range(groups)],
                [wide_ref[4 * b + a, j] for a in range(4)],
            )

        gradient(load, col_len, 4 * b, sizes, la_ref, lb_ref, (d,), dl_ref, (spot(d, b),))
        return carry

    lax.fori_loop(0, (row_len // 4) * cols, left_back, 0)


def weight_sums_kernel(
    cols,
    area,
    width,
    x_ref,
    own_x_ref,
    other_x_ref,
    dl_ref,
    dr_ref,
    low_ref,
    gate_ref,
    cot_ref,
    update_low_ref,
    wout_ref,
    send_ref,
    keep_ref,
    out_ref,
    logit_ref,
    sum_ref,
):
    row, core, col, step, pair = place(cols)
    update = dot(low_ref[...], wout_ref[...])
    out_ref[...] = gate_ref[...] * update
    grad_logit = (cot_ref[...] * update).astype(BF16)
    logit_ref[...] = grad_logit
    left_w = dot_tn(x_ref[...], dl_ref[...])
    right_w = dot_tn(own_x_ref[...], dr_ref[core]) + dot_tn(other_x_ref[...], dr_ref[1 - core])
    sum_ref[0, :width, :] = left_w[:, :width]
    sum_ref[0, width : 2 * width, :] = left_w[:, width:]
    sum_ref[0, 2 * width :, :] = right_w[:, :width]
    sum_ref[1, :width, :] = right_w[:, width:]
    sum_ref[1, width : 2 * width, :] = dot_tn(x_ref[rows_of(step, area), :], grad_logit)
    sum_ref[1, 2 * width :, :] = dot_tn(low_ref[...], update_low_ref[...])
    send_ref[...] = sum_ref[1 - core].astype(BF16)
    keep_ref[...] = sum_ref[core]


def back_right_kernel(cols, area, width, other, dr_ref, w_ref, part_ref):
    core = lax.axis_index("row") & 1
    half = 1 - core if other else core

    def back(d):
        rows = rows_of(d, area)
        part = dot_nt(dr_ref[half, rows, :], w_ref[:, 2 * width : 4 * width])
        part_ref[rows, :] = part.astype(part_ref.dtype)

    by_fours(cols, back)


def back_left_kernel(cols, area, width, dl_ref, logit_ref, w_ref, gx_ref):
    row, core, col, step, pair = place(cols)

    def back(d):
        rows = rows_of(d, area)
        gx_ref[rows, :] = dot_nt(dl_ref[rows, :], w_ref[:, : 2 * width])

    by_fours(cols, back)
    gx_ref[rows_of(step, area), :] += dot_nt(logit_ref[...], w_ref[:, 4 * width :])


def core_sum_kernel(keep_ref, got_ref, y_ref):
    y_ref[...] = (keep_ref[...] + got_ref[...].astype(F32)).astype(BF16)


def chunks_kernel(cols, keep_ref, got_ref, own_ref, *rest):
    chunk_refs, sum_ref = rest[:-1], rest[-1]
    col = lax.axis_index("col")
    total = keep_ref[...] + got_ref[...].astype(F32)
    sum_ref[...] = total.reshape(sum_ref.shape)
    own_ref[...] = sum_ref[col]
    for d in range(1, cols):
        chunk_refs[d - 1][...] = sum_ref[col ^ d].astype(BF16)


def row_sum_kernel(cols, area, gx_ref, got_ref, y_ref, chunk_ref, swapped_ref, own_ref, *send_refs):
    chunk = chunk_ref.shape[0]
    row, core, col, step, pair = place(cols)
    stays = pair == row >> 1

    def total(d):
        rows = slice(d * area, (d + 1) * area)
        return gx_ref[rows, :] + jnp.where(stays, y_ref[rows, :], got_ref[rows, :]).astype(F32)

    own_ref[...] = total(0)
    for d in range(1, cols):
        send_refs[d - 1][:area, :] = total(d).astype(BF16)
        send_refs[d - 1][area : area + chunk, :] = chunk_ref[...]
        send_refs[d - 1][area + chunk :, :] = swapped_ref[...]


def final_kernel(
    cols, area, own_ref, pair_ref, chunk_ref, swapped_ref, home_ref, own_out_ref, *rest
):
    got_refs = rest[: cols - 1]
    grad_ref, proj_ref, out_ref, home_out_ref, order_ref = rest[cols - 1 :]
    chunk, width = chunk_ref.shape
    row, core, col, step, pair = place(cols)
    home_out_ref[...] = jnp.where(step == 0, own_out_ref[...], home_ref[...])
    total = own_ref[...]
    order_ref[core, col] = chunk_ref[...].astype(F32)
    order_ref[1 - core, col] = swapped_ref[...].astype(F32)
    for d in range(1, cols):
        got = got_refs[d - 1]
        total = total + got[:area, :].astype(F32)
        order_ref[core, col ^ d] = got[area : area + chunk, :].astype(F32)
        order_ref[1 - core, col ^ d] = got[area + chunk :, :].astype(F32)
    normed, scaled = layer_norm(pair_ref[...])
    grad_ref[...] = norm_back(total, normed, scaled)
    whole = order_ref[...].reshape(6 * width, width)
    for n in range(5):
        proj_ref[:, n * width : (n + 1) * width] = whole[n * width : (n + 1) * width]
    out_ref[...] = whole[5 * width :]


def call(kernel, name, micros, out_shape, args, scratch=(), smem=0, aliases=None):
    specs = [pl.BlockSpec(memory_space=pltpu.SMEM if n < smem else pltpu.VMEM) for n in range(len(args))]
    total = sum(_bytes(ref) for ref in [*args, *out_shape, *scratch])
    return pl.pallas_call(
        kernel,
        out_shape=tuple(out_shape),
        in_specs=specs,
        out_specs=tuple(pl.BlockSpec(memory_space=pltpu.VMEM) for _ in out_shape),
        scratch_shapes=list(scratch),
        input_output_aliases=aliases or {},
        cost_estimate=pl.CostEstimate(
            flops=0, transcendentals=0, bytes_accessed=int(micros * 3_690_000)
        ),
        compiler_params=pltpu.CompilerParams(vmem_limit_bytes=min(60 << 20, total + (8 << 20))),
        name=name,
    )(*args)


def _bytes(ref):
    size = jnp.dtype(ref.dtype).itemsize
    for n in ref.shape:
        size *= n
    return size


def body(rows, cols, pair_input, block_valid, proj_weight, out_weight, cotangent):
    row_len, col_len, width = pair_input.shape
    area = row_len * col_len
    sizes = (row_len, col_len, width)
    planes = rows // 2
    assert planes == cols and col_len == 2 * row_len and cols & (cols - 1) == 0
    assert col_len % SEG == 0 and out_weight.shape == (width, width)

    def permute(value, target):
        pairs = []
        for z in range(planes):
            for core in range(2):
                for col in range(cols):
                    to = target(z, core, col)
                    if to == (z, core, col):
                        to = (z, 1 - core, col)
                    pairs.append(((2 * z + core) * cols + col, (2 * to[0] + to[1]) * cols + to[2]))
        return lax.ppermute(value, ("row", "col"), pairs)

    def in_plane(value, d):
        return permute(value, lambda z, core, col: (z, core, col ^ d))

    def across(value, d):
        return permute(value, lambda z, core, col: (z ^ d, core, col))

    def to_pair(value):
        return permute(value, lambda z, core, col: (z, core, col ^ flip(z, cols)))

    def swap(value):
        return permute(value, lambda z, core, col: (z, 1 - core, col))

    def like(*shape, dtype=F32):
        return jax.ShapeDtypeStruct(shape, dtype)

    pair = pair_input.reshape(area, width)
    cot = cotangent.reshape(area, width)
    tall, half = cols * area, 3 * width
    chunk = half // cols
    (low,) = call(norm_kernel, "norm", 0.3, [like(area, width, dtype=BF16)], [pair])
    blocks = [low] + [in_plane(low, d) for d in range(1, cols)]
    x = jnp.concatenate(blocks, axis=0)
    got_x = permute(x, lambda z, core, col: (flip(col ^ z, cols), core, col))
    cot, x = lax.optimization_barrier((cot, x))
    got_cot = to_pair(cot)
    left = call(
        functools.partial(project_kernel, 0, cols, sizes),
        "left",
        0.9,
        [like(cols, row_len, col_len, width)] * 3,
        [block_valid, x, x, proj_weight],
        smem=1,
    )
    out_gate, cot, back, update_low = call(
        functools.partial(gate_kernel, cols, area, width),
        "gate",
        0.3,
        [like(area, width)] * 3 + [like(area, width, dtype=BF16)],
        [x, got_cot, cot, proj_weight, out_weight],
    )
    left, back, got_x = lax.optimization_barrier((left, back, got_x))
    swapped_x = swap(got_x)
    right_shape = [like(tall, width, dtype=BF16)] + [like(2, cols, row_len, col_len, width)] * 3
    own_x, *right = call(
        functools.partial(project_kernel, 1, cols, sizes),
        "right_own",
        0.9,
        right_shape,
        [block_valid, got_x, x, proj_weight],
        smem=1,
    )
    other_x, *right = call(
        functools.partial(project_kernel, 2, cols, sizes),
        "right_other",
        0.9,
        right_shape,
        [block_valid, swapped_x, got_x, proj_weight, *right],
        smem=1,
        aliases={4: 1, 5: 2, 6: 3},
    )
    flat = pltpu.VMEM((row_len, col_len, width), F32)
    mixed_low, wide = call(
        functools.partial(mix_kernel, cols, sizes),
        "mix",
        1.8,
        [like(area, width, dtype=BF16), like(row_len, col_len, SEG, width)],
        [left[0], right[0], back],
        [flat, flat],
    )
    dl, dr = call(
        functools.partial(grads_kernel, cols, sizes),
        "grads",
        3.0,
        [like(tall, 2 * width, dtype=BF16), like(2, tall, 2 * width, dtype=BF16)],
        [*left, *right, wide],
    )
    send_w, keep_w, pair_out, grad_logit = call(
        functools.partial(weight_sums_kernel, cols, area, width),
        "weight_sums",
        0.6,
        [
            like(half, width, dtype=BF16),
            like(half, width),
            like(area, width),
            like(area, width, dtype=BF16),
        ],
        [x, own_x, other_x, dl, dr, mixed_low, out_gate, cot, update_low, out_weight],
        [pltpu.VMEM((2, half, width), F32)],
    )
    got_w = swap(send_w)
    dr, send_w = lax.optimization_barrier((dr, send_w))
    (send_y,) = call(
        functools.partial(back_right_kernel, cols, area, width, True),
        "back_other",
        0.3,
        [like(tall, width, dtype=BF16)],
        [dr, proj_weight],
    )
    got_y = swap(send_y)
    mine, *chunks = call(
        functools.partial(chunks_kernel, cols),
        "chunks",
        0.1,
        [like(chunk, width)] + [like(chunk, width, dtype=BF16)] * (cols - 1),
        [keep_w, got_w],
        [pltpu.VMEM((cols, chunk, width), F32)],
    )
    dr, dl, mine = lax.optimization_barrier((dr, dl, mine))
    (keep_y,) = call(
        functools.partial(back_right_kernel, cols, area, width, False),
        "back_own",
        0.3,
        [like(tall, width)],
        [dr, proj_weight],
    )
    (y,) = call(core_sum_kernel, "core_sum", 0.1, [like(tall, width, dtype=BF16)], [keep_y, got_y])
    back_y = permute(y, lambda z, core, col: (col ^ flip(z, cols), core, col))
    (gx,) = call(
        functools.partial(back_left_kernel, cols, area, width),
        "back_left",
        0.3,
        [like(tall, width)],
        [dl, grad_logit, proj_weight],
    )
    for d in range(1, cols):
        mine = mine + in_plane(chunks[d - 1], d).astype(F32)
    low_mine = mine.astype(BF16)
    low_mine, pair_out, gx = lax.optimization_barrier((low_mine, pair_out, gx))
    home = to_pair(pair_out)
    for d in range(1, cols):
        mine = mine + across(low_mine, d).astype(F32)
    low_mine = mine.astype(BF16)
    swapped = swap(low_mine)
    swapped, home = lax.optimization_barrier((swapped, home))
    own, *sends = call(
        functools.partial(row_sum_kernel, cols, area),
        "row_sum",
        0.1,
        [like(area, width)] + [like(area + 2 * chunk, width, dtype=BF16)] * (cols - 1),
        [gx, back_y, y, low_mine, swapped],
    )
    gets = [in_plane(sends[d - 1], d) for d in range(1, cols)]
    pair_grad, proj_grad, out_grad, pair_out = call(
        functools.partial(final_kernel, cols, area),
        "final",
        1.0,
        [like(area, width), like(*proj_weight.shape), like(width, width), like(area, width)],
        [own, pair, low_mine, swapped, home, pair_out, *gets],
        [pltpu.VMEM((2, cols, chunk, width), F32)],
    )
    shape = pair_input.shape
    return pair_out.reshape(shape), pair_grad.reshape(shape), proj_grad, out_grad


def solution(mesh):
    return jax.shard_map(
        functools.partial(body, mesh.shape["row"], mesh.shape["col"]),
        mesh=mesh,
        in_specs=(P("row", "col", None), P(), P(), P(), P("row", "col", None)),
        out_specs=(P("row", "col", None), P("row", "col", None), P(), P()),
        check_vma=False,
    )
```

```python
import functools

import jax
import jax.numpy as jnp
from jax import lax
from jax.experimental import pallas as pl
from jax.experimental.pallas import tpu as pltpu
from jax.sharding import PartitionSpec as P

SEG = 8
F32 = jnp.float32
BF16 = jnp.bfloat16


def sigmoid(values):
    return 0.5 * jnp.tanh(0.5 * values) + 0.5


def layer_norm(values):
    center = values - jnp.mean(values, axis=-1, keepdims=True)
    scaled = lax.rsqrt(jnp.mean(center * center, axis=-1, keepdims=True) + 1e-05)
    return center * scaled, scaled


def norm_back(grad_norm, normed, scaled):
    first_mean = jnp.mean(grad_norm, axis=-1, keepdims=True)
    second = jnp.mean(grad_norm * normed, axis=-1, keepdims=True)
    return scaled * (grad_norm - first_mean - normed * second)


def dot(a, b):
    return jnp.dot(a, b, preferred_element_type=F32)


def dot_nt(a, b):
    return lax.dot_general(a, b, (((1,), (1,)), ((), ())), preferred_element_type=F32)


def dot_tn(a, b):
    return lax.dot_general(a, b, (((0,), (0,)), ((), ())), preferred_element_type=F32)


def flip(z, count):
    out, bit = z & 0, 1
    top = count >> 1
    while bit < count:
        if isinstance(z, int):
            out |= top if z & bit else 0
        else:
            out = out + jnp.where((z & bit) != 0, top, 0)
        bit, top = bit << 1, top >> 1
    return out


def place(cols):
    row, col = lax.axis_index("row"), lax.axis_index("col")
    z, core = row >> 1, row & 1
    step = flip(z, cols)
    return row, core, col, step, col ^ step


def norm_kernel(pair_ref, low_ref):
    low_ref[...] = layer_norm(pair_ref[...])[0].astype(BF16)


def mask_kernel(valid_ref, mask_ref):
    spot = lax.broadcasted_iota(jnp.int32, (SEG, mask_ref.shape[1]), 0)
    for g in range(mask_ref.shape[0] // SEG):
        mask_ref[tile(g), :] = jnp.where(spot < valid_ref[g], 1.0, 0.0)


def project_block(projected, mask_ref, row, block, sizes, index, v_ref, a_ref, b_ref):
    row_len, col_len, width = sizes
    keep_col = mask_ref[pl.ds(pl.multiple_of(block * col_len, SEG), col_len), :]
    for i in range(row_len):
        keep = keep_col * mask_ref[pl.ds(row * row_len + i, 1), :]
        part = projected[i * col_len : (i + 1) * col_len]
        gate = sigmoid(part[:, :width])
        kept = keep * gate
        gated = kept * part[:, width:]
        v_ref[index + (i,)] = gated.astype(BF16).astype(F32)
        a_ref[index + (i,)] = gated * (1.0 - gate)
        b_ref[index + (i,)] = kept


def project_kernel(side, cols, sizes, mask_ref, x_ref, home_ref, w_ref, *refs):
    row_len, col_len, width = sizes
    area = row_len * col_len
    row, core, col, step, pair = place(cols)
    half = core if side < 2 else 1 - core
    row_here = row
    if side:
        row = 2 * pair + half
    base = 2 * width if side else 0
    outs = refs[-3:]

    def one(d):
        rows = rows_of(d, area)
        used = x_ref[rows, :]
        if side:
            used = jnp.where(pair == row_here >> 1, home_ref[rows, :], used)
            refs[-4][rows, :] = used
        projected = dot(used, w_ref[:, base : base + 2 * width])
        index = (half, d) if side else (d,)
        project_block(projected, mask_ref, row, col ^ d, sizes, index, *outs)

    by_fours(cols, one)


def tile(g):
    return slice(g * SEG, (g + 1) * SEG)


def rows_of(d, area):
    if isinstance(d, int):
        return pl.ds(d * area, area)
    return pl.ds(pl.multiple_of(d * area, area), area)


def by_fours(count, one):
    def four(q, carry):
        for n in range(4):
            one(4 * q + n)
        return carry

    if count == 4:
        four(0, 0)
    else:
        lax.fori_loop(0, count // 4, four, 0)


def gate_kernel(cols, area, width, x_ref, cot_ref, own_cot_ref, w_ref, wout_ref, gate_ref, cot_out_ref, grad_ref, low_ref):
    row, core, col, step, pair = place(cols)
    out_gate = sigmoid(dot(x_ref[rows_of(step, area), :], w_ref[:, 4 * width :]))
    gated = jnp.where(step == 0, own_cot_ref[...], cot_ref[...]) * out_gate
    low = gated.astype(BF16)
    gate_ref[...] = out_gate
    cot_out_ref[...] = gated * (1.0 - out_gate)
    low_ref[...] = low
    grad_ref[...] = dot_nt(low, wout_ref[...])


def mix_kernel(cols, sizes, lv_ref, rv_ref, back_ref, low_ref, wide_ref, mixed_ref, grad_ref):
    row_len, col_len, width = sizes
    area = row_len * col_len
    groups = col_len // SEG
    zero = jnp.zeros((SEG, width), F32)

    def mix_rows(pair_at, carry):
        for jt in range(groups):

            def over(d, acc):
                for g in range(groups):
                    left = [lv_ref[d, 2 * pair_at + a, tile(g), :] for a in range(2)]
                    right = [
                        rv_ref[j // row_len, d, j % row_len, tile(g), :]
                        for j in range(jt * SEG, (jt + 1) * SEG)
                    ]
                    acc = tuple(acc[n] + left[n // SEG] * right[n % SEG] for n in range(2 * SEG))
                return acc

            acc = lax.fori_loop(0, cols, over, (zero,) * (2 * SEG))
            for a in range(2):
                mixed_ref[2 * pair_at + a, tile(jt), :] = jnp.concatenate(
                    [jnp.sum(acc[a * SEG + n], axis=0, keepdims=True) for n in range(SEG)], axis=0
                )
        return carry

    lax.fori_loop(0, row_len // 2, mix_rows, 0)

    mixed_norm, mixed_scale = layer_norm(mixed_ref[...].reshape(area, width))
    low_ref[...] = mixed_norm.astype(BF16)
    grad_mixed = norm_back(back_ref[...], mixed_norm, mixed_scale)
    grad_ref[...] = grad_mixed.astype(BF16).astype(F32).reshape(row_len, col_len, width)

    def widen(i, carry):
        for j in range(col_len):
            wide_ref[i, j] = jnp.broadcast_to(grad_ref[i, j : j + 1, :], (SEG, width))
        return carry

    lax.fori_loop(0, row_len, widen, 0)


def gradient(load, count, first, sizes, a_ref, b_ref, index, d_ref, d_index):
    row_len, col_len, width = sizes
    groups = col_len // SEG
    acc = [[jnp.zeros((SEG, width), F32)] * groups for _ in range(4)]
    for n in range(count):
        value, weights = load(n)
        for a in range(4):
            for g in range(groups):
                acc[a][g] = acc[a][g] + value[g] * weights[a]
    full = [jnp.concatenate(acc[a], axis=0) for a in range(4)]
    gates = [full[a] * a_ref[index + (first + a,)] for a in range(4)]
    values = [full[a] * b_ref[index + (first + a,)] for a in range(4)]
    d_ref[d_index + (slice(0, width),)] = jnp.concatenate(gates, axis=0).astype(BF16)
    d_ref[d_index + (slice(width, 2 * width),)] = jnp.concatenate(values, axis=0).astype(BF16)


def grads_kernel(
    cols, sizes, lv_ref, la_ref, lb_ref, rv_ref, ra_ref, rb_ref, wide_ref, dl_ref, dr_ref
):
    row_len, col_len, width = sizes
    area = row_len * col_len
    groups = col_len // SEG
    quarter = 4 * col_len

    def spot(d, b):
        return pl.ds(pl.multiple_of(d * area + b * quarter, quarter), quarter)

    for half in range(2):

        def right_back(n, carry):
            b, d = n // cols, n % cols

            def load(i):
                return (
                    [lv_ref[d, i, tile(g), :] for g in range(groups)],
                    [wide_ref[i, half * row_len + 4 * b + a] for a in range(4)],
                )

            where = (half, spot(d, b))
            gradient(load, row_len, 4 * b, sizes, ra_ref, rb_ref, (half, d), dr_ref, where)
            return carry

        lax.fori_loop(0, (row_len // 4) * cols, right_back, 0)

    def left_back(n, carry):
        b, d = n // cols, n % cols

        def load(j):
            return (
                [rv_ref[j // row_len, d, j % row_len, tile(g), :] for g in range(groups)],
                [wide_ref[4 * b + a, j] for a in range(4)],
            )

        gradient(load, col_len, 4 * b, sizes, la_ref, lb_ref, (d,), dl_ref, (spot(d, b),))
        return carry

    lax.fori_loop(0, (row_len // 4) * cols, left_back, 0)


def weight_sums_kernel(
    cols,
    area,
    width,
    x_ref,
    own_x_ref,
    other_x_ref,
    dl_ref,
    dr_ref,
    low_ref,
    gate_ref,
    cot_ref,
    update_low_ref,
    wout_ref,
    send_ref,
    keep_ref,
    out_ref,
    logit_ref,
    sum_ref,
):
    row, core, col, step, pair = place(cols)
    update = dot(low_ref[...], wout_ref[...])
    out_ref[...] = gate_ref[...] * update
    grad_logit = (cot_ref[...] * update).astype(BF16)
    logit_ref[...] = grad_logit
    left_w = dot_tn(x_ref[...], dl_ref[...])
    right_w = dot_tn(own_x_ref[...], dr_ref[core]) + dot_tn(other_x_ref[...], dr_ref[1 - core])
    sum_ref[0, :width, :] = left_w[:, :width]
    sum_ref[0, width : 2 * width, :] = left_w[:, width:]
    sum_ref[0, 2 * width :, :] = right_w[:, :width]
    sum_ref[1, :width, :] = right_w[:, width:]
    sum_ref[1, width : 2 * width, :] = dot_tn(x_ref[rows_of(step, area), :], grad_logit)
    sum_ref[1, 2 * width :, :] = dot_tn(low_ref[...], update_low_ref[...])
    send_ref[...] = sum_ref[1 - core].astype(BF16)
    keep_ref[...] = sum_ref[core]


def back_right_kernel(cols, area, width, other, dr_ref, w_ref, part_ref):
    core = lax.axis_index("row") & 1
    half = 1 - core if other else core

    def back(d):
        rows = rows_of(d, area)
        part = dot_nt(dr_ref[half, rows, :], w_ref[:, 2 * width : 4 * width])
        part_ref[rows, :] = part.astype(part_ref.dtype)

    by_fours(cols, back)


def back_left_kernel(cols, area, width, dl_ref, logit_ref, w_ref, gx_ref):
    row, core, col, step, pair = place(cols)

    def back(d):
        rows = rows_of(d, area)
        gx_ref[rows, :] = dot_nt(dl_ref[rows, :], w_ref[:, : 2 * width])

    by_fours(cols, back)
    gx_ref[rows_of(step, area), :] += dot_nt(logit_ref[...], w_ref[:, 4 * width :])


def core_sum_kernel(keep_ref, got_ref, y_ref):
    y_ref[...] = (keep_ref[...] + got_ref[...].astype(F32)).astype(BF16)


def chunks_kernel(cols, keep_ref, got_ref, own_ref, *rest):
    chunk_refs, sum_ref = rest[:-1], rest[-1]
    col = lax.axis_index("col")
    total = keep_ref[...] + got_ref[...].astype(F32)
    sum_ref[...] = total.reshape(sum_ref.shape)
    own_ref[...] = sum_ref[col]
    for d in range(1, cols):
        chunk_refs[d - 1][...] = sum_ref[col ^ d].astype(BF16)


def row_sum_kernel(cols, area, gx_ref, got_ref, y_ref, chunk_ref, own_ref, *send_refs):
    row, core, col, step, pair = place(cols)
    stays = pair == row >> 1

    def total(d):
        rows = slice(d * area, (d + 1) * area)
        return gx_ref[rows, :] + jnp.where(stays, y_ref[rows, :], got_ref[rows, :]).astype(F32)

    own_ref[...] = total(0)
    for d in range(1, cols):
        send_refs[d - 1][:area, :] = total(d).astype(BF16)
        send_refs[d - 1][area:, :] = chunk_ref[...]


def join_kernel(cols, area, chunk_ref, *rest):
    got_refs, (half_ref, order_ref) = rest[: cols - 1], rest[cols - 1 :]
    col = lax.axis_index("col")
    order_ref[col] = chunk_ref[...].astype(F32)
    for d in range(1, cols):
        order_ref[col ^ d] = got_refs[d - 1][area:, :].astype(F32)
    half_ref[...] = order_ref[...].reshape(half_ref.shape).astype(BF16)


def pair_grad_kernel(cols, area, own_ref, pair_ref, home_ref, own_out_ref, *rest):
    got_refs, (grad_ref, out_ref) = rest[:-2], rest[-2:]
    row, core, col, step, pair = place(cols)
    out_ref[...] = jnp.where(step == 0, own_out_ref[...], home_ref[...])
    total = own_ref[...]
    for got in got_refs:
        total = total + got[:area, :].astype(F32)
    normed, scaled = layer_norm(pair_ref[...])
    grad_ref[...] = norm_back(total, normed, scaled)


def weights_kernel(width, mine_ref, other_ref, proj_ref, out_ref):
    first = (lax.axis_index("row") & 1) == 0
    mine, other = mine_ref[...].astype(F32), other_ref[...].astype(F32)
    low, high = jnp.where(first, mine, other), jnp.where(first, other, mine)
    for n in range(3):
        proj_ref[:, n * width : (n + 1) * width] = low[n * width : (n + 1) * width]
    for n in range(2):
        proj_ref[:, (3 + n) * width : (4 + n) * width] = high[n * width : (n + 1) * width]
    out_ref[...] = high[2 * width :]


def call(kernel, name, micros, out_shape, args, scratch=(), aliases=None, space=pltpu.VMEM):
    specs = [pl.BlockSpec(memory_space=space) for _ in args]
    total = sum(_bytes(ref) for ref in [*args, *out_shape, *scratch])
    return pl.pallas_call(
        kernel,
        out_shape=tuple(out_shape),
        in_specs=specs,
        out_specs=tuple(pl.BlockSpec(memory_space=pltpu.VMEM) for _ in out_shape),
        scratch_shapes=list(scratch),
        input_output_aliases=aliases or {},
        cost_estimate=pl.CostEstimate(
            flops=0, transcendentals=0, bytes_accessed=int(micros * 3_690_000)
        ),
        compiler_params=pltpu.CompilerParams(vmem_limit_bytes=min(60 << 20, total + (8 << 20))),
        name=name,
    )(*args)


def _bytes(ref):
    size = jnp.dtype(ref.dtype).itemsize
    for n in ref.shape:
        size *= n
    return size


def body(rows, cols, pair_input, block_valid, proj_weight, out_weight, cotangent):
    row_len, col_len, width = pair_input.shape
    area = row_len * col_len
    sizes = (row_len, col_len, width)
    planes = rows // 2
    assert planes == cols and col_len == 2 * row_len and cols & (cols - 1) == 0
    assert col_len % SEG == 0 and out_weight.shape == (width, width)

    def permute(value, target):
        pairs = []
        for z in range(planes):
            for core in range(2):
                for col in range(cols):
                    to = target(z, core, col)
                    if to == (z, core, col):
                        to = (z, 1 - core, col)
                    pairs.append(((2 * z + core) * cols + col, (2 * to[0] + to[1]) * cols + to[2]))
        return lax.ppermute(value, ("row", "col"), pairs)

    def in_plane(value, d):
        return permute(value, lambda z, core, col: (z, core, col ^ d))

    def across(value, d):
        return permute(value, lambda z, core, col: (z ^ d, core, col))

    def to_pair(value):
        return permute(value, lambda z, core, col: (z, core, col ^ flip(z, cols)))

    def swap(value):
        return permute(value, lambda z, core, col: (z, 1 - core, col))

    def like(*shape, dtype=F32):
        return jax.ShapeDtypeStruct(shape, dtype)

    pair = pair_input.reshape(area, width)
    cot = cotangent.reshape(area, width)
    tall, half = cols * area, 3 * width
    chunk = half // cols
    (low,) = call(norm_kernel, "norm", 0.3, [like(area, width, dtype=BF16)], [pair])
    blocks = [low] + [in_plane(low, d) for d in range(1, cols)]
    x = jnp.concatenate(blocks, axis=0)
    got_x = permute(x, lambda z, core, col: (flip(col ^ z, cols), core, col))
    cot, x, block_valid = lax.optimization_barrier((cot, x, block_valid))
    got_cot = to_pair(cot)
    (mask,) = call(
        mask_kernel, "mask", 0.1, [like(col_len * cols, width)], [block_valid], space=pltpu.SMEM
    )
    left = call(
        functools.partial(project_kernel, 0, cols, sizes),
        "left",
        0.9,
        [like(cols, row_len, col_len, width)] * 3,
        [mask, x, x, proj_weight],
    )
    out_gate, cot, back, update_low = call(
        functools.partial(gate_kernel, cols, area, width),
        "gate",
        0.3,
        [like(area, width)] * 3 + [like(area, width, dtype=BF16)],
        [x, got_cot, cot, proj_weight, out_weight],
    )
    left, back, got_x = lax.optimization_barrier((left, back, got_x))
    swapped_x = swap(got_x)
    right_shape = [like(tall, width, dtype=BF16)] + [like(2, cols, row_len, col_len, width)] * 3
    own_x, *right = call(
        functools.partial(project_kernel, 1, cols, sizes),
        "right_own",
        0.9,
        right_shape,
        [mask, got_x, x, proj_weight],
    )
    other_x, *right = call(
        functools.partial(project_kernel, 2, cols, sizes),
        "right_other",
        0.9,
        right_shape,
        [mask, swapped_x, got_x, proj_weight, *right],
        aliases={4: 1, 5: 2, 6: 3},
    )
    flat = pltpu.VMEM((row_len, col_len, width), F32)
    mixed_low, wide = call(
        functools.partial(mix_kernel, cols, sizes),
        "mix",
        1.8,
        [like(area, width, dtype=BF16), like(row_len, col_len, SEG, width)],
        [left[0], right[0], back],
        [flat, flat],
    )
    dl, dr = call(
        functools.partial(grads_kernel, cols, sizes),
        "grads",
        3.0,
        [like(tall, 2 * width, dtype=BF16), like(2, tall, 2 * width, dtype=BF16)],
        [*left, *right, wide],
    )
    send_w, keep_w, pair_out, grad_logit = call(
        functools.partial(weight_sums_kernel, cols, area, width),
        "weight_sums",
        0.6,
        [
            like(half, width, dtype=BF16),
            like(half, width),
            like(area, width),
            like(area, width, dtype=BF16),
        ],
        [x, own_x, other_x, dl, dr, mixed_low, out_gate, cot, update_low, out_weight],
        [pltpu.VMEM((2, half, width), F32)],
    )
    got_w = swap(send_w)
    dr, send_w = lax.optimization_barrier((dr, send_w))
    (send_y,) = call(
        functools.partial(back_right_kernel, cols, area, width, True),
        "back_other",
        0.3,
        [like(tall, width, dtype=BF16)],
        [dr, proj_weight],
    )
    got_y = swap(send_y)
    mine, *chunks = call(
        functools.partial(chunks_kernel, cols),
        "chunks",
        0.1,
        [like(chunk, width)] + [like(chunk, width, dtype=BF16)] * (cols - 1),
        [keep_w, got_w],
        [pltpu.VMEM((cols, chunk, width), F32)],
    )
    dr, dl, mine = lax.optimization_barrier((dr, dl, mine))
    (keep_y,) = call(
        functools.partial(back_right_kernel, cols, area, width, False),
        "back_own",
        0.3,
        [like(tall, width)],
        [dr, proj_weight],
    )
    (y,) = call(core_sum_kernel, "core_sum", 0.1, [like(tall, width, dtype=BF16)], [keep_y, got_y])
    back_y = permute(y, lambda z, core, col: (col ^ flip(z, cols), core, col))
    (gx,) = call(
        functools.partial(back_left_kernel, cols, area, width),
        "back_left",
        0.3,
        [like(tall, width)],
        [dl, grad_logit, proj_weight],
    )
    for d in range(1, cols):
        mine = mine + in_plane(chunks[d - 1], d).astype(F32)
    low_mine = mine.astype(BF16)
    low_mine, pair_out, gx = lax.optimization_barrier((low_mine, pair_out, gx))
    home = to_pair(pair_out)
    for d in range(1, cols):
        mine = mine + across(low_mine, d).astype(F32)
    low_mine = mine.astype(BF16)
    low_mine, home = lax.optimization_barrier((low_mine, home))
    own, *sends = call(
        functools.partial(row_sum_kernel, cols, area),
        "row_sum",
        0.1,
        [like(area, width)] + [like(area + chunk, width, dtype=BF16)] * (cols - 1),
        [gx, back_y, y, low_mine],
    )
    gets = [in_plane(sends[d - 1], d) for d in range(1, cols)]
    (half_w,) = call(
        functools.partial(join_kernel, cols, area),
        "join",
        0.1,
        [like(half, width, dtype=BF16)],
        [low_mine, *gets],
        [pltpu.VMEM((cols, chunk, width), F32)],
    )
    other_w = swap(half_w)
    half_w, own = lax.optimization_barrier((half_w, own))
    pair_grad, pair_out = call(
        functools.partial(pair_grad_kernel, cols, area),
        "pair_grad",
        1.0,
        [like(area, width)] * 2,
        [own, pair, home, pair_out, *gets],
    )
    proj_grad, out_grad = call(
        functools.partial(weights_kernel, width),
        "weights",
        0.8,
        [like(*proj_weight.shape), like(width, width)],
        [half_w, other_w],
    )
    shape = pair_input.shape
    return pair_out.reshape(shape), pair_grad.reshape(shape), proj_grad, out_grad


def solution(mesh):
    return jax.shard_map(
        functools.partial(body, mesh.shape["row"], mesh.shape["col"]),
        mesh=mesh,
        in_specs=(P("row", "col", None), P(), P(), P(), P("row", "col", None)),
        out_specs=(P("row", "col", None), P("row", "col", None), P(), P()),
        check_vma=False,
    )
```

```python
import functools

import jax
import jax.numpy as jnp
from jax import lax
from jax.experimental import pallas as pl
from jax.experimental.pallas import tpu as pltpu
from jax.sharding import PartitionSpec as P

SEG = 8
F32 = jnp.float32
BF16 = jnp.bfloat16


def sigmoid(values):
    return 0.5 * jnp.tanh(0.5 * values) + 0.5


def layer_norm(values):
    center = values - jnp.mean(values, axis=-1, keepdims=True)
    scaled = lax.rsqrt(jnp.mean(center * center, axis=-1, keepdims=True) + 1e-05)
    return center * scaled, scaled


def norm_back(grad_norm, normed, scaled):
    first_mean = jnp.mean(grad_norm, axis=-1, keepdims=True)
    second = jnp.mean(grad_norm * normed, axis=-1, keepdims=True)
    return scaled * (grad_norm - first_mean - normed * second)


def dot(a, b):
    return jnp.dot(a, b, preferred_element_type=F32)


def dot_nt(a, b):
    return lax.dot_general(a, b, (((1,), (1,)), ((), ())), preferred_element_type=F32)


def dot_tn(a, b):
    return lax.dot_general(a, b, (((0,), (0,)), ((), ())), preferred_element_type=F32)


def flip(z, count):
    out, bit = z & 0, 1
    top = count >> 1
    while bit < count:
        if isinstance(z, int):
            out |= top if z & bit else 0
        else:
            out = out + jnp.where((z & bit) != 0, top, 0)
        bit, top = bit << 1, top >> 1
    return out


def place(cols):
    row, col = lax.axis_index("row"), lax.axis_index("col")
    z, core = row >> 1, row & 1
    step = flip(z, cols)
    return row, core, col, step, col ^ step


def norm_kernel(pair_ref, low_ref):
    low_ref[...] = layer_norm(pair_ref[...])[0].astype(BF16)


def mask_kernel(valid_ref, mask_ref):
    spot = lax.broadcasted_iota(jnp.int32, (SEG, mask_ref.shape[1]), 0)
    for g in range(mask_ref.shape[0] // SEG):
        mask_ref[tile(g), :] = jnp.where(spot < valid_ref[g], 1.0, 0.0)


def project_block(projected, mask_ref, row, block, sizes, index, v_ref, a_ref, b_ref):
    row_len, col_len, width = sizes
    keep_col = mask_ref[pl.ds(pl.multiple_of(block * col_len, SEG), col_len), :]
    for i in range(row_len):
        keep = keep_col * mask_ref[pl.ds(row * row_len + i, 1), :]
        part = projected[i * col_len : (i + 1) * col_len]
        gate = sigmoid(part[:, :width])
        kept = keep * gate
        gated = kept * part[:, width:]
        v_ref[index + (i,)] = gated.astype(BF16).astype(F32)
        a_ref[index + (i,)] = gated * (1.0 - gate)
        b_ref[index + (i,)] = kept


def project_kernel(side, cols, sizes, mask_ref, x_ref, home_ref, w_ref, *refs):
    row_len, col_len, width = sizes
    area = row_len * col_len
    row, core, col, step, pair = place(cols)
    stays = pair == row >> 1
    if side:
        row = 2 * pair + (core if side == 1 else 1 - core)
    base = 2 * width if side else 0

    def one(d):
        rows = rows_of(d, area)
        used = x_ref[rows, :]
        if side:
            used = jnp.where(stays, home_ref[rows, :], used)
            refs[0][rows, :] = used
        projected = dot(used, w_ref[:, base : base + 2 * width])
        project_block(projected, mask_ref, row, col ^ d, sizes, (d,), *refs[-3:])

    by_fours(cols, one)


def tile(g):
    return slice(g * SEG, (g + 1) * SEG)


def rows_of(d, area):
    if isinstance(d, int):
        return pl.ds(d * area, area)
    return pl.ds(pl.multiple_of(d * area, area), area)


def by_fours(count, one):
    def four(q, carry):
        for n in range(4):
            one(4 * q + n)
        return carry

    if count == 4:
        four(0, 0)
    else:
        lax.fori_loop(0, count // 4, four, 0)


def gate_kernel(cols, area, width, x_ref, cot_ref, own_cot_ref, w_ref, wout_ref, gate_ref, cot_out_ref, grad_ref, low_ref):
    row, core, col, step, pair = place(cols)
    out_gate = sigmoid(dot(x_ref[rows_of(step, area), :], w_ref[:, 4 * width :]))
    gated = jnp.where(step == 0, own_cot_ref[...], cot_ref[...]) * out_gate
    low = gated.astype(BF16)
    gate_ref[...] = out_gate
    cot_out_ref[...] = gated * (1.0 - out_gate)
    low_ref[...] = low
    grad_ref[...] = dot_nt(low, wout_ref[...])


def fold(parts):
    spot = lax.broadcasted_iota(jnp.int32, parts[0].shape, 0)
    shift = 1
    while len(parts) > 1:
        first = (spot & shift) == 0
        parts = [
            jnp.where(first, a, b) + pltpu.roll(jnp.where(first, b, a), shift, 0)
            for a, b in zip(parts[::2], parts[1::2])
        ]
        shift *= 2
    return parts[0]


def block_of(row_len):
    return next(n for n in (6, 4, 2) if row_len % n == 0)


def mix_half(cols, sizes, lv_ref, rv_ref, mixed_ref):
    row_len, col_len, width = sizes
    groups = col_len // SEG
    many = block_of(row_len)
    zero = jnp.zeros((SEG, width), F32)

    def rows(block, carry):
        start = block * many
        for jt in range(row_len // 4):

            def over(q, acc):
                for d in range(4):
                    for g in range(groups):
                        left = [lv_ref[4 * q + d, start + a, tile(g), :] for a in range(many)]
                        right = [rv_ref[4 * q + d, 4 * jt + n, tile(g), :] for n in range(4)]
                        acc = tuple(
                            acc[4 * a + n] + left[a] * right[n] for a in range(many) for n in range(4)
                        )
                return acc

            acc = (zero,) * (4 * many)
            acc = over(0, acc) if cols == 4 else lax.fori_loop(0, cols // 4, over, acc)
            for a in range(0, many, 2):
                sums = fold(list(acc[4 * a : 4 * a + 8]))
                mixed_ref[start + a, 4 * jt : 4 * jt + 4, :] = sums[:4]
                mixed_ref[start + a + 1, 4 * jt : 4 * jt + 4, :] = sums[4:]
        return carry

    lax.fori_loop(0, row_len // many, rows, 0)


def mix_own_kernel(cols, sizes, lv_ref, rv_ref, mixed_ref):
    mix_half(cols, sizes, lv_ref, rv_ref, mixed_ref)


def mix_kernel(
    cols, sizes, lv_ref, rv_ref, own_ref, back_ref, low_ref, wide_ref, other_ref, grad_ref
):
    row_len, col_len, width = sizes
    area = row_len * col_len
    mix_half(cols, sizes, lv_ref, rv_ref, other_ref)
    first = (lax.axis_index("row") & 1) == 0
    for i in range(row_len):
        own, other = own_ref[i], other_ref[i]
        low, high = jnp.where(first, own, other), jnp.where(first, other, own)
        grad_ref[i, :row_len, :] = low[:row_len]
        grad_ref[i, row_len:, :] = high[:row_len]
    mixed_norm, mixed_scale = layer_norm(grad_ref[...].reshape(area, width))
    low_ref[...] = mixed_norm.astype(BF16)
    grad_mixed = norm_back(back_ref[...], mixed_norm, mixed_scale)
    grad_ref[...] = grad_mixed.astype(BF16).astype(F32).reshape(row_len, col_len, width)

    def widen(i, carry):
        for j in range(col_len):
            wide_ref[i, j] = jnp.broadcast_to(grad_ref[i, j : j + 1, :], (SEG, width))
        return carry

    lax.fori_loop(0, row_len, widen, 0)


def gradient(load, count, many, first, sizes, a_ref, b_ref, d, d_ref):
    row_len, col_len, width = sizes
    groups = col_len // SEG
    acc = [[jnp.zeros((SEG, width), F32)] * groups for _ in range(many)]
    for n in range(count):
        value, weights = load(n)
        for a in range(many):
            for g in range(groups):
                acc[a][g] = acc[a][g] + value[g] * weights[a]
    full = [jnp.concatenate(acc[a], axis=0) for a in range(many)]
    gates = [full[a] * a_ref[d, first + a] for a in range(many)]
    values = [full[a] * b_ref[d, first + a] for a in range(many)]
    start = pl.multiple_of((d * row_len + first) * col_len, many * col_len)
    rows = pl.ds(start, many * col_len)
    d_ref[rows, :width] = jnp.concatenate(gates, axis=0).astype(BF16)
    d_ref[rows, width:] = jnp.concatenate(values, axis=0).astype(BF16)


def grads_kernel(
    cols,
    sizes,
    lv_ref,
    la_ref,
    lb_ref,
    ov_ref,
    oa_ref,
    ob_ref,
    rv_ref,
    ra_ref,
    rb_ref,
    wide_ref,
    dl_ref,
    do_ref,
    dr_ref,
):
    row_len, col_len, width = sizes
    groups = col_len // SEG
    many = block_of(row_len)
    core = lax.axis_index("row") & 1

    def blocks(one):
        def at(n, carry):
            one(n // cols * many, n % cols)
            return carry

        lax.fori_loop(0, row_len // many * cols, at, 0)

    def right_back(base, a_ref, b_ref, d_ref):
        def one(first, d):
            def load(i):
                return (
                    [lv_ref[d, i, tile(g), :] for g in range(groups)],
                    [wide_ref[i, base + first + a] for a in range(many)],
                )

            gradient(load, row_len, many, first, sizes, a_ref, b_ref, d, d_ref)

        blocks(one)

    right_back(core * row_len, oa_ref, ob_ref, do_ref)
    right_back((1 - core) * row_len, ra_ref, rb_ref, dr_ref)

    def left_back(first, d):
        def load(n):
            ref = ov_ref if n < row_len else rv_ref
            j = (core if n < row_len else 1 - core) * row_len + n % row_len
            return (
                [ref[d, n % row_len, tile(g), :] for g in range(groups)],
                [wide_ref[first + a, j] for a in range(many)],
            )

        gradient(load, col_len, many, first, sizes, la_ref, lb_ref, d, dl_ref)

    blocks(left_back)


def weight_sums_kernel(
    cols,
    area,
    width,
    x_ref,
    own_x_ref,
    other_x_ref,
    dl_ref,
    do_ref,
    dr_ref,
    low_ref,
    gate_ref,
    cot_ref,
    update_low_ref,
    wout_ref,
    send_ref,
    keep_ref,
    out_ref,
    logit_ref,
    sum_ref,
):
    row, core, col, step, pair = place(cols)
    update = dot(low_ref[...], wout_ref[...])
    out_ref[...] = gate_ref[...] * update
    grad_logit = (cot_ref[...] * update).astype(BF16)
    logit_ref[...] = grad_logit
    left_w = dot_tn(x_ref[...], dl_ref[...])
    right_w = dot_tn(own_x_ref[...], do_ref[...]) + dot_tn(other_x_ref[...], dr_ref[...])
    sum_ref[0, :width, :] = left_w[:, :width]
    sum_ref[0, width : 2 * width, :] = left_w[:, width:]
    sum_ref[0, 2 * width :, :] = right_w[:, :width]
    sum_ref[1, :width, :] = right_w[:, width:]
    sum_ref[1, width : 2 * width, :] = dot_tn(x_ref[rows_of(step, area), :], grad_logit)
    sum_ref[1, 2 * width :, :] = dot_tn(low_ref[...], update_low_ref[...])
    send_ref[...] = sum_ref[1 - core].astype(BF16)
    keep_ref[...] = sum_ref[core]


def back_right_kernel(cols, area, width, dr_ref, w_ref, part_ref):
    def back(d):
        rows = rows_of(d, area)
        part = dot_nt(dr_ref[rows, :], w_ref[:, 2 * width : 4 * width])
        part_ref[rows, :] = part.astype(part_ref.dtype)

    by_fours(cols, back)


def back_left_kernel(cols, area, width, dl_ref, logit_ref, w_ref, gx_ref):
    row, core, col, step, pair = place(cols)

    def back(d):
        rows = rows_of(d, area)
        gx_ref[rows, :] = dot_nt(dl_ref[rows, :], w_ref[:, : 2 * width])

    by_fours(cols, back)
    gx_ref[rows_of(step, area), :] += dot_nt(logit_ref[...], w_ref[:, 4 * width :])


def core_sum_kernel(keep_ref, got_ref, y_ref):
    y_ref[...] = (keep_ref[...] + got_ref[...].astype(F32)).astype(BF16)


def chunks_kernel(cols, keep_ref, got_ref, own_ref, *rest):
    chunk_refs, sum_ref = rest[:-1], rest[-1]
    col = lax.axis_index("col")
    total = keep_ref[...] + got_ref[...].astype(F32)
    sum_ref[...] = total.reshape(sum_ref.shape)
    own_ref[...] = sum_ref[col]
    for d in range(1, cols):
        chunk_refs[d - 1][...] = sum_ref[col ^ d].astype(BF16)


def row_sum_kernel(cols, area, gx_ref, got_ref, y_ref, own_ref, *part_refs):
    row, core, col, step, pair = place(cols)
    stays = pair == row >> 1

    def total(d):
        rows = slice(d * area, (d + 1) * area)
        return gx_ref[rows, :] + jnp.where(stays, y_ref[rows, :], got_ref[rows, :]).astype(F32)

    own_ref[...] = total(0)
    for d in range(1, cols):
        part_refs[d - 1][...] = total(d).astype(BF16)


def pack_kernel(cols, area, chunk_ref, *refs):
    for d in range(cols - 1):
        refs[cols - 1 + d][:area, :] = refs[d][...]
        refs[cols - 1 + d][area:, :] = chunk_ref[...]


def home_kernel(cols, own_ref, got_ref, out_ref):
    row, core, col, step, pair = place(cols)
    out_ref[...] = jnp.where(step == 0, own_ref[...], got_ref[...])


def join_kernel(cols, area, chunk_ref, *rest):
    got_refs, (half_ref, order_ref) = rest[: cols - 1], rest[cols - 1 :]
    col = lax.axis_index("col")
    order_ref[col] = chunk_ref[...].astype(F32)
    for d in range(1, cols):
        order_ref[col ^ d] = got_refs[d - 1][area:, :].astype(F32)
    half_ref[...] = order_ref[...].reshape(half_ref.shape).astype(BF16)


def pair_grad_kernel(area, own_ref, pair_ref, *rest):
    got_refs, grad_ref = rest[:-1], rest[-1]
    total = own_ref[...]
    for got in got_refs:
        total = total + got[:area, :].astype(F32)
    normed, scaled = layer_norm(pair_ref[...])
    grad_ref[...] = norm_back(total, normed, scaled)


def weights_kernel(width, mine_ref, other_ref, proj_ref, out_ref):
    first = (lax.axis_index("row") & 1) == 0
    mine, other = mine_ref[...].astype(F32), other_ref[...].astype(F32)
    low, high = jnp.where(first, mine, other), jnp.where(first, other, mine)
    for n in range(3):
        proj_ref[:, n * width : (n + 1) * width] = low[n * width : (n + 1) * width]
    for n in range(2):
        proj_ref[:, (3 + n) * width : (4 + n) * width] = high[n * width : (n + 1) * width]
    out_ref[...] = high[2 * width :]


def call(kernel, name, micros, out_shape, args, scratch=(), space=pltpu.VMEM):
    specs = [pl.BlockSpec(memory_space=space) for _ in args]
    total = sum(_bytes(ref) for ref in [*args, *out_shape, *scratch])
    return pl.pallas_call(
        kernel,
        out_shape=tuple(out_shape),
        in_specs=specs,
        out_specs=tuple(pl.BlockSpec(memory_space=pltpu.VMEM) for _ in out_shape),
        scratch_shapes=list(scratch),
        cost_estimate=pl.CostEstimate(
            flops=0, transcendentals=0, bytes_accessed=int(micros * 3_690_000)
        ),
        compiler_params=pltpu.CompilerParams(vmem_limit_bytes=min(60 << 20, total + (8 << 20))),
        name=name,
    )(*args)


def _bytes(ref):
    size = jnp.dtype(ref.dtype).itemsize
    for n in ref.shape:
        size *= n
    return size


def body(rows, cols, pair_input, block_valid, proj_weight, out_weight, cotangent):
    row_len, col_len, width = pair_input.shape
    area = row_len * col_len
    sizes = (row_len, col_len, width)
    planes = rows // 2
    assert planes == cols and col_len == 2 * row_len and cols & (cols - 1) == 0
    assert col_len % SEG == 0 and out_weight.shape == (width, width)

    def permute(value, target):
        pairs = []
        for z in range(planes):
            for core in range(2):
                for col in range(cols):
                    to = target(z, core, col)
                    if to == (z, core, col):
                        to = (z, 1 - core, col)
                    pairs.append(((2 * z + core) * cols + col, (2 * to[0] + to[1]) * cols + to[2]))
        return lax.ppermute(value, ("row", "col"), pairs)

    def in_plane(value, d):
        return permute(value, lambda z, core, col: (z, core, col ^ d))

    def across(value, d):
        return permute(value, lambda z, core, col: (z ^ d, core, col))

    def to_pair(value):
        return permute(value, lambda z, core, col: (z, core, col ^ flip(z, cols)))

    def swap(value):
        return permute(value, lambda z, core, col: (z, 1 - core, col))

    def like(*shape, dtype=F32):
        return jax.ShapeDtypeStruct(shape, dtype)

    pair = pair_input.reshape(area, width)
    cot = cotangent.reshape(area, width)
    tall, half = cols * area, 3 * width
    chunk = half // cols
    (low,) = call(norm_kernel, "norm", 0.3, [like(area, width, dtype=BF16)], [pair])
    blocks = [low] + [in_plane(low, d) for d in range(1, cols)]
    x = jnp.concatenate(blocks, axis=0)
    got_x = permute(x, lambda z, core, col: (flip(col ^ z, cols), core, col))
    cot, x, block_valid = lax.optimization_barrier((cot, x, block_valid))
    got_cot = to_pair(cot)
    (mask,) = call(
        mask_kernel, "mask", 0.1, [like(col_len * cols, width)], [block_valid], space=pltpu.SMEM
    )
    left = call(
        functools.partial(project_kernel, 0, cols, sizes),
        "left",
        0.9,
        [like(cols, row_len, col_len, width)] * 3,
        [mask, x, x, proj_weight],
    )
    out_gate, cot, back, update_low = call(
        functools.partial(gate_kernel, cols, area, width),
        "gate",
        0.3,
        [like(area, width)] * 3 + [like(area, width, dtype=BF16)],
        [x, got_cot, cot, proj_weight, out_weight],
    )
    left, back, got_x = lax.optimization_barrier((left, back, got_x))
    swapped_x = swap(got_x)
    right_shape = [like(tall, width, dtype=BF16)] + [like(cols, row_len, col_len, width)] * 3
    own_x, *own = call(
        functools.partial(project_kernel, 1, cols, sizes),
        "right_own",
        0.4,
        right_shape,
        [mask, got_x, x, proj_weight],
    )
    (mixed_own,) = call(
        functools.partial(mix_own_kernel, cols, sizes),
        "mix_own",
        0.7,
        [like(row_len, 2 * SEG * (-(-row_len // (2 * SEG))), width)],
        [left[0], own[0]],
    )
    swapped_x, mixed_own = lax.optimization_barrier((swapped_x, mixed_own))
    other_x, *right = call(
        functools.partial(project_kernel, 2, cols, sizes),
        "right_other",
        0.4,
        right_shape,
        [mask, swapped_x, got_x, proj_weight],
    )
    mixed_low, wide = call(
        functools.partial(mix_kernel, cols, sizes),
        "mix",
        1.2,
        [like(area, width, dtype=BF16), like(row_len, col_len, SEG, width)],
        [left[0], right[0], mixed_own, back],
        [pltpu.VMEM(mixed_own.shape, F32), pltpu.VMEM((row_len, col_len, width), F32)],
    )
    dl, do, dr = call(
        functools.partial(grads_kernel, cols, sizes),
        "grads",
        2.5,
        [like(tall, 2 * width, dtype=BF16)] * 3,
        [*left, *own, *right, wide],
    )
    send_w, keep_w, pair_out, grad_logit = call(
        functools.partial(weight_sums_kernel, cols, area, width),
        "weight_sums",
        0.6,
        [
            like(half, width, dtype=BF16),
            like(half, width),
            like(area, width),
            like(area, width, dtype=BF16),
        ],
        [x, own_x, other_x, dl, do, dr, mixed_low, out_gate, cot, update_low, out_weight],
        [pltpu.VMEM((2, half, width), F32)],
    )
    got_w = swap(send_w)
    dr, send_w = lax.optimization_barrier((dr, send_w))
    (send_y,) = call(
        functools.partial(back_right_kernel, cols, area, width),
        "back_other",
        0.3,
        [like(tall, width, dtype=BF16)],
        [dr, proj_weight],
    )
    got_y = swap(send_y)
    mine, *chunks = call(
        functools.partial(chunks_kernel, cols),
        "chunks",
        0.1,
        [like(chunk, width)] + [like(chunk, width, dtype=BF16)] * (cols - 1),
        [keep_w, got_w],
        [pltpu.VMEM((cols, chunk, width), F32)],
    )
    do, dl, mine = lax.optimization_barrier((do, dl, mine))
    (keep_y,) = call(
        functools.partial(back_right_kernel, cols, area, width),
        "back_own",
        0.3,
        [like(tall, width)],
        [do, proj_weight],
    )
    (y,) = call(core_sum_kernel, "core_sum", 0.1, [like(tall, width, dtype=BF16)], [keep_y, got_y])
    back_y = permute(y, lambda z, core, col: (col ^ flip(z, cols), core, col))
    (gx,) = call(
        functools.partial(back_left_kernel, cols, area, width),
        "back_left",
        0.3,
        [like(tall, width)],
        [dl, grad_logit, proj_weight],
    )
    for d in range(1, cols):
        mine = mine + in_plane(chunks[d - 1], d).astype(F32)
    low_mine = mine.astype(BF16)
    low_mine, pair_out, gx = lax.optimization_barrier((low_mine, pair_out, gx))
    home = to_pair(pair_out)
    rest, *parts = call(
        functools.partial(row_sum_kernel, cols, area),
        "row_sum",
        4.0,
        [like(area, width)] + [like(area, width, dtype=BF16)] * (cols - 1),
        [gx, back_y, y],
    )
    planes_got = [across(low_mine, d) for d in range(1, cols)]
    *planes_got, rest, home = lax.optimization_barrier((*planes_got, rest, home))
    for got in planes_got:
        mine = mine + got.astype(F32)
    low_mine = mine.astype(BF16)
    sends = call(
        functools.partial(pack_kernel, cols, area),
        "pack",
        0.1,
        [like(area + chunk, width, dtype=BF16)] * (cols - 1),
        [low_mine, *parts],
    )
    gets = [in_plane(sends[d - 1], d) for d in range(1, cols)]
    (pair_out,) = call(
        functools.partial(home_kernel, cols), "home", 0.6, [like(area, width)], [pair_out, home]
    )
    pair_out, *gets = lax.optimization_barrier((pair_out, *gets))
    (half_w,) = call(
        functools.partial(join_kernel, cols, area),
        "join",
        0.1,
        [like(half, width, dtype=BF16)],
        [low_mine, *gets],
        [pltpu.VMEM((cols, chunk, width), F32)],
    )
    other_w = swap(half_w)
    half_w, rest = lax.optimization_barrier((half_w, rest))
    (pair_grad,) = call(
        functools.partial(pair_grad_kernel, area),
        "pair_grad",
        1.0,
        [like(area, width)],
        [rest, pair, *gets],
    )
    proj_grad, out_grad = call(
        functools.partial(weights_kernel, width),
        "weights",
        0.8,
        [like(*proj_weight.shape), like(width, width)],
        [half_w, other_w],
    )
    shape = pair_input.shape
    return pair_out.reshape(shape), pair_grad.reshape(shape), proj_grad, out_grad


def solution(mesh):
    return jax.shard_map(
        functools.partial(body, mesh.shape["row"], mesh.shape["col"]),
        mesh=mesh,
        in_specs=(P("row", "col", None), P(), P(), P(), P("row", "col", None)),
        out_specs=(P("row", "col", None), P("row", "col", None), P(), P()),
        check_vma=False,
    )
```

```python
import functools

import jax
import jax.numpy as jnp
from jax import lax
from jax.experimental import pallas as pl
from jax.experimental.pallas import tpu as pltpu
from jax.sharding import PartitionSpec as P

SEG = 8
F32 = jnp.float32
BF16 = jnp.bfloat16


def sigmoid(values):
    return 0.5 * jnp.tanh(0.5 * values) + 0.5


def layer_norm(values):
    center = values - jnp.mean(values, axis=-1, keepdims=True)
    scaled = lax.rsqrt(jnp.mean(center * center, axis=-1, keepdims=True) + 1e-05)
    return center * scaled, scaled


def norm_back(grad_norm, normed, scaled):
    first_mean = jnp.mean(grad_norm, axis=-1, keepdims=True)
    second = jnp.mean(grad_norm * normed, axis=-1, keepdims=True)
    return scaled * (grad_norm - first_mean - normed * second)


def dot(a, b):
    return jnp.dot(a, b, preferred_element_type=F32)


def dot_nt(a, b):
    return lax.dot_general(a, b, (((1,), (1,)), ((), ())), preferred_element_type=F32)


def dot_tn(a, b):
    return lax.dot_general(a, b, (((0,), (0,)), ((), ())), preferred_element_type=F32)


def flip(z, count):
    out, bit = z & 0, 1
    top = count >> 1
    while bit < count:
        if isinstance(z, int):
            out |= top if z & bit else 0
        else:
            out = out + jnp.where((z & bit) != 0, top, 0)
        bit, top = bit << 1, top >> 1
    return out


def place(cols):
    row, col = lax.axis_index("row"), lax.axis_index("col")
    z, core = row >> 1, row & 1
    step = flip(z, cols)
    return row, core, col, step, col ^ step


def norm_kernel(pair_ref, low_ref):
    low_ref[...] = layer_norm(pair_ref[...])[0].astype(BF16)


def mask_kernel(valid_ref, mask_ref):
    spot = lax.broadcasted_iota(jnp.int32, (SEG, mask_ref.shape[1]), 0)
    for g in range(mask_ref.shape[0] // SEG):
        mask_ref[tile(g), :] = jnp.where(spot < valid_ref[g], 1.0, 0.0)


def project_block(projected, mask_ref, row, block, sizes, index, v_ref, a_ref, b_ref):
    row_len, col_len, width = sizes
    keep_col = mask_ref[pl.ds(pl.multiple_of(block * col_len, SEG), col_len), :]
    for i in range(row_len):
        keep = keep_col * mask_ref[pl.ds(row * row_len + i, 1), :]
        part = projected[i * col_len : (i + 1) * col_len]
        gate = sigmoid(part[:, :width])
        kept = keep * gate
        gated = kept * part[:, width:]
        v_ref[index + (i,)] = gated.astype(BF16).astype(F32)
        a_ref[index + (i,)] = gated * (1.0 - gate)
        b_ref[index + (i,)] = kept


def project_kernel(side, cols, sizes, mask_ref, x_ref, home_ref, w_ref, *refs):
    row_len, col_len, width = sizes
    area = row_len * col_len
    row, core, col, step, pair = place(cols)
    stays = pair == row >> 1
    if side:
        row = 2 * pair + (core if side == 1 else 1 - core)
    base = 2 * width if side else 0

    def one(d):
        rows = rows_of(d, area)
        used = x_ref[rows, :]
        if side:
            used = jnp.where(stays, home_ref[rows, :], used)
            refs[0][rows, :] = used
        projected = dot(used, w_ref[:, base : base + 2 * width])
        project_block(projected, mask_ref, row, col ^ d, sizes, (d,), *refs[-3:])

    by_fours(cols, one)


def tile(g):
    return slice(g * SEG, (g + 1) * SEG)


def rows_of(d, area):
    if isinstance(d, int):
        return pl.ds(d * area, area)
    return pl.ds(pl.multiple_of(d * area, area), area)


def by_fours(count, one):
    def four(q, carry):
        for n in range(4):
            one(4 * q + n)
        return carry

    if count == 4:
        four(0, 0)
    else:
        lax.fori_loop(0, count // 4, four, 0)


def gate_kernel(cols, area, width, x_ref, cot_ref, own_cot_ref, w_ref, wout_ref, gate_ref, cot_out_ref, grad_ref, low_ref):
    row, core, col, step, pair = place(cols)
    out_gate = sigmoid(dot(x_ref[rows_of(step, area), :], w_ref[:, 4 * width :]))
    gated = jnp.where(step == 0, own_cot_ref[...], cot_ref[...]) * out_gate
    low = gated.astype(BF16)
    gate_ref[...] = out_gate
    cot_out_ref[...] = gated * (1.0 - out_gate)
    low_ref[...] = low
    grad_ref[...] = dot_nt(low, wout_ref[...])


def fold(parts):
    spot = lax.broadcasted_iota(jnp.int32, parts[0].shape, 0)
    shift = 1
    while len(parts) > 1:
        first = (spot & shift) == 0
        parts = [
            jnp.where(first, a, b) + pltpu.roll(jnp.where(first, b, a), shift, 0)
            for a, b in zip(parts[::2], parts[1::2])
        ]
        shift *= 2
    return parts[0]


def block_of(row_len):
    return next(n for n in (6, 4, 2) if row_len % n == 0)


def mix_half(cols, sizes, lv_ref, rv_ref, mixed_ref):
    row_len, col_len, width = sizes
    groups = col_len // SEG
    many = block_of(row_len)
    zero = jnp.zeros((SEG, width), F32)

    def rows(block, carry):
        start = block * many
        for jt in range(row_len // 4):

            def over(q, acc):
                for d in range(4):
                    for g in range(groups):
                        left = [lv_ref[4 * q + d, start + a, tile(g), :] for a in range(many)]
                        right = [rv_ref[4 * q + d, 4 * jt + n, tile(g), :] for n in range(4)]
                        acc = tuple(
                            acc[4 * a + n] + left[a] * right[n] for a in range(many) for n in range(4)
                        )
                return acc

            acc = (zero,) * (4 * many)
            acc = over(0, acc) if cols == 4 else lax.fori_loop(0, cols // 4, over, acc)
            for a in range(0, many, 2):
                sums = fold(list(acc[4 * a : 4 * a + 8]))
                mixed_ref[start + a, 4 * jt : 4 * jt + 4, :] = sums[:4]
                mixed_ref[start + a + 1, 4 * jt : 4 * jt + 4, :] = sums[4:]
        return carry

    lax.fori_loop(0, row_len // many, rows, 0)


def mix_own_kernel(cols, sizes, lv_ref, rv_ref, mixed_ref):
    mix_half(cols, sizes, lv_ref, rv_ref, mixed_ref)


def mix_kernel(
    cols, sizes, lv_ref, rv_ref, own_ref, back_ref, low_ref, wide_ref, other_ref, grad_ref
):
    row_len, col_len, width = sizes
    area = row_len * col_len
    mix_half(cols, sizes, lv_ref, rv_ref, other_ref)
    first = (lax.axis_index("row") & 1) == 0
    for i in range(row_len):
        own, other = own_ref[i], other_ref[i]
        low, high = jnp.where(first, own, other), jnp.where(first, other, own)
        grad_ref[i, :row_len, :] = low[:row_len]
        grad_ref[i, row_len:, :] = high[:row_len]
    mixed_norm, mixed_scale = layer_norm(grad_ref[...].reshape(area, width))
    low_ref[...] = mixed_norm.astype(BF16)
    grad_mixed = norm_back(back_ref[...], mixed_norm, mixed_scale)
    grad_ref[...] = grad_mixed.astype(BF16).astype(F32).reshape(row_len, col_len, width)

    def widen(i, carry):
        for j in range(col_len):
            wide_ref[i, j] = jnp.broadcast_to(grad_ref[i, j : j + 1, :], (SEG, width))
        return carry

    lax.fori_loop(0, row_len, widen, 0)


def gradient(load, count, many, first, sizes, a_ref, b_ref, d, d_ref):
    row_len, col_len, width = sizes
    groups = col_len // SEG
    acc = [[jnp.zeros((SEG, width), F32)] * groups for _ in range(many)]
    for n in range(count):
        value, weights = load(n)
        for a in range(many):
            for g in range(groups):
                acc[a][g] = acc[a][g] + value[g] * weights[a]
    full = [jnp.concatenate(acc[a], axis=0) for a in range(many)]
    gates = [full[a] * a_ref[d, first + a] for a in range(many)]
    values = [full[a] * b_ref[d, first + a] for a in range(many)]
    start = pl.multiple_of((d * row_len + first) * col_len, many * col_len)
    rows = pl.ds(start, many * col_len)
    d_ref[rows, :width] = jnp.concatenate(gates, axis=0).astype(BF16)
    d_ref[rows, width:] = jnp.concatenate(values, axis=0).astype(BF16)


def grads_kernel(
    cols,
    sizes,
    lv_ref,
    la_ref,
    lb_ref,
    ov_ref,
    oa_ref,
    ob_ref,
    rv_ref,
    ra_ref,
    rb_ref,
    wide_ref,
    dl_ref,
    do_ref,
    dr_ref,
):
    row_len, col_len, width = sizes
    groups = col_len // SEG
    many = block_of(row_len)
    core = lax.axis_index("row") & 1

    def blocks(one):
        def at(n, carry):
            one(n // cols * many, n % cols)
            return carry

        lax.fori_loop(0, row_len // many * cols, at, 0)

    def right_back(base, a_ref, b_ref, d_ref):
        def one(first, d):
            def load(i):
                return (
                    [lv_ref[d, i, tile(g), :] for g in range(groups)],
                    [wide_ref[i, base + first + a] for a in range(many)],
                )

            gradient(load, row_len, many, first, sizes, a_ref, b_ref, d, d_ref)

        blocks(one)

    right_back(core * row_len, oa_ref, ob_ref, do_ref)
    right_back((1 - core) * row_len, ra_ref, rb_ref, dr_ref)

    def left_back(first, d):
        def load(n):
            ref = ov_ref if n < row_len else rv_ref
            j = (core if n < row_len else 1 - core) * row_len + n % row_len
            return (
                [ref[d, n % row_len, tile(g), :] for g in range(groups)],
                [wide_ref[first + a, j] for a in range(many)],
            )

        gradient(load, col_len, many, first, sizes, la_ref, lb_ref, d, dl_ref)

    blocks(left_back)


def weight_sums_kernel(
    cols,
    area,
    width,
    x_ref,
    own_x_ref,
    other_x_ref,
    dl_ref,
    do_ref,
    dr_ref,
    low_ref,
    gate_ref,
    cot_ref,
    update_low_ref,
    wout_ref,
    send_ref,
    keep_ref,
    out_ref,
    logit_ref,
    sum_ref,
):
    row, core, col, step, pair = place(cols)
    update = dot(low_ref[...], wout_ref[...])
    out_ref[...] = gate_ref[...] * update
    grad_logit = (cot_ref[...] * update).astype(BF16)
    logit_ref[...] = grad_logit
    left_w = dot_tn(x_ref[...], dl_ref[...])
    right_w = dot_tn(own_x_ref[...], do_ref[...]) + dot_tn(other_x_ref[...], dr_ref[...])
    sum_ref[0, :width, :] = left_w[:, :width]
    sum_ref[0, width : 2 * width, :] = left_w[:, width:]
    sum_ref[0, 2 * width :, :] = right_w[:, :width]
    sum_ref[1, :width, :] = right_w[:, width:]
    sum_ref[1, width : 2 * width, :] = dot_tn(x_ref[rows_of(step, area), :], grad_logit)
    sum_ref[1, 2 * width :, :] = dot_tn(low_ref[...], update_low_ref[...])
    send_ref[...] = sum_ref[1 - core].astype(BF16)
    keep_ref[...] = sum_ref[core]


def back_right_kernel(cols, area, width, dr_ref, w_ref, part_ref):
    def back(d):
        rows = rows_of(d, area)
        part = dot_nt(dr_ref[rows, :], w_ref[:, 2 * width : 4 * width])
        part_ref[rows, :] = part.astype(part_ref.dtype)

    by_fours(cols, back)


def back_left_kernel(cols, area, width, dl_ref, logit_ref, w_ref, gx_ref):
    row, core, col, step, pair = place(cols)

    def back(d):
        rows = rows_of(d, area)
        gx_ref[rows, :] = dot_nt(dl_ref[rows, :], w_ref[:, : 2 * width])

    by_fours(cols, back)
    gx_ref[rows_of(step, area), :] += dot_nt(logit_ref[...], w_ref[:, 4 * width :])


def core_sum_kernel(keep_ref, got_ref, y_ref):
    y_ref[...] = (keep_ref[...] + got_ref[...].astype(F32)).astype(BF16)


def chunks_kernel(cols, keep_ref, got_ref, own_ref, *rest):
    chunk_refs, sum_ref = rest[:-1], rest[-1]
    col = lax.axis_index("col")
    total = keep_ref[...] + got_ref[...].astype(F32)
    sum_ref[...] = total.reshape(sum_ref.shape)
    own_ref[...] = sum_ref[col]
    for d in range(1, cols):
        chunk_refs[d - 1][...] = sum_ref[col ^ d].astype(BF16)


def row_sum_kernel(cols, area, gx_ref, got_ref, y_ref, own_ref, *part_refs):
    row, core, col, step, pair = place(cols)
    stays = pair == row >> 1

    def total(d):
        rows = slice(d * area, (d + 1) * area)
        return gx_ref[rows, :] + jnp.where(stays, y_ref[rows, :], got_ref[rows, :]).astype(F32)

    own_ref[...] = total(0)
    for d in range(1, cols):
        part_refs[d - 1][...] = total(d).astype(BF16)


def pack_kernel(cols, area, chunk_ref, *refs):
    for d in range(cols - 1):
        refs[cols - 1 + d][:area, :] = refs[d][...]
        refs[cols - 1 + d][area:, :] = chunk_ref[...]


def home_kernel(cols, own_ref, got_ref, out_ref):
    row, core, col, step, pair = place(cols)
    out_ref[...] = jnp.where(step == 0, own_ref[...], got_ref[...])


def join_kernel(cols, area, chunk_ref, *rest):
    got_refs, (half_ref, order_ref) = rest[: cols - 1], rest[cols - 1 :]
    col = lax.axis_index("col")
    order_ref[col] = chunk_ref[...].astype(F32)
    for d in range(1, cols):
        order_ref[col ^ d] = got_refs[d - 1][area:, :].astype(F32)
    half_ref[...] = order_ref[...].reshape(half_ref.shape).astype(BF16)


def pair_grad_kernel(area, own_ref, pair_ref, *rest):
    got_refs, grad_ref = rest[:-1], rest[-1]
    total = own_ref[...]
    for got in got_refs:
        total = total + got[:area, :].astype(F32)
    normed, scaled = layer_norm(pair_ref[...])
    grad_ref[...] = norm_back(total, normed, scaled)


def weights_kernel(width, mine_ref, other_ref, proj_ref, out_ref):
    first = (lax.axis_index("row") & 1) == 0
    mine, other = mine_ref[...].astype(F32), other_ref[...].astype(F32)
    low, high = jnp.where(first, mine, other), jnp.where(first, other, mine)
    for n in range(3):
        proj_ref[:, n * width : (n + 1) * width] = low[n * width : (n + 1) * width]
    for n in range(2):
        proj_ref[:, (3 + n) * width : (4 + n) * width] = high[n * width : (n + 1) * width]
    out_ref[...] = high[2 * width :]


def call(kernel, name, micros, out_shape, args, scratch=(), space=pltpu.VMEM):
    specs = [pl.BlockSpec(memory_space=space) for _ in args]
    total = sum(_bytes(ref) for ref in [*args, *out_shape, *scratch])
    return pl.pallas_call(
        kernel,
        out_shape=tuple(out_shape),
        in_specs=specs,
        out_specs=tuple(pl.BlockSpec(memory_space=pltpu.VMEM) for _ in out_shape),
        scratch_shapes=list(scratch),
        cost_estimate=pl.CostEstimate(
            flops=0, transcendentals=0, bytes_accessed=int(micros * 3_690_000)
        ),
        compiler_params=pltpu.CompilerParams(vmem_limit_bytes=min(60 << 20, total + (8 << 20))),
        name=name,
    )(*args)


def _bytes(ref):
    size = jnp.dtype(ref.dtype).itemsize
    for n in ref.shape:
        size *= n
    return size


def body(rows, cols, pair_input, block_valid, proj_weight, out_weight, cotangent):
    row_len, col_len, width = pair_input.shape
    area = row_len * col_len
    sizes = (row_len, col_len, width)
    planes = rows // 2
    assert planes == cols and col_len == 2 * row_len and cols & (cols - 1) == 0
    assert col_len % SEG == 0 and out_weight.shape == (width, width)

    def permute(value, target):
        pairs = []
        for z in range(planes):
            for core in range(2):
                for col in range(cols):
                    to = target(z, core, col)
                    if to == (z, core, col):
                        to = (z, 1 - core, col)
                    pairs.append(((2 * z + core) * cols + col, (2 * to[0] + to[1]) * cols + to[2]))
        return lax.ppermute(value, ("row", "col"), pairs)

    def in_plane(value, d):
        return permute(value, lambda z, core, col: (z, core, col ^ d))

    def across(value, d):
        return permute(value, lambda z, core, col: (z ^ d, core, col))

    def to_pair(value):
        return permute(value, lambda z, core, col: (z, core, col ^ flip(z, cols)))

    def swap(value):
        return permute(value, lambda z, core, col: (z, 1 - core, col))

    def like(*shape, dtype=F32):
        return jax.ShapeDtypeStruct(shape, dtype)

    pair = pair_input.reshape(area, width)
    cot = cotangent.reshape(area, width)
    tall, half = cols * area, 3 * width
    chunk = half // cols
    (low,) = call(norm_kernel, "norm", 0.3, [like(area, width, dtype=BF16)], [pair])
    blocks = [low] + [in_plane(low, d) for d in range(1, cols)]
    x = jnp.concatenate(blocks, axis=0)
    got_x = permute(x, lambda z, core, col: (flip(col ^ z, cols), core, col))
    cot, x, block_valid = lax.optimization_barrier((cot, x, block_valid))
    got_cot = to_pair(cot)
    (mask,) = call(
        mask_kernel, "mask", 0.1, [like(col_len * cols, width)], [block_valid], space=pltpu.SMEM
    )
    left = call(
        functools.partial(project_kernel, 0, cols, sizes),
        "left",
        0.9,
        [like(cols, row_len, col_len, width)] * 3,
        [mask, x, x, proj_weight],
    )
    out_gate, cot, back, update_low = call(
        functools.partial(gate_kernel, cols, area, width),
        "gate",
        0.3,
        [like(area, width)] * 3 + [like(area, width, dtype=BF16)],
        [x, got_cot, cot, proj_weight, out_weight],
    )
    left, back, got_x = lax.optimization_barrier((left, back, got_x))
    swapped_x = swap(got_x)
    right_shape = [like(tall, width, dtype=BF16)] + [like(cols, row_len, col_len, width)] * 3
    own_x, *own = call(
        functools.partial(project_kernel, 1, cols, sizes),
        "right_own",
        0.4,
        right_shape,
        [mask, got_x, x, proj_weight],
    )
    (mixed_own,) = call(
        functools.partial(mix_own_kernel, cols, sizes),
        "mix_own",
        0.7,
        [like(row_len, 2 * SEG * (-(-row_len // (2 * SEG))), width)],
        [left[0], own[0]],
    )
    swapped_x, mixed_own = lax.optimization_barrier((swapped_x, mixed_own))
    other_x, *right = call(
        functools.partial(project_kernel, 2, cols, sizes),
        "right_other",
        0.4,
        right_shape,
        [mask, swapped_x, got_x, proj_weight],
    )
    mixed_low, wide = call(
        functools.partial(mix_kernel, cols, sizes),
        "mix",
        1.2,
        [like(area, width, dtype=BF16), like(row_len, col_len, SEG, width)],
        [left[0], right[0], mixed_own, back],
        [pltpu.VMEM(mixed_own.shape, F32), pltpu.VMEM((row_len, col_len, width), F32)],
    )
    dl, do, dr = call(
        functools.partial(grads_kernel, cols, sizes),
        "grads",
        2.5,
        [like(tall, 2 * width, dtype=BF16)] * 3,
        [*left, *own, *right, wide],
    )
    send_w, keep_w, pair_out, grad_logit = call(
        functools.partial(weight_sums_kernel, cols, area, width),
        "weight_sums",
        0.6,
        [
            like(half, width, dtype=BF16),
            like(half, width),
            like(area, width),
            like(area, width, dtype=BF16),
        ],
        [x, own_x, other_x, dl, do, dr, mixed_low, out_gate, cot, update_low, out_weight],
        [pltpu.VMEM((2, half, width), F32)],
    )
    got_w = swap(send_w)
    (send_y,) = call(
        functools.partial(back_right_kernel, cols, area, width),
        "back_other",
        0.3,
        [like(tall, width, dtype=BF16)],
        [dr, proj_weight],
    )
    got_y = swap(send_y)
    mine, *chunks = call(
        functools.partial(chunks_kernel, cols),
        "chunks",
        0.1,
        [like(chunk, width)] + [like(chunk, width, dtype=BF16)] * (cols - 1),
        [keep_w, got_w],
        [pltpu.VMEM((cols, chunk, width), F32)],
    )
    dl, mine = lax.optimization_barrier((dl, mine))
    (keep_y,) = call(
        functools.partial(back_right_kernel, cols, area, width),
        "back_own",
        0.3,
        [like(tall, width)],
        [do, proj_weight],
    )
    (y,) = call(core_sum_kernel, "core_sum", 0.1, [like(tall, width, dtype=BF16)], [keep_y, got_y])
    back_y = permute(y, lambda z, core, col: (col ^ flip(z, cols), core, col))
    (gx,) = call(
        functools.partial(back_left_kernel, cols, area, width),
        "back_left",
        0.3,
        [like(tall, width)],
        [dl, grad_logit, proj_weight],
    )
    for d in range(1, cols):
        mine = mine + in_plane(chunks[d - 1], d).astype(F32)
    low_mine = mine.astype(BF16)
    home = to_pair(pair_out)
    back_y, home = lax.optimization_barrier((back_y, home))
    rest, *parts = call(
        functools.partial(row_sum_kernel, cols, area),
        "row_sum",
        4.0,
        [like(area, width)] + [like(area, width, dtype=BF16)] * (cols - 1),
        [gx, back_y, y],
    )
    planes_got = [across(low_mine, d) for d in range(1, cols)]
    *planes_got, rest = lax.optimization_barrier((*planes_got, rest))
    for got in planes_got:
        mine = mine + got.astype(F32)
    low_mine = mine.astype(BF16)
    sends = call(
        functools.partial(pack_kernel, cols, area),
        "pack",
        0.1,
        [like(area + chunk, width, dtype=BF16)] * (cols - 1),
        [low_mine, *parts],
    )
    gets = [in_plane(sends[d - 1], d) for d in range(1, cols)]
    (pair_out,) = call(
        functools.partial(home_kernel, cols), "home", 0.6, [like(area, width)], [pair_out, home]
    )
    pair_out, *gets = lax.optimization_barrier((pair_out, *gets))
    (half_w,) = call(
        functools.partial(join_kernel, cols, area),
        "join",
        0.1,
        [like(half, width, dtype=BF16)],
        [low_mine, *gets],
        [pltpu.VMEM((cols, chunk, width), F32)],
    )
    other_w = swap(half_w)
    half_w, rest = lax.optimization_barrier((half_w, rest))
    (pair_grad,) = call(
        functools.partial(pair_grad_kernel, area),
        "pair_grad",
        1.0,
        [like(area, width)],
        [rest, pair, *gets],
    )
    proj_grad, out_grad = call(
        functools.partial(weights_kernel, width),
        "weights",
        0.8,
        [like(*proj_weight.shape), like(width, width)],
        [half_w, other_w],
    )
    shape = pair_input.shape
    return pair_out.reshape(shape), pair_grad.reshape(shape), proj_grad, out_grad


def solution(mesh):
    return jax.shard_map(
        functools.partial(body, mesh.shape["row"], mesh.shape["col"]),
        mesh=mesh,
        in_specs=(P("row", "col", None), P(), P(), P(), P("row", "col", None)),
        out_specs=(P("row", "col", None), P("row", "col", None), P(), P()),
        check_vma=False,
    )
```

```python
import functools

import jax
import jax.numpy as jnp
from jax import lax
from jax.experimental import pallas as pl
from jax.experimental.pallas import tpu as pltpu
from jax.sharding import PartitionSpec as P

SEG = 8
F32 = jnp.float32
BF16 = jnp.bfloat16


def sigmoid(values):
    return 0.5 * jnp.tanh(0.5 * values) + 0.5


def layer_norm(values):
    center = values - jnp.mean(values, axis=-1, keepdims=True)
    scaled = lax.rsqrt(jnp.mean(center * center, axis=-1, keepdims=True) + 1e-05)
    return center * scaled, scaled


def norm_back(grad_norm, normed, scaled):
    first_mean = jnp.mean(grad_norm, axis=-1, keepdims=True)
    second = jnp.mean(grad_norm * normed, axis=-1, keepdims=True)
    return scaled * (grad_norm - first_mean - normed * second)


def dot(a, b):
    return jnp.dot(a, b, preferred_element_type=F32)


def dot_nt(a, b):
    return lax.dot_general(a, b, (((1,), (1,)), ((), ())), preferred_element_type=F32)


def dot_tn(a, b):
    return lax.dot_general(a, b, (((0,), (0,)), ((), ())), preferred_element_type=F32)


def flip(z, count):
    out, bit = z & 0, 1
    top = count >> 1
    while bit < count:
        if isinstance(z, int):
            out |= top if z & bit else 0
        else:
            out = out + jnp.where((z & bit) != 0, top, 0)
        bit, top = bit << 1, top >> 1
    return out


def place(cols):
    row, col = lax.axis_index("row"), lax.axis_index("col")
    z, core = row >> 1, row & 1
    step = flip(z, cols)
    return row, core, col, step, col ^ step


def norm_kernel(pair_ref, low_ref):
    low_ref[...] = layer_norm(pair_ref[...])[0].astype(BF16)


def mask_kernel(valid_ref, mask_ref):
    spot = lax.broadcasted_iota(jnp.int32, (SEG, mask_ref.shape[1]), 0)
    for g in range(mask_ref.shape[0] // SEG):
        mask_ref[tile(g), :] = jnp.where(spot < valid_ref[g], 1.0, 0.0)


def project_block(projected, mask_ref, row, block, sizes, index, v_ref, a_ref, b_ref):
    row_len, col_len, width = sizes
    keep_col = mask_ref[pl.ds(pl.multiple_of(block * col_len, SEG), col_len), :]
    for i in range(row_len):
        keep = keep_col * mask_ref[pl.ds(row * row_len + i, 1), :]
        part = projected[i * col_len : (i + 1) * col_len]
        gate = sigmoid(part[:, :width])
        kept = keep * gate
        gated = kept * part[:, width:]
        v_ref[index + (i,)] = gated.astype(BF16).astype(F32)
        a_ref[index + (i,)] = gated * (1.0 - gate)
        b_ref[index + (i,)] = kept


def project_kernel(side, cols, sizes, mask_ref, x_ref, home_ref, w_ref, *refs):
    row_len, col_len, width = sizes
    area = row_len * col_len
    row, core, col, step, pair = place(cols)
    stays = pair == row >> 1
    if side:
        row = 2 * pair + (core if side == 1 else 1 - core)
    base = 2 * width if side else 0

    def one(d):
        rows = rows_of(d, area)
        used = x_ref[rows, :]
        if side:
            used = jnp.where(stays, home_ref[rows, :], used)
            refs[0][rows, :] = used
        projected = dot(used, w_ref[:, base : base + 2 * width])
        project_block(projected, mask_ref, row, col ^ d, sizes, (d,), *refs[-3:])

    by_fours(cols, one)


def tile(g):
    return slice(g * SEG, (g + 1) * SEG)


def rows_of(d, area):
    if isinstance(d, int):
        return pl.ds(d * area, area)
    return pl.ds(pl.multiple_of(d * area, area), area)


def by_fours(count, one):
    def four(q, carry):
        for n in range(4):
            one(4 * q + n)
        return carry

    if count == 4:
        four(0, 0)
    else:
        lax.fori_loop(0, count // 4, four, 0)


def gate_kernel(cols, area, width, x_ref, cot_ref, own_cot_ref, w_ref, wout_ref, gate_ref, cot_out_ref, grad_ref, low_ref):
    row, core, col, step, pair = place(cols)
    out_gate = sigmoid(dot(x_ref[rows_of(step, area), :], w_ref[:, 4 * width :]))
    gated = jnp.where(step == 0, own_cot_ref[...], cot_ref[...]) * out_gate
    low = gated.astype(BF16)
    gate_ref[...] = out_gate
    cot_out_ref[...] = gated * (1.0 - out_gate)
    low_ref[...] = low
    grad_ref[...] = dot_nt(low, wout_ref[...])


def fold(parts):
    spot = lax.broadcasted_iota(jnp.int32, parts[0].shape, 0)
    shift = 1
    while len(parts) > 1:
        first = (spot & shift) == 0
        parts = [
            jnp.where(first, a, b) + pltpu.roll(jnp.where(first, b, a), shift, 0)
            for a, b in zip(parts[::2], parts[1::2])
        ]
        shift *= 2
    return parts[0]


def block_of(row_len):
    return next(n for n in (4, 2) if row_len % n == 0)


def mix_half(cols, sizes, lv_ref, rv_ref, mixed_ref):
    row_len, col_len, width = sizes
    groups = col_len // SEG
    many = block_of(row_len)
    zero = jnp.zeros((SEG, width), F32)

    for start in range(0, row_len, many):
        for jt in range(row_len // 4):

            def over(q, acc):
                for d in range(4):
                    for g in range(groups):
                        left = [lv_ref[4 * q + d, start + a, tile(g), :] for a in range(many)]
                        right = [rv_ref[4 * q + d, 4 * jt + n, tile(g), :] for n in range(4)]
                        acc = tuple(
                            acc[4 * a + n] + left[a] * right[n] for a in range(many) for n in range(4)
                        )
                return acc

            acc = (zero,) * (4 * many)
            acc = over(0, acc) if cols == 4 else lax.fori_loop(0, cols // 4, over, acc)
            for a in range(0, many, 2):
                sums = fold(list(acc[4 * a : 4 * a + 8]))
                mixed_ref[start + a, 4 * jt : 4 * jt + 4, :] = sums[:4]
                mixed_ref[start + a + 1, 4 * jt : 4 * jt + 4, :] = sums[4:]


def mix_own_kernel(cols, sizes, lv_ref, rv_ref, mixed_ref):
    mix_half(cols, sizes, lv_ref, rv_ref, mixed_ref)


def mix_kernel(
    cols, sizes, lv_ref, rv_ref, own_ref, back_ref, low_ref, wide_ref, other_ref, grad_ref
):
    row_len, col_len, width = sizes
    area = row_len * col_len
    mix_half(cols, sizes, lv_ref, rv_ref, other_ref)
    first = (lax.axis_index("row") & 1) == 0
    for i in range(row_len):
        own, other = own_ref[i], other_ref[i]
        low, high = jnp.where(first, own, other), jnp.where(first, other, own)
        grad_ref[i, :row_len, :] = low[:row_len]
        grad_ref[i, row_len:, :] = high[:row_len]
    mixed_norm, mixed_scale = layer_norm(grad_ref[...].reshape(area, width))
    low_ref[...] = mixed_norm.astype(BF16)
    grad_mixed = norm_back(back_ref[...], mixed_norm, mixed_scale)
    grad_ref[...] = grad_mixed.astype(BF16).astype(F32).reshape(row_len, col_len, width)

    for i in range(row_len):
        for j in range(col_len):
            wide_ref[i, j] = jnp.broadcast_to(grad_ref[i, j : j + 1, :], (SEG, width))


def gradient(load, count, many, first, sizes, a_ref, b_ref, d, d_ref):
    row_len, col_len, width = sizes
    groups = col_len // SEG
    acc = [[jnp.zeros((SEG, width), F32)] * groups for _ in range(many)]
    for n in range(count):
        value, weights = load(n)
        for a in range(many):
            for g in range(groups):
                acc[a][g] = acc[a][g] + value[g] * weights[a]
    full = [jnp.concatenate(acc[a], axis=0) for a in range(many)]
    gates = [full[a] * a_ref[d, first + a] for a in range(many)]
    values = [full[a] * b_ref[d, first + a] for a in range(many)]
    start = (d * row_len + first) * col_len
    rows = pl.ds(start if isinstance(start, int) else pl.multiple_of(start, many * col_len), many * col_len)
    d_ref[rows, :width] = jnp.concatenate(gates, axis=0).astype(BF16)
    d_ref[rows, width:] = jnp.concatenate(values, axis=0).astype(BF16)


def grads_kernel(
    cols,
    sizes,
    lv_ref,
    la_ref,
    lb_ref,
    ov_ref,
    oa_ref,
    ob_ref,
    rv_ref,
    ra_ref,
    rb_ref,
    wide_ref,
    dl_ref,
    do_ref,
    dr_ref,
):
    row_len, col_len, width = sizes
    groups = col_len // SEG
    many = block_of(row_len)
    core = lax.axis_index("row") & 1

    def blocks(one):
        for first in range(0, row_len, many):
            by_fours(cols, functools.partial(one, first))

    def right_back(base, a_ref, b_ref, d_ref):
        def one(first, d):
            def load(i):
                return (
                    [lv_ref[d, i, tile(g), :] for g in range(groups)],
                    [wide_ref[i, base + first + a] for a in range(many)],
                )

            gradient(load, row_len, many, first, sizes, a_ref, b_ref, d, d_ref)

        blocks(one)

    right_back(core * row_len, oa_ref, ob_ref, do_ref)
    right_back((1 - core) * row_len, ra_ref, rb_ref, dr_ref)

    def left_back(first, d):
        def load(n):
            ref = ov_ref if n < row_len else rv_ref
            j = (core if n < row_len else 1 - core) * row_len + n % row_len
            return (
                [ref[d, n % row_len, tile(g), :] for g in range(groups)],
                [wide_ref[first + a, j] for a in range(many)],
            )

        gradient(load, col_len, many, first, sizes, la_ref, lb_ref, d, dl_ref)

    blocks(left_back)


def weight_sums_kernel(
    cols,
    area,
    width,
    x_ref,
    own_x_ref,
    other_x_ref,
    dl_ref,
    do_ref,
    dr_ref,
    low_ref,
    gate_ref,
    cot_ref,
    update_low_ref,
    wout_ref,
    send_ref,
    keep_ref,
    out_ref,
    logit_ref,
    sum_ref,
):
    row, core, col, step, pair = place(cols)
    update = dot(low_ref[...], wout_ref[...])
    out_ref[...] = gate_ref[...] * update
    grad_logit = (cot_ref[...] * update).astype(BF16)
    logit_ref[...] = grad_logit
    left_w = dot_tn(x_ref[...], dl_ref[...])
    right_w = dot_tn(own_x_ref[...], do_ref[...]) + dot_tn(other_x_ref[...], dr_ref[...])
    sum_ref[0, :width, :] = left_w[:, :width]
    sum_ref[0, width : 2 * width, :] = left_w[:, width:]
    sum_ref[0, 2 * width :, :] = right_w[:, :width]
    sum_ref[1, :width, :] = right_w[:, width:]
    sum_ref[1, width : 2 * width, :] = dot_tn(x_ref[rows_of(step, area), :], grad_logit)
    sum_ref[1, 2 * width :, :] = dot_tn(low_ref[...], update_low_ref[...])
    send_ref[...] = sum_ref[1 - core].astype(BF16)
    keep_ref[...] = sum_ref[core]


def back_right_kernel(cols, area, width, dr_ref, w_ref, part_ref):
    def back(d):
        rows = rows_of(d, area)
        part = dot_nt(dr_ref[rows, :], w_ref[:, 2 * width : 4 * width])
        part_ref[rows, :] = part.astype(part_ref.dtype)

    by_fours(cols, back)


def back_left_kernel(cols, area, width, dl_ref, logit_ref, w_ref, gx_ref):
    row, core, col, step, pair = place(cols)

    def back(d):
        rows = rows_of(d, area)
        gx_ref[rows, :] = dot_nt(dl_ref[rows, :], w_ref[:, : 2 * width])

    by_fours(cols, back)
    gx_ref[rows_of(step, area), :] += dot_nt(logit_ref[...], w_ref[:, 4 * width :])


def core_sum_kernel(keep_ref, got_ref, y_ref):
    y_ref[...] = (keep_ref[...] + got_ref[...].astype(F32)).astype(BF16)


def chunks_kernel(cols, keep_ref, got_ref, own_ref, *rest):
    chunk_refs, sum_ref = rest[:-1], rest[-1]
    col = lax.axis_index("col")
    total = keep_ref[...] + got_ref[...].astype(F32)
    sum_ref[...] = total.reshape(sum_ref.shape)
    own_ref[...] = sum_ref[col]
    for d in range(1, cols):
        chunk_refs[d - 1][...] = sum_ref[col ^ d].astype(BF16)


def row_sum_kernel(cols, area, gx_ref, got_ref, y_ref, own_ref, *part_refs):
    row, core, col, step, pair = place(cols)
    stays = pair == row >> 1

    def total(d):
        rows = slice(d * area, (d + 1) * area)
        return gx_ref[rows, :] + jnp.where(stays, y_ref[rows, :], got_ref[rows, :]).astype(F32)

    own_ref[...] = total(0)
    for d in range(1, cols):
        part_refs[d - 1][...] = total(d).astype(BF16)


def pack_kernel(cols, area, chunk_ref, *refs):
    for d in range(cols - 1):
        refs[cols - 1 + d][:area, :] = refs[d][...]
        refs[cols - 1 + d][area:, :] = chunk_ref[...]


def home_kernel(cols, own_ref, got_ref, pair_ref, out_ref, normed_ref, scaled_ref):
    row, core, col, step, pair = place(cols)
    out_ref[...] = jnp.where(step == 0, own_ref[...], got_ref[...])
    normed, scaled = layer_norm(pair_ref[...])
    normed_ref[...] = normed
    scaled_ref[...] = jnp.broadcast_to(scaled, normed.shape)


def join_kernel(cols, area, chunk_ref, *rest):
    got_refs, (half_ref, order_ref) = rest[: cols - 1], rest[cols - 1 :]
    col = lax.axis_index("col")
    order_ref[col] = chunk_ref[...].astype(F32)
    for d in range(1, cols):
        order_ref[col ^ d] = got_refs[d - 1][area:, :].astype(F32)
    half_ref[...] = order_ref[...].reshape(half_ref.shape).astype(BF16)


def pair_grad_kernel(area, own_ref, normed_ref, scaled_ref, *rest):
    got_refs, grad_ref = rest[:-1], rest[-1]
    total = own_ref[...]
    for got in got_refs:
        total = total + got[:area, :].astype(F32)
    grad_ref[...] = norm_back(total, normed_ref[...], scaled_ref[...])


def weights_kernel(width, mine_ref, other_ref, proj_ref, out_ref):
    first = (lax.axis_index("row") & 1) == 0
    mine, other = mine_ref[...].astype(F32), other_ref[...].astype(F32)
    low, high = jnp.where(first, mine, other), jnp.where(first, other, mine)
    for n in range(3):
        proj_ref[:, n * width : (n + 1) * width] = low[n * width : (n + 1) * width]
    for n in range(2):
        proj_ref[:, (3 + n) * width : (4 + n) * width] = high[n * width : (n + 1) * width]
    out_ref[...] = high[2 * width :]


def call(kernel, name, micros, out_shape, args, scratch=(), space=pltpu.VMEM):
    specs = [pl.BlockSpec(memory_space=space) for _ in args]
    total = sum(_bytes(ref) for ref in [*args, *out_shape, *scratch])
    return pl.pallas_call(
        kernel,
        out_shape=tuple(out_shape),
        in_specs=specs,
        out_specs=tuple(pl.BlockSpec(memory_space=pltpu.VMEM) for _ in out_shape),
        scratch_shapes=list(scratch),
        cost_estimate=pl.CostEstimate(
            flops=0, transcendentals=0, bytes_accessed=int(micros * 3_690_000)
        ),
        compiler_params=pltpu.CompilerParams(vmem_limit_bytes=min(60 << 20, total + (8 << 20))),
        name=name,
    )(*args)


def _bytes(ref):
    size = jnp.dtype(ref.dtype).itemsize
    for n in ref.shape:
        size *= n
    return size


def body(rows, cols, pair_input, block_valid, proj_weight, out_weight, cotangent):
    row_len, col_len, width = pair_input.shape
    area = row_len * col_len
    sizes = (row_len, col_len, width)
    planes = rows // 2
    assert planes == cols and col_len == 2 * row_len and cols & (cols - 1) == 0
    assert col_len % SEG == 0 and out_weight.shape == (width, width)

    def permute(value, target):
        pairs = []
        for z in range(planes):
            for core in range(2):
                for col in range(cols):
                    to = target(z, core, col)
                    if to == (z, core, col):
                        to = (z, 1 - core, col)
                    pairs.append(((2 * z + core) * cols + col, (2 * to[0] + to[1]) * cols + to[2]))
        return lax.ppermute(value, ("row", "col"), pairs)

    def in_plane(value, d):
        return permute(value, lambda z, core, col: (z, core, col ^ d))

    def across(value, d):
        return permute(value, lambda z, core, col: (z ^ d, core, col))

    def to_pair(value):
        return permute(value, lambda z, core, col: (z, core, col ^ flip(z, cols)))

    def swap(value):
        return permute(value, lambda z, core, col: (z, 1 - core, col))

    def like(*shape, dtype=F32):
        return jax.ShapeDtypeStruct(shape, dtype)

    pair = pair_input.reshape(area, width)
    cot = cotangent.reshape(area, width)
    tall, half = cols * area, 3 * width
    chunk = half // cols
    (low,) = call(norm_kernel, "norm", 0.3, [like(area, width, dtype=BF16)], [pair])
    blocks = [low] + [in_plane(low, d) for d in range(1, cols)]
    x = jnp.concatenate(blocks, axis=0)
    got_x = permute(x, lambda z, core, col: (flip(col ^ z, cols), core, col))
    cot, x, block_valid = lax.optimization_barrier((cot, x, block_valid))
    got_cot = to_pair(cot)
    (mask,) = call(
        mask_kernel, "mask", 0.1, [like(col_len * cols, width)], [block_valid], space=pltpu.SMEM
    )
    left = call(
        functools.partial(project_kernel, 0, cols, sizes),
        "left",
        0.9,
        [like(cols, row_len, col_len, width)] * 3,
        [mask, x, x, proj_weight],
    )
    out_gate, cot, back, update_low = call(
        functools.partial(gate_kernel, cols, area, width),
        "gate",
        0.3,
        [like(area, width)] * 3 + [like(area, width, dtype=BF16)],
        [x, got_cot, cot, proj_weight, out_weight],
    )
    left, back, got_x = lax.optimization_barrier((left, back, got_x))
    swapped_x = swap(got_x)
    right_shape = [like(tall, width, dtype=BF16)] + [like(cols, row_len, col_len, width)] * 3
    own_x, *own = call(
        functools.partial(project_kernel, 1, cols, sizes),
        "right_own",
        0.4,
        right_shape,
        [mask, got_x, x, proj_weight],
    )
    (mixed_own,) = call(
        functools.partial(mix_own_kernel, cols, sizes),
        "mix_own",
        0.7,
        [like(row_len, 2 * SEG * (-(-row_len // (2 * SEG))), width)],
        [left[0], own[0]],
    )
    swapped_x, mixed_own = lax.optimization_barrier((swapped_x, mixed_own))
    other_x, *right = call(
        functools.partial(project_kernel, 2, cols, sizes),
        "right_other",
        0.4,
        right_shape,
        [mask, swapped_x, got_x, proj_weight],
    )
    mixed_low, wide = call(
        functools.partial(mix_kernel, cols, sizes),
        "mix",
        1.2,
        [like(area, width, dtype=BF16), like(row_len, col_len, SEG, width)],
        [left[0], right[0], mixed_own, back],
        [pltpu.VMEM(mixed_own.shape, F32), pltpu.VMEM((row_len, col_len, width), F32)],
    )
    dl, do, dr = call(
        functools.partial(grads_kernel, cols, sizes),
        "grads",
        2.5,
        [like(tall, 2 * width, dtype=BF16)] * 3,
        [*left, *own, *right, wide],
    )
    send_w, keep_w, pair_out, grad_logit = call(
        functools.partial(weight_sums_kernel, cols, area, width),
        "weight_sums",
        0.6,
        [
            like(half, width, dtype=BF16),
            like(half, width),
            like(area, width),
            like(area, width, dtype=BF16),
        ],
        [x, own_x, other_x, dl, do, dr, mixed_low, out_gate, cot, update_low, out_weight],
        [pltpu.VMEM((2, half, width), F32)],
    )
    got_w = swap(send_w)
    (send_y,) = call(
        functools.partial(back_right_kernel, cols, area, width),
        "back_other",
        0.3,
        [like(tall, width, dtype=BF16)],
        [dr, proj_weight],
    )
    got_y = swap(send_y)
    mine, *chunks = call(
        functools.partial(chunks_kernel, cols),
        "chunks",
        0.1,
        [like(chunk, width)] + [like(chunk, width, dtype=BF16)] * (cols - 1),
        [keep_w, got_w],
        [pltpu.VMEM((cols, chunk, width), F32)],
    )
    dl, mine = lax.optimization_barrier((dl, mine))
    (keep_y,) = call(
        functools.partial(back_right_kernel, cols, area, width),
        "back_own",
        0.3,
        [like(tall, width)],
        [do, proj_weight],
    )
    (y,) = call(core_sum_kernel, "core_sum", 0.1, [like(tall, width, dtype=BF16)], [keep_y, got_y])
    back_y = permute(y, lambda z, core, col: (col ^ flip(z, cols), core, col))
    (gx,) = call(
        functools.partial(back_left_kernel, cols, area, width),
        "back_left",
        0.3,
        [like(tall, width)],
        [dl, grad_logit, proj_weight],
    )
    for d in range(1, cols):
        mine = mine + in_plane(chunks[d - 1], d).astype(F32)
    low_mine = mine.astype(BF16)
    home = to_pair(pair_out)
    back_y, home = lax.optimization_barrier((back_y, home))
    rest, *parts = call(
        functools.partial(row_sum_kernel, cols, area),
        "row_sum",
        4.0,
        [like(area, width)] + [like(area, width, dtype=BF16)] * (cols - 1),
        [gx, back_y, y],
    )
    planes_got = [across(low_mine, d) for d in range(1, cols)]
    *planes_got, rest = lax.optimization_barrier((*planes_got, rest))
    for got in planes_got:
        mine = mine + got.astype(F32)
    low_mine = mine.astype(BF16)
    sends = call(
        functools.partial(pack_kernel, cols, area),
        "pack",
        0.1,
        [like(area + chunk, width, dtype=BF16)] * (cols - 1),
        [low_mine, *parts],
    )
    gets = [in_plane(sends[d - 1], d) for d in range(1, cols)]
    pair_out, normed, scaled = call(
        functools.partial(home_kernel, cols),
        "home",
        0.6,
        [like(area, width)] * 3,
        [pair_out, home, pair],
    )
    pair_out, *gets = lax.optimization_barrier((pair_out, *gets))
    (half_w,) = call(
        functools.partial(join_kernel, cols, area),
        "join",
        0.1,
        [like(half, width, dtype=BF16)],
        [low_mine, *gets],
        [pltpu.VMEM((cols, chunk, width), F32)],
    )
    other_w = swap(half_w)
    half_w, rest = lax.optimization_barrier((half_w, rest))
    (pair_grad,) = call(
        functools.partial(pair_grad_kernel, area),
        "pair_grad",
        1.0,
        [like(area, width)],
        [rest, normed, scaled, *gets],
    )
    proj_grad, out_grad = call(
        functools.partial(weights_kernel, width),
        "weights",
        0.8,
        [like(*proj_weight.shape), like(width, width)],
        [half_w, other_w],
    )
    shape = pair_input.shape
    return pair_out.reshape(shape), pair_grad.reshape(shape), proj_grad, out_grad


def solution(mesh):
    return jax.shard_map(
        functools.partial(body, mesh.shape["row"], mesh.shape["col"]),
        mesh=mesh,
        in_specs=(P("row", "col", None), P(), P(), P(), P("row", "col", None)),
        out_specs=(P("row", "col", None), P("row", "col", None), P(), P()),
        check_vma=False,
    )
```

```python
import functools

import jax
import jax.numpy as jnp
from jax import lax
from jax.experimental import pallas as pl
from jax.experimental.pallas import tpu as pltpu
from jax.sharding import PartitionSpec as P

SEG = 8
F32 = jnp.float32
BF16 = jnp.bfloat16


def sigmoid(values):
    return 0.5 * jnp.tanh(0.5 * values) + 0.5


def layer_norm(values):
    center = values - jnp.mean(values, axis=-1, keepdims=True)
    scaled = lax.rsqrt(jnp.mean(center * center, axis=-1, keepdims=True) + 1e-05)
    return center * scaled, scaled


def norm_back(grad_norm, normed, scaled):
    first_mean = jnp.mean(grad_norm, axis=-1, keepdims=True)
    second = jnp.mean(grad_norm * normed, axis=-1, keepdims=True)
    return scaled * (grad_norm - first_mean - normed * second)


def dot(a, b):
    return jnp.dot(a, b, preferred_element_type=F32)


def dot_nt(a, b):
    return lax.dot_general(a, b, (((1,), (1,)), ((), ())), preferred_element_type=F32)


def dot_tn(a, b):
    return lax.dot_general(a, b, (((0,), (0,)), ((), ())), preferred_element_type=F32)


def flip(z, count):
    out, bit = z & 0, 1
    top = count >> 1
    while bit < count:
        if isinstance(z, int):
            out |= top if z & bit else 0
        else:
            out = out + jnp.where((z & bit) != 0, top, 0)
        bit, top = bit << 1, top >> 1
    return out


def place(cols):
    row, col = lax.axis_index("row"), lax.axis_index("col")
    z, core = row >> 1, row & 1
    step = flip(z, cols)
    return row, core, col, step, col ^ step


def norm_kernel(pair_ref, low_ref):
    low_ref[...] = layer_norm(pair_ref[...])[0].astype(BF16)


def mask_kernel(valid_ref, mask_ref):
    spot = lax.broadcasted_iota(jnp.int32, (SEG, mask_ref.shape[1]), 0)
    for g in range(mask_ref.shape[0] // SEG):
        mask_ref[tile(g), :] = jnp.where(spot < valid_ref[g], 1.0, 0.0)


def project_block(projected, mask_ref, row, block, sizes, index, v_ref, a_ref, b_ref):
    row_len, col_len, width = sizes
    keep_col = mask_ref[pl.ds(pl.multiple_of(block * col_len, SEG), col_len), :]
    for i in range(row_len):
        keep = keep_col * mask_ref[pl.ds(row * row_len + i, 1), :]
        part = projected[i * col_len : (i + 1) * col_len]
        gate = sigmoid(part[:, :width])
        kept = keep * gate
        gated = kept * part[:, width:]
        v_ref[index + (i,)] = gated.astype(BF16).astype(F32)
        a_ref[index + (i,)] = gated * (1.0 - gate)
        b_ref[index + (i,)] = kept


def project_kernel(side, cols, sizes, mask_ref, x_ref, home_ref, w_ref, *refs):
    row_len, col_len, width = sizes
    area = row_len * col_len
    row, core, col, step, pair = place(cols)
    stays = pair == row >> 1
    if side:
        row = 2 * pair + (core if side == 1 else 1 - core)
    base = 2 * width if side else 0

    def one(d):
        rows = rows_of(d, area)
        used = x_ref[rows, :]
        if side:
            used = jnp.where(stays, home_ref[rows, :], used)
            refs[0][rows, :] = used
        projected = dot(used, w_ref[:, base : base + 2 * width])
        project_block(projected, mask_ref, row, col ^ d, sizes, (d,), *refs[-3:])

    by_fours(cols, one)
    if side == 0:
        refs[0][...] = x_ref[...].T


def tile(g):
    return slice(g * SEG, (g + 1) * SEG)


def rows_of(d, area):
    if isinstance(d, int):
        return pl.ds(d * area, area)
    return pl.ds(pl.multiple_of(d * area, area), area)


def by_fours(count, one):
    def four(q, carry):
        for n in range(4):
            one(4 * q + n)
        return carry

    if count == 4:
        four(0, 0)
    else:
        lax.fori_loop(0, count // 4, four, 0)


def gate_kernel(cols, area, width, x_ref, cot_ref, own_cot_ref, w_ref, wout_ref, gate_ref, cot_out_ref, grad_ref, low_ref):
    row, core, col, step, pair = place(cols)
    out_gate = sigmoid(dot(x_ref[rows_of(step, area), :], w_ref[:, 4 * width :]))
    gated = jnp.where(step == 0, own_cot_ref[...], cot_ref[...]) * out_gate
    low = gated.astype(BF16)
    gate_ref[...] = out_gate
    cot_out_ref[...] = gated * (1.0 - out_gate)
    low_ref[...] = low
    grad_ref[...] = dot_nt(low, wout_ref[...])


def fold(parts):
    spot = lax.broadcasted_iota(jnp.int32, parts[0].shape, 0)
    shift = 1
    while len(parts) > 1:
        first = (spot & shift) == 0
        parts = [
            jnp.where(first, a, b) + pltpu.roll(jnp.where(first, b, a), shift, 0)
            for a, b in zip(parts[::2], parts[1::2])
        ]
        shift *= 2
    return parts[0]


def block_of(row_len):
    return next(n for n in (4, 2) if row_len % n == 0)


def mix_half(cols, sizes, lv_ref, rv_ref, mixed_ref):
    row_len, col_len, width = sizes
    groups = col_len // SEG
    many = block_of(row_len)
    zero = jnp.zeros((SEG, width), F32)

    for start in range(0, row_len, many):
        for jt in range(row_len // 4):

            def over(q, acc):
                for d in range(4):
                    for g in range(groups):
                        left = [lv_ref[4 * q + d, start + a, tile(g), :] for a in range(many)]
                        right = [rv_ref[4 * q + d, 4 * jt + n, tile(g), :] for n in range(4)]
                        acc = tuple(
                            acc[4 * a + n] + left[a] * right[n] for a in range(many) for n in range(4)
                        )
                return acc

            acc = (zero,) * (4 * many)
            acc = over(0, acc) if cols == 4 else lax.fori_loop(0, cols // 4, over, acc)
            for a in range(0, many, 2):
                sums = fold(list(acc[4 * a : 4 * a + 8]))
                mixed_ref[start + a, 4 * jt : 4 * jt + 4, :] = sums[:4]
                mixed_ref[start + a + 1, 4 * jt : 4 * jt + 4, :] = sums[4:]


def mix_own_kernel(cols, sizes, lv_ref, rv_ref, mixed_ref):
    mix_half(cols, sizes, lv_ref, rv_ref, mixed_ref)


def mix_kernel(
    cols, sizes, lv_ref, rv_ref, own_ref, back_ref, low_ref, wide_ref, other_ref, grad_ref
):
    row_len, col_len, width = sizes
    area = row_len * col_len
    mix_half(cols, sizes, lv_ref, rv_ref, other_ref)
    first = (lax.axis_index("row") & 1) == 0
    for i in range(row_len):
        own, other = own_ref[i], other_ref[i]
        low, high = jnp.where(first, own, other), jnp.where(first, other, own)
        grad_ref[i, :row_len, :] = low[:row_len]
        grad_ref[i, row_len:, :] = high[:row_len]
    mixed_norm, mixed_scale = layer_norm(grad_ref[...].reshape(area, width))
    low_ref[...] = mixed_norm.astype(BF16)
    grad_mixed = norm_back(back_ref[...], mixed_norm, mixed_scale)
    grad_ref[...] = grad_mixed.astype(BF16).astype(F32).reshape(row_len, col_len, width)

    for i in range(row_len):
        for j in range(col_len):
            wide_ref[i, j] = jnp.broadcast_to(grad_ref[i, j : j + 1, :], (SEG, width))


def gradient(load, count, many, first, sizes, a_ref, b_ref, d, d_ref):
    row_len, col_len, width = sizes
    groups = col_len // SEG
    acc = [[jnp.zeros((SEG, width), F32)] * groups for _ in range(many)]
    for n in range(count):
        value, weights = load(n)
        for a in range(many):
            for g in range(groups):
                acc[a][g] = acc[a][g] + value[g] * weights[a]
    full = [jnp.concatenate(acc[a], axis=0) for a in range(many)]
    gates = [full[a] * a_ref[d, first + a] for a in range(many)]
    values = [full[a] * b_ref[d, first + a] for a in range(many)]
    start = (d * row_len + first) * col_len
    rows = pl.ds(start if isinstance(start, int) else pl.multiple_of(start, many * col_len), many * col_len)
    d_ref[rows, :width] = jnp.concatenate(gates, axis=0).astype(BF16)
    d_ref[rows, width:] = jnp.concatenate(values, axis=0).astype(BF16)


def grads_kernel(
    cols,
    sizes,
    lv_ref,
    la_ref,
    lb_ref,
    ov_ref,
    oa_ref,
    ob_ref,
    rv_ref,
    ra_ref,
    rb_ref,
    wide_ref,
    dl_ref,
    do_ref,
    dr_ref,
):
    row_len, col_len, width = sizes
    groups = col_len // SEG
    many = block_of(row_len)
    core = lax.axis_index("row") & 1

    def blocks(one):
        for first in range(0, row_len, many):
            by_fours(cols, functools.partial(one, first))

    def right_back(base, a_ref, b_ref, d_ref):
        def one(first, d):
            def load(i):
                return (
                    [lv_ref[d, i, tile(g), :] for g in range(groups)],
                    [wide_ref[i, base + first + a] for a in range(many)],
                )

            gradient(load, row_len, many, first, sizes, a_ref, b_ref, d, d_ref)

        blocks(one)

    right_back(core * row_len, oa_ref, ob_ref, do_ref)
    right_back((1 - core) * row_len, ra_ref, rb_ref, dr_ref)

    def left_back(first, d):
        def load(n):
            ref = ov_ref if n < row_len else rv_ref
            j = (core if n < row_len else 1 - core) * row_len + n % row_len
            return (
                [ref[d, n % row_len, tile(g), :] for g in range(groups)],
                [wide_ref[first + a, j] for a in range(many)],
            )

        gradient(load, col_len, many, first, sizes, la_ref, lb_ref, d, dl_ref)

    blocks(left_back)


def weight_sums_kernel(
    cols,
    area,
    width,
    x_ref,
    x_turned_ref,
    own_x_ref,
    other_x_ref,
    dl_ref,
    do_ref,
    dr_ref,
    low_ref,
    gate_ref,
    cot_ref,
    update_low_ref,
    wout_ref,
    send_ref,
    keep_ref,
    out_ref,
    logit_ref,
    sum_ref,
):
    row, core, col, step, pair = place(cols)
    update = dot(low_ref[...], wout_ref[...])
    out_ref[...] = gate_ref[...] * update
    grad_logit = (cot_ref[...] * update).astype(BF16)
    logit_ref[...] = grad_logit
    left_w = dot(x_turned_ref[...], dl_ref[...])
    right_w = dot_tn(own_x_ref[...], do_ref[...]) + dot_tn(other_x_ref[...], dr_ref[...])
    sum_ref[0, :width, :] = left_w[:, :width]
    sum_ref[0, width : 2 * width, :] = left_w[:, width:]
    sum_ref[0, 2 * width :, :] = right_w[:, :width]
    sum_ref[1, :width, :] = right_w[:, width:]
    sum_ref[1, width : 2 * width, :] = dot_tn(x_ref[rows_of(step, area), :], grad_logit)
    sum_ref[1, 2 * width :, :] = dot_tn(low_ref[...], update_low_ref[...])
    send_ref[...] = sum_ref[1 - core].astype(BF16)
    keep_ref[...] = sum_ref[core]


def back_right_kernel(cols, area, width, dr_ref, w_ref, part_ref):
    def back(d):
        rows = rows_of(d, area)
        part = dot_nt(dr_ref[rows, :], w_ref[:, 2 * width : 4 * width])
        part_ref[rows, :] = part.astype(part_ref.dtype)

    by_fours(cols, back)


def back_left_kernel(cols, area, width, dl_ref, logit_ref, w_ref, gx_ref):
    row, core, col, step, pair = place(cols)

    def back(d):
        rows = rows_of(d, area)
        gx_ref[rows, :] = dot_nt(dl_ref[rows, :], w_ref[:, : 2 * width])

    by_fours(cols, back)
    gx_ref[rows_of(step, area), :] += dot_nt(logit_ref[...], w_ref[:, 4 * width :])


def core_sum_kernel(keep_ref, got_ref, y_ref):
    y_ref[...] = (keep_ref[...] + got_ref[...].astype(F32)).astype(BF16)


def chunks_kernel(cols, keep_ref, got_ref, own_ref, *rest):
    chunk_refs, sum_ref = rest[:-1], rest[-1]
    col = lax.axis_index("col")
    total = keep_ref[...] + got_ref[...].astype(F32)
    sum_ref[...] = total.reshape(sum_ref.shape)
    own_ref[...] = sum_ref[col]
    for d in range(1, cols):
        chunk_refs[d - 1][...] = sum_ref[col ^ d].astype(BF16)


def row_sum_kernel(cols, area, gx_ref, got_ref, y_ref, own_ref, *part_refs):
    row, core, col, step, pair = place(cols)
    stays = pair == row >> 1

    def total(d):
        rows = slice(d * area, (d + 1) * area)
        return gx_ref[rows, :] + jnp.where(stays, y_ref[rows, :], got_ref[rows, :]).astype(F32)

    own_ref[...] = total(0)
    for d in range(1, cols):
        part_refs[d - 1][...] = total(d).astype(BF16)


def pack_kernel(cols, area, chunk_ref, *refs):
    for d in range(cols - 1):
        refs[cols - 1 + d][:area, :] = refs[d][...]
        refs[cols - 1 + d][area:, :] = chunk_ref[...]


def home_kernel(cols, own_ref, got_ref, pair_ref, out_ref, normed_ref, scaled_ref):
    row, core, col, step, pair = place(cols)
    out_ref[...] = jnp.where(step == 0, own_ref[...], got_ref[...])
    normed, scaled = layer_norm(pair_ref[...])
    normed_ref[...] = normed
    scaled_ref[...] = jnp.broadcast_to(scaled, normed.shape)


def join_kernel(cols, area, chunk_ref, *rest):
    got_refs, (half_ref, order_ref) = rest[: cols - 1], rest[cols - 1 :]
    col = lax.axis_index("col")
    order_ref[col] = chunk_ref[...].astype(F32)
    for d in range(1, cols):
        order_ref[col ^ d] = got_refs[d - 1][area:, :].astype(F32)
    half_ref[...] = order_ref[...].reshape(half_ref.shape).astype(BF16)


def pair_grad_kernel(area, own_ref, normed_ref, scaled_ref, *rest):
    got_refs, grad_ref = rest[:-1], rest[-1]
    total = own_ref[...]
    for got in got_refs:
        total = total + got[:area, :].astype(F32)
    grad_ref[...] = norm_back(total, normed_ref[...], scaled_ref[...])


def weights_kernel(width, mine_ref, other_ref, proj_ref, out_ref):
    first = (lax.axis_index("row") & 1) == 0
    mine, other = mine_ref[...].astype(F32), other_ref[...].astype(F32)
    low, high = jnp.where(first, mine, other), jnp.where(first, other, mine)
    for n in range(3):
        proj_ref[:, n * width : (n + 1) * width] = low[n * width : (n + 1) * width]
    for n in range(2):
        proj_ref[:, (3 + n) * width : (4 + n) * width] = high[n * width : (n + 1) * width]
    out_ref[...] = high[2 * width :]


def call(kernel, name, micros, out_shape, args, scratch=(), space=pltpu.VMEM):
    specs = [pl.BlockSpec(memory_space=space) for _ in args]
    total = sum(_bytes(ref) for ref in [*args, *out_shape, *scratch])
    return pl.pallas_call(
        kernel,
        out_shape=tuple(out_shape),
        in_specs=specs,
        out_specs=tuple(pl.BlockSpec(memory_space=pltpu.VMEM) for _ in out_shape),
        scratch_shapes=list(scratch),
        cost_estimate=pl.CostEstimate(
            flops=0, transcendentals=0, bytes_accessed=int(micros * 3_690_000)
        ),
        compiler_params=pltpu.CompilerParams(vmem_limit_bytes=min(60 << 20, total + (8 << 20))),
        name=name,
    )(*args)


def _bytes(ref):
    size = jnp.dtype(ref.dtype).itemsize
    for n in ref.shape:
        size *= n
    return size


def body(rows, cols, pair_input, block_valid, proj_weight, out_weight, cotangent):
    row_len, col_len, width = pair_input.shape
    area = row_len * col_len
    sizes = (row_len, col_len, width)
    planes = rows // 2
    assert planes == cols and col_len == 2 * row_len and cols & (cols - 1) == 0
    assert col_len % SEG == 0 and out_weight.shape == (width, width)

    def permute(value, target):
        pairs = []
        for z in range(planes):
            for core in range(2):
                for col in range(cols):
                    to = target(z, core, col)
                    if to == (z, core, col):
                        to = (z, 1 - core, col)
                    pairs.append(((2 * z + core) * cols + col, (2 * to[0] + to[1]) * cols + to[2]))
        return lax.ppermute(value, ("row", "col"), pairs)

    def in_plane(value, d):
        return permute(value, lambda z, core, col: (z, core, col ^ d))

    def across(value, d):
        return permute(value, lambda z, core, col: (z ^ d, core, col))

    def to_pair(value):
        return permute(value, lambda z, core, col: (z, core, col ^ flip(z, cols)))

    def swap(value):
        return permute(value, lambda z, core, col: (z, 1 - core, col))

    def like(*shape, dtype=F32):
        return jax.ShapeDtypeStruct(shape, dtype)

    pair = pair_input.reshape(area, width)
    cot = cotangent.reshape(area, width)
    tall, half = cols * area, 3 * width
    chunk = half // cols
    (low,) = call(norm_kernel, "norm", 0.3, [like(area, width, dtype=BF16)], [pair])
    blocks = [low] + [in_plane(low, d) for d in range(1, cols)]
    x = jnp.concatenate(blocks, axis=0)
    got_x = permute(x, lambda z, core, col: (flip(col ^ z, cols), core, col))
    cot, x, block_valid = lax.optimization_barrier((cot, x, block_valid))
    got_cot = to_pair(cot)
    (mask,) = call(
        mask_kernel, "mask", 0.1, [like(col_len * cols, width)], [block_valid], space=pltpu.SMEM
    )
    x_turned, *left = call(
        functools.partial(project_kernel, 0, cols, sizes),
        "left",
        0.9,
        [like(width, tall, dtype=BF16)] + [like(cols, row_len, col_len, width)] * 3,
        [mask, x, x, proj_weight],
    )
    out_gate, cot, back, update_low = call(
        functools.partial(gate_kernel, cols, area, width),
        "gate",
        0.3,
        [like(area, width)] * 3 + [like(area, width, dtype=BF16)],
        [x, got_cot, cot, proj_weight, out_weight],
    )
    left, back, got_x = lax.optimization_barrier((left, back, got_x))
    swapped_x = swap(got_x)
    right_shape = [like(tall, width, dtype=BF16)] + [like(cols, row_len, col_len, width)] * 3
    own_x, *own = call(
        functools.partial(project_kernel, 1, cols, sizes),
        "right_own",
        0.4,
        right_shape,
        [mask, got_x, x, proj_weight],
    )
    (mixed_own,) = call(
        functools.partial(mix_own_kernel, cols, sizes),
        "mix_own",
        0.7,
        [like(row_len, 2 * SEG * (-(-row_len // (2 * SEG))), width)],
        [left[0], own[0]],
    )
    swapped_x, mixed_own = lax.optimization_barrier((swapped_x, mixed_own))
    other_x, *right = call(
        functools.partial(project_kernel, 2, cols, sizes),
        "right_other",
        0.4,
        right_shape,
        [mask, swapped_x, got_x, proj_weight],
    )
    mixed_low, wide = call(
        functools.partial(mix_kernel, cols, sizes),
        "mix",
        1.2,
        [like(area, width, dtype=BF16), like(row_len, col_len, SEG, width)],
        [left[0], right[0], mixed_own, back],
        [pltpu.VMEM(mixed_own.shape, F32), pltpu.VMEM((row_len, col_len, width), F32)],
    )
    dl, do, dr = call(
        functools.partial(grads_kernel, cols, sizes),
        "grads",
        2.5,
        [like(tall, 2 * width, dtype=BF16)] * 3,
        [*left, *own, *right, wide],
    )
    send_w, keep_w, pair_out, grad_logit = call(
        functools.partial(weight_sums_kernel, cols, area, width),
        "weight_sums",
        0.6,
        [
            like(half, width, dtype=BF16),
            like(half, width),
            like(area, width),
            like(area, width, dtype=BF16),
        ],
        [x, x_turned, own_x, other_x, dl, do, dr, mixed_low, out_gate, cot, update_low, out_weight],
        [pltpu.VMEM((2, half, width), F32)],
    )
    got_w = swap(send_w)
    (send_y,) = call(
        functools.partial(back_right_kernel, cols, area, width),
        "back_other",
        0.3,
        [like(tall, width, dtype=BF16)],
        [dr, proj_weight],
    )
    got_y = swap(send_y)
    mine, *chunks = call(
        functools.partial(chunks_kernel, cols),
        "chunks",
        0.1,
        [like(chunk, width)] + [like(chunk, width, dtype=BF16)] * (cols - 1),
        [keep_w, got_w],
        [pltpu.VMEM((cols, chunk, width), F32)],
    )
    dl, mine = lax.optimization_barrier((dl, mine))
    (keep_y,) = call(
        functools.partial(back_right_kernel, cols, area, width),
        "back_own",
        0.3,
        [like(tall, width)],
        [do, proj_weight],
    )
    (y,) = call(core_sum_kernel, "core_sum", 0.1, [like(tall, width, dtype=BF16)], [keep_y, got_y])
    back_y = permute(y, lambda z, core, col: (col ^ flip(z, cols), core, col))
    (gx,) = call(
        functools.partial(back_left_kernel, cols, area, width),
        "back_left",
        0.3,
        [like(tall, width)],
        [dl, grad_logit, proj_weight],
    )
    for d in range(1, cols):
        mine = mine + in_plane(chunks[d - 1], d).astype(F32)
    low_mine = mine.astype(BF16)
    home = to_pair(pair_out)
    back_y, home = lax.optimization_barrier((back_y, home))
    rest, *parts = call(
        functools.partial(row_sum_kernel, cols, area),
        "row_sum",
        4.0,
        [like(area, width)] + [like(area, width, dtype=BF16)] * (cols - 1),
        [gx, back_y, y],
    )
    planes_got = [across(low_mine, d) for d in range(1, cols)]
    *planes_got, rest = lax.optimization_barrier((*planes_got, rest))
    for got in planes_got:
        mine = mine + got.astype(F32)
    low_mine = mine.astype(BF16)
    sends = call(
        functools.partial(pack_kernel, cols, area),
        "pack",
        0.1,
        [like(area + chunk, width, dtype=BF16)] * (cols - 1),
        [low_mine, *parts],
    )
    gets = [in_plane(sends[d - 1], d) for d in range(1, cols)]
    pair_out, normed, scaled = call(
        functools.partial(home_kernel, cols),
        "home",
        0.6,
        [like(area, width)] * 3,
        [pair_out, home, pair],
    )
    pair_out, *gets = lax.optimization_barrier((pair_out, *gets))
    (half_w,) = call(
        functools.partial(join_kernel, cols, area),
        "join",
        0.1,
        [like(half, width, dtype=BF16)],
        [low_mine, *gets],
        [pltpu.VMEM((cols, chunk, width), F32)],
    )
    other_w = swap(half_w)
    half_w, rest = lax.optimization_barrier((half_w, rest))
    (pair_grad,) = call(
        functools.partial(pair_grad_kernel, area),
        "pair_grad",
        1.0,
        [like(area, width)],
        [rest, normed, scaled, *gets],
    )
    proj_grad, out_grad = call(
        functools.partial(weights_kernel, width),
        "weights",
        0.8,
        [like(*proj_weight.shape), like(width, width)],
        [half_w, other_w],
    )
    shape = pair_input.shape
    return pair_out.reshape(shape), pair_grad.reshape(shape), proj_grad, out_grad


def solution(mesh):
    return jax.shard_map(
        functools.partial(body, mesh.shape["row"], mesh.shape["col"]),
        mesh=mesh,
        in_specs=(P("row", "col", None), P(), P(), P(), P("row", "col", None)),
        out_specs=(P("row", "col", None), P("row", "col", None), P(), P()),
        check_vma=False,
    )
```

```python
import functools

import jax
import jax.numpy as jnp
from jax import lax
from jax.experimental import pallas as pl
from jax.experimental.pallas import tpu as pltpu
from jax.sharding import PartitionSpec as P

SEG = 8
F32 = jnp.float32
BF16 = jnp.bfloat16


def sigmoid(values):
    return 0.5 * jnp.tanh(0.5 * values) + 0.5


def layer_norm(values):
    center = values - jnp.mean(values, axis=-1, keepdims=True)
    scaled = lax.rsqrt(jnp.mean(center * center, axis=-1, keepdims=True) + 1e-05)
    return center * scaled, scaled


def norm_back(grad_norm, normed, scaled):
    first_mean = jnp.mean(grad_norm, axis=-1, keepdims=True)
    second = jnp.mean(grad_norm * normed, axis=-1, keepdims=True)
    return scaled * (grad_norm - first_mean - normed * second)


def dot(a, b):
    return jnp.dot(a, b, preferred_element_type=F32)


def dot_nt(a, b):
    return lax.dot_general(a, b, (((1,), (1,)), ((), ())), preferred_element_type=F32)


def dot_tn(a, b):
    return lax.dot_general(a, b, (((0,), (0,)), ((), ())), preferred_element_type=F32)


def flip(z, count):
    out, bit = z & 0, 1
    top = count >> 1
    while bit < count:
        if isinstance(z, int):
            out |= top if z & bit else 0
        else:
            out = out + jnp.where((z & bit) != 0, top, 0)
        bit, top = bit << 1, top >> 1
    return out


def place(cols):
    row, col = lax.axis_index("row"), lax.axis_index("col")
    z, core = row >> 1, row & 1
    step = flip(z, cols)
    return row, core, col, step, col ^ step


def norm_kernel(pair_ref, low_ref):
    low_ref[...] = layer_norm(pair_ref[...])[0].astype(BF16)


def mask_kernel(valid_ref, mask_ref):
    spot = lax.broadcasted_iota(jnp.int32, (SEG, mask_ref.shape[1]), 0)
    for g in range(mask_ref.shape[0] // SEG):
        mask_ref[tile(g), :] = jnp.where(spot < valid_ref[g], 1.0, 0.0)


def project_block(projected, mask_ref, row, block, sizes, index, v_ref, a_ref, b_ref):
    row_len, col_len, width = sizes
    keep_col = mask_ref[pl.ds(pl.multiple_of(block * col_len, SEG), col_len), :]
    for i in range(row_len):
        keep = keep_col * mask_ref[pl.ds(row * row_len + i, 1), :]
        part = projected[i * col_len : (i + 1) * col_len]
        gate = sigmoid(part[:, :width])
        kept = keep * gate
        gated = kept * part[:, width:]
        v_ref[index + (i,)] = gated.astype(BF16).astype(F32)
        a_ref[index + (i,)] = gated * (1.0 - gate)
        b_ref[index + (i,)] = kept


def project_kernel(side, cols, sizes, mask_ref, x_ref, home_ref, w_ref, *refs):
    row_len, col_len, width = sizes
    area = row_len * col_len
    row, core, col, step, pair = place(cols)
    stays = pair == row >> 1
    if side:
        row = 2 * pair + (core if side == 1 else 1 - core)
    base = 2 * width if side else 0

    def one(d):
        rows = rows_of(d, area)
        used = x_ref[rows, :]
        if side:
            used = jnp.where(stays, home_ref[rows, :], used)
            refs[0][rows, :] = used
        projected = dot(used, w_ref[:, base : base + 2 * width])
        project_block(projected, mask_ref, row, col ^ d, sizes, (d,), *refs[-3:])

    by_fours(cols, one)
    if side == 0:
        refs[0][...] = x_ref[...].T


def tile(g):
    return slice(g * SEG, (g + 1) * SEG)


def rows_of(d, area):
    if isinstance(d, int):
        return pl.ds(d * area, area)
    return pl.ds(pl.multiple_of(d * area, area), area)


def by_fours(count, one):
    def four(q, carry):
        for n in range(4):
            one(4 * q + n)
        return carry

    if count == 4:
        four(0, 0)
    else:
        lax.fori_loop(0, count // 4, four, 0)


def gate_kernel(cols, area, width, x_ref, cot_ref, own_cot_ref, w_ref, wout_ref, gate_ref, cot_out_ref, grad_ref, low_ref):
    row, core, col, step, pair = place(cols)
    out_gate = sigmoid(dot(x_ref[rows_of(step, area), :], w_ref[:, 4 * width :]))
    gated = jnp.where(step == 0, own_cot_ref[...], cot_ref[...]) * out_gate
    low = gated.astype(BF16)
    gate_ref[...] = out_gate
    cot_out_ref[...] = gated * (1.0 - out_gate)
    low_ref[...] = low
    grad_ref[...] = dot_nt(low, wout_ref[...])


def fold(parts):
    spot = lax.broadcasted_iota(jnp.int32, parts[0].shape, 0)
    shift = 1
    while len(parts) > 1:
        first = (spot & shift) == 0
        parts = [
            jnp.where(first, a, b) + pltpu.roll(jnp.where(first, b, a), shift, 0)
            for a, b in zip(parts[::2], parts[1::2])
        ]
        shift *= 2
    return parts[0]


def block_of(row_len):
    return next(n for n in (4, 2) if row_len % n == 0)


def mix_half(cols, sizes, lv_ref, rv_ref, mixed_ref):
    row_len, col_len, width = sizes
    groups = col_len // SEG
    many = block_of(row_len)
    zero = jnp.zeros((SEG, width), F32)

    for start in range(0, row_len, many):
        for jt in range(row_len // 4):

            def over(q, acc):
                for d in range(4):
                    for g in range(groups):
                        left = [lv_ref[4 * q + d, start + a, tile(g), :] for a in range(many)]
                        right = [rv_ref[4 * q + d, 4 * jt + n, tile(g), :] for n in range(4)]
                        acc = tuple(
                            acc[4 * a + n] + left[a] * right[n] for a in range(many) for n in range(4)
                        )
                return acc

            acc = (zero,) * (4 * many)
            acc = over(0, acc) if cols == 4 else lax.fori_loop(0, cols // 4, over, acc)
            for a in range(0, many, 2):
                sums = fold(list(acc[4 * a : 4 * a + 8]))
                mixed_ref[start + a, 4 * jt : 4 * jt + 4, :] = sums[:4]
                mixed_ref[start + a + 1, 4 * jt : 4 * jt + 4, :] = sums[4:]


def mix_own_kernel(cols, sizes, lv_ref, rv_ref, mixed_ref):
    mix_half(cols, sizes, lv_ref, rv_ref, mixed_ref)


def mix_kernel(
    cols, sizes, lv_ref, rv_ref, own_ref, back_ref, low_ref, wide_ref, other_ref, grad_ref
):
    row_len, col_len, width = sizes
    area = row_len * col_len
    mix_half(cols, sizes, lv_ref, rv_ref, other_ref)
    first = (lax.axis_index("row") & 1) == 0
    for i in range(row_len):
        own, other = own_ref[i], other_ref[i]
        low, high = jnp.where(first, own, other), jnp.where(first, other, own)
        grad_ref[i, :row_len, :] = low[:row_len]
        grad_ref[i, row_len:, :] = high[:row_len]
    mixed_norm, mixed_scale = layer_norm(grad_ref[...].reshape(area, width))
    low_ref[...] = mixed_norm.astype(BF16)
    grad_mixed = norm_back(back_ref[...], mixed_norm, mixed_scale)
    grad_ref[...] = grad_mixed.astype(BF16).astype(F32).reshape(row_len, col_len, width)

    for i in range(row_len):
        for j in range(col_len):
            wide_ref[i, j] = jnp.broadcast_to(grad_ref[i, j : j + 1, :], (SEG, width))


def gradient(load, count, many, first, sizes, a_ref, b_ref, d, d_ref):
    row_len, col_len, width = sizes
    groups = col_len // SEG
    acc = [[jnp.zeros((SEG, width), F32)] * groups for _ in range(many)]
    for n in range(count):
        value, weights = load(n)
        for a in range(many):
            for g in range(groups):
                acc[a][g] = acc[a][g] + value[g] * weights[a]
    full = [jnp.concatenate(acc[a], axis=0) for a in range(many)]
    gates = [full[a] * a_ref[d, first + a] for a in range(many)]
    values = [full[a] * b_ref[d, first + a] for a in range(many)]
    start = (d * row_len + first) * col_len
    rows = pl.ds(start if isinstance(start, int) else pl.multiple_of(start, many * col_len), many * col_len)
    d_ref[rows, :width] = jnp.concatenate(gates, axis=0).astype(BF16)
    d_ref[rows, width:] = jnp.concatenate(values, axis=0).astype(BF16)


def grads_kernel(
    cols,
    sizes,
    lv_ref,
    la_ref,
    lb_ref,
    ov_ref,
    oa_ref,
    ob_ref,
    rv_ref,
    ra_ref,
    rb_ref,
    wide_ref,
    dl_ref,
    do_ref,
    dr_ref,
):
    row_len, col_len, width = sizes
    groups = col_len // SEG
    many = block_of(row_len)
    core = lax.axis_index("row") & 1

    def blocks(one):
        for first in range(0, row_len, many):
            by_fours(cols, functools.partial(one, first))

    def right_back(base, a_ref, b_ref, d_ref):
        def one(first, d):
            def load(i):
                return (
                    [lv_ref[d, i, tile(g), :] for g in range(groups)],
                    [wide_ref[i, base + first + a] for a in range(many)],
                )

            gradient(load, row_len, many, first, sizes, a_ref, b_ref, d, d_ref)

        blocks(one)

    right_back(core * row_len, oa_ref, ob_ref, do_ref)
    right_back((1 - core) * row_len, ra_ref, rb_ref, dr_ref)

    def left_back(first, d):
        def load(n):
            ref = ov_ref if n < row_len else rv_ref
            j = (core if n < row_len else 1 - core) * row_len + n % row_len
            return (
                [ref[d, n % row_len, tile(g), :] for g in range(groups)],
                [wide_ref[first + a, j] for a in range(many)],
            )

        gradient(load, col_len, many, first, sizes, la_ref, lb_ref, d, dl_ref)

    blocks(left_back)


def weight_sums_kernel(
    cols,
    area,
    width,
    x_ref,
    x_turned_ref,
    own_x_ref,
    other_x_ref,
    dl_ref,
    do_ref,
    dr_ref,
    low_ref,
    gate_ref,
    cot_ref,
    update_low_ref,
    wout_ref,
    send_ref,
    keep_ref,
    out_ref,
    logit_ref,
    sum_ref,
):
    row, core, col, step, pair = place(cols)
    update = dot(low_ref[...], wout_ref[...])
    out_ref[...] = gate_ref[...] * update
    grad_logit = (cot_ref[...] * update).astype(BF16)
    logit_ref[...] = grad_logit
    left_w = dot(x_turned_ref[...], dl_ref[...])
    right_w = dot_tn(own_x_ref[...], do_ref[...]) + dot_tn(other_x_ref[...], dr_ref[...])
    sum_ref[0, :width, :] = left_w[:, :width]
    sum_ref[0, width : 2 * width, :] = left_w[:, width:]
    sum_ref[0, 2 * width :, :] = right_w[:, :width]
    sum_ref[1, :width, :] = right_w[:, width:]
    sum_ref[1, width : 2 * width, :] = dot_tn(x_ref[rows_of(step, area), :], grad_logit)
    sum_ref[1, 2 * width :, :] = dot_tn(low_ref[...], update_low_ref[...])
    send_ref[...] = sum_ref[1 - core].astype(BF16)
    keep_ref[...] = sum_ref[core]


def back_right_kernel(cols, area, width, dr_ref, w_ref, part_ref):
    def back(d):
        rows = rows_of(d, area)
        part = dot_nt(dr_ref[rows, :], w_ref[:, 2 * width : 4 * width])
        part_ref[rows, :] = part.astype(part_ref.dtype)

    by_fours(cols, back)


def back_left_kernel(cols, area, width, dl_ref, logit_ref, w_ref, gx_ref):
    row, core, col, step, pair = place(cols)

    def back(d):
        rows = rows_of(d, area)
        gx_ref[rows, :] = dot_nt(dl_ref[rows, :], w_ref[:, : 2 * width])

    by_fours(cols, back)
    gx_ref[rows_of(step, area), :] += dot_nt(logit_ref[...], w_ref[:, 4 * width :])


def core_sum_kernel(keep_ref, got_ref, y_ref):
    y_ref[...] = (keep_ref[...] + got_ref[...].astype(F32)).astype(BF16)


def chunks_kernel(cols, keep_ref, got_ref, own_ref, *rest):
    chunk_refs, sum_ref = rest[:-1], rest[-1]
    col = lax.axis_index("col")
    total = keep_ref[...] + got_ref[...].astype(F32)
    sum_ref[...] = total.reshape(sum_ref.shape)
    own_ref[...] = sum_ref[col]
    for d in range(1, cols):
        chunk_refs[d - 1][...] = sum_ref[col ^ d].astype(BF16)


def row_sum_kernel(cols, area, gx_ref, got_ref, y_ref, own_ref, *part_refs):
    row, core, col, step, pair = place(cols)
    stays = pair == row >> 1

    def total(d):
        rows = slice(d * area, (d + 1) * area)
        return gx_ref[rows, :] + jnp.where(stays, y_ref[rows, :], got_ref[rows, :]).astype(F32)

    own_ref[...] = total(0)
    for d in range(1, cols):
        part_refs[d - 1][...] = total(d).astype(BF16)


def pack_kernel(cols, area, chunk_ref, *refs):
    for d in range(cols - 1):
        refs[cols - 1 + d][:area, :] = refs[d][...]
        refs[cols - 1 + d][area:, :] = chunk_ref[...]


def home_kernel(cols, own_ref, got_ref, pair_ref, out_ref, normed_ref, scaled_ref):
    row, core, col, step, pair = place(cols)
    out_ref[...] = jnp.where(step == 0, own_ref[...], got_ref[...])
    normed, scaled = layer_norm(pair_ref[...])
    normed_ref[...] = normed
    scaled_ref[...] = jnp.broadcast_to(scaled, normed.shape)


def join_kernel(cols, area, chunk_ref, *rest):
    got_refs, (half_ref, order_ref) = rest[: cols - 1], rest[cols - 1 :]
    col = lax.axis_index("col")
    order_ref[col] = chunk_ref[...].astype(F32)
    for d in range(1, cols):
        order_ref[col ^ d] = got_refs[d - 1][area:, :].astype(F32)
    half_ref[...] = order_ref[...].reshape(half_ref.shape).astype(BF16)


def pair_grad_kernel(area, own_ref, normed_ref, scaled_ref, *rest):
    got_refs, grad_ref = rest[:-1], rest[-1]
    total = own_ref[...]
    for got in got_refs:
        total = total + got[:area, :].astype(F32)
    grad_ref[...] = norm_back(total, normed_ref[...], scaled_ref[...])


def weights_kernel(width, mine_ref, other_ref, proj_ref, out_ref):
    first = (lax.axis_index("row") & 1) == 0
    mine, other = mine_ref[...].astype(F32), other_ref[...].astype(F32)
    low, high = jnp.where(first, mine, other), jnp.where(first, other, mine)
    for n in range(3):
        proj_ref[:, n * width : (n + 1) * width] = low[n * width : (n + 1) * width]
    for n in range(2):
        proj_ref[:, (3 + n) * width : (4 + n) * width] = high[n * width : (n + 1) * width]
    out_ref[...] = high[2 * width :]


def call(kernel, name, micros, out_shape, args, scratch=(), space=pltpu.VMEM):
    specs = [pl.BlockSpec(memory_space=space) for _ in args]
    total = sum(_bytes(ref) for ref in [*args, *out_shape, *scratch])
    return pl.pallas_call(
        kernel,
        out_shape=tuple(out_shape),
        in_specs=specs,
        out_specs=tuple(pl.BlockSpec(memory_space=pltpu.VMEM) for _ in out_shape),
        scratch_shapes=list(scratch),
        cost_estimate=pl.CostEstimate(
            flops=0, transcendentals=0, bytes_accessed=int(micros * 3_690_000)
        ),
        compiler_params=pltpu.CompilerParams(vmem_limit_bytes=min(60 << 20, total + (8 << 20))),
        name=name,
    )(*args)


def _bytes(ref):
    size = jnp.dtype(ref.dtype).itemsize
    for n in ref.shape:
        size *= n
    return size


def body(rows, cols, pair_input, block_valid, proj_weight, out_weight, cotangent):
    row_len, col_len, width = pair_input.shape
    area = row_len * col_len
    sizes = (row_len, col_len, width)
    planes = rows // 2
    assert planes == cols and col_len == 2 * row_len and cols & (cols - 1) == 0
    assert col_len % SEG == 0 and out_weight.shape == (width, width)

    def permute(value, target):
        pairs = []
        for z in range(planes):
            for core in range(2):
                for col in range(cols):
                    to = target(z, core, col)
                    if to == (z, core, col):
                        to = (z, 1 - core, col)
                    pairs.append(((2 * z + core) * cols + col, (2 * to[0] + to[1]) * cols + to[2]))
        return lax.ppermute(value, ("row", "col"), pairs)

    def in_plane(value, d):
        return permute(value, lambda z, core, col: (z, core, col ^ d))

    def across(value, d):
        return permute(value, lambda z, core, col: (z ^ d, core, col))

    def to_pair(value):
        return permute(value, lambda z, core, col: (z, core, col ^ flip(z, cols)))

    def swap(value):
        return permute(value, lambda z, core, col: (z, 1 - core, col))

    def like(*shape, dtype=F32):
        return jax.ShapeDtypeStruct(shape, dtype)

    pair = pair_input.reshape(area, width)
    cot = cotangent.reshape(area, width)
    tall, half = cols * area, 3 * width
    chunk = half // cols
    (low,) = call(norm_kernel, "norm", 0.3, [like(area, width, dtype=BF16)], [pair])
    blocks = [low] + [in_plane(low, d) for d in range(1, cols)]
    x = jnp.concatenate(blocks, axis=0)
    got_x = permute(x, lambda z, core, col: (flip(col ^ z, cols), core, col))
    cot, x, block_valid = lax.optimization_barrier((cot, x, block_valid))
    got_cot = to_pair(cot)
    (mask,) = call(
        mask_kernel, "mask", 0.1, [like(col_len * cols, width)], [block_valid], space=pltpu.SMEM
    )
    x_turned, *left = call(
        functools.partial(project_kernel, 0, cols, sizes),
        "left",
        0.9,
        [like(width, tall, dtype=BF16)] + [like(cols, row_len, col_len, width)] * 3,
        [mask, x, x, proj_weight],
    )
    out_gate, cot, back, update_low = call(
        functools.partial(gate_kernel, cols, area, width),
        "gate",
        0.3,
        [like(area, width)] * 3 + [like(area, width, dtype=BF16)],
        [x, got_cot, cot, proj_weight, out_weight],
    )
    left, back, got_x = lax.optimization_barrier((left, back, got_x))
    swapped_x = swap(got_x)
    right_shape = [like(tall, width, dtype=BF16)] + [like(cols, row_len, col_len, width)] * 3
    own_x, *own = call(
        functools.partial(project_kernel, 1, cols, sizes),
        "right_own",
        0.4,
        right_shape,
        [mask, got_x, x, proj_weight],
    )
    (mixed_own,) = call(
        functools.partial(mix_own_kernel, cols, sizes),
        "mix_own",
        0.7,
        [like(row_len, 2 * SEG * (-(-row_len // (2 * SEG))), width)],
        [left[0], own[0]],
    )
    swapped_x, mixed_own = lax.optimization_barrier((swapped_x, mixed_own))
    other_x, *right = call(
        functools.partial(project_kernel, 2, cols, sizes),
        "right_other",
        0.4,
        right_shape,
        [mask, swapped_x, got_x, proj_weight],
    )
    mixed_low, wide = call(
        functools.partial(mix_kernel, cols, sizes),
        "mix",
        1.2,
        [like(area, width, dtype=BF16), like(row_len, col_len, SEG, width)],
        [left[0], right[0], mixed_own, back],
        [pltpu.VMEM(mixed_own.shape, F32), pltpu.VMEM((row_len, col_len, width), F32)],
    )
    dl, do, dr = call(
        functools.partial(grads_kernel, cols, sizes),
        "grads",
        2.5,
        [like(tall, 2 * width, dtype=BF16)] * 3,
        [*left, *own, *right, wide],
    )
    send_w, keep_w, pair_out, grad_logit = call(
        functools.partial(weight_sums_kernel, cols, area, width),
        "weight_sums",
        0.6,
        [
            like(half, width, dtype=BF16),
            like(half, width),
            like(area, width),
            like(area, width, dtype=BF16),
        ],
        [x, x_turned, own_x, other_x, dl, do, dr, mixed_low, out_gate, cot, update_low, out_weight],
        [pltpu.VMEM((2, half, width), F32)],
    )
    got_w = swap(send_w)
    (send_y,) = call(
        functools.partial(back_right_kernel, cols, area, width),
        "back_other",
        0.3,
        [like(tall, width, dtype=BF16)],
        [dr, proj_weight],
    )
    got_y = swap(send_y)
    mine, *chunks = call(
        functools.partial(chunks_kernel, cols),
        "chunks",
        0.1,
        [like(chunk, width)] + [like(chunk, width, dtype=BF16)] * (cols - 1),
        [keep_w, got_w],
        [pltpu.VMEM((cols, chunk, width), F32)],
    )
    dl, mine = lax.optimization_barrier((dl, mine))
    (keep_y,) = call(
        functools.partial(back_right_kernel, cols, area, width),
        "back_own",
        0.3,
        [like(tall, width)],
        [do, proj_weight],
    )
    (y,) = call(core_sum_kernel, "core_sum", 0.1, [like(tall, width, dtype=BF16)], [keep_y, got_y])
    back_y = permute(y, lambda z, core, col: (col ^ flip(z, cols), core, col))
    (gx,) = call(
        functools.partial(back_left_kernel, cols, area, width),
        "back_left",
        0.3,
        [like(tall, width)],
        [dl, grad_logit, proj_weight],
    )
    for d in range(1, cols):
        mine = mine + in_plane(chunks[d - 1], d).astype(F32)
    low_mine = mine.astype(BF16)
    home = to_pair(pair_out)
    rest, *parts = call(
        functools.partial(row_sum_kernel, cols, area),
        "row_sum",
        4.0,
        [like(area, width)] + [like(area, width, dtype=BF16)] * (cols - 1),
        [gx, back_y, y],
    )
    planes_got = [across(low_mine, d) for d in range(1, cols)]
    *planes_got, rest, home = lax.optimization_barrier((*planes_got, rest, home))
    for got in planes_got:
        mine = mine + got.astype(F32)
    low_mine = mine.astype(BF16)
    sends = call(
        functools.partial(pack_kernel, cols, area),
        "pack",
        0.1,
        [like(area + chunk, width, dtype=BF16)] * (cols - 1),
        [low_mine, *parts],
    )
    gets = [in_plane(sends[d - 1], d) for d in range(1, cols)]
    pair_out, normed, scaled = call(
        functools.partial(home_kernel, cols),
        "home",
        0.6,
        [like(area, width)] * 3,
        [pair_out, home, pair],
    )
    pair_out, *gets = lax.optimization_barrier((pair_out, *gets))
    (half_w,) = call(
        functools.partial(join_kernel, cols, area),
        "join",
        0.1,
        [like(half, width, dtype=BF16)],
        [low_mine, *gets],
        [pltpu.VMEM((cols, chunk, width), F32)],
    )
    other_w = swap(half_w)
    half_w, rest = lax.optimization_barrier((half_w, rest))
    (pair_grad,) = call(
        functools.partial(pair_grad_kernel, area),
        "pair_grad",
        1.0,
        [like(area, width)],
        [rest, normed, scaled, *gets],
    )
    proj_grad, out_grad = call(
        functools.partial(weights_kernel, width),
        "weights",
        0.8,
        [like(*proj_weight.shape), like(width, width)],
        [half_w, other_w],
    )
    shape = pair_input.shape
    return pair_out.reshape(shape), pair_grad.reshape(shape), proj_grad, out_grad


def solution(mesh):
    return jax.shard_map(
        functools.partial(body, mesh.shape["row"], mesh.shape["col"]),
        mesh=mesh,
        in_specs=(P("row", "col", None), P(), P(), P(), P("row", "col", None)),
        out_specs=(P("row", "col", None), P("row", "col", None), P(), P()),
        check_vma=False,
    )
```
